32 devices in a mesh: dp: 4 (over x, core), ctx: 8 (over z, y).
Axes of the slice: x: 2, y: 2, z: 4, core: 2. Of those that a mesh axis runs over, the one named last changes fastest.
Arguments:
- gate_input: bfloat16 [4, 1024, 4096], P('dp', 'ctx'), may hold values from -6 to 6
- values: bfloat16 [4, 1024, 4096], P('dp', 'ctx'), may hold values from -6 to 6
- cotangent: bfloat16 [4, 1024, 4096], P('dp', 'ctx'), may hold values from -6 to 6
- filter_taps: float32 [1024, 4096], P(('dp', 'ctx')), may hold values from -4 to 4
Outputs:
- output: bfloat16 [4, 1024, 4096], P('dp', 'ctx')
- gate_grad: bfloat16 [4, 1024, 4096], P('dp', 'ctx')
- values_grad: bfloat16 [4, 1024, 4096], P('dp', 'ctx')
- filter_grad: float32 [1024, 4096], P(('dp', 'ctx'))
The draws below stay inside these ranges and needn't reach their ends.
All inputs are finite; a program needn't handle non-finite values.
Results may differ from the reference program's by a relative error of at most 0.013.
Values may be sent and summed in bfloat16 or wider, within the bound.
A program may use at most 128 MiB of HBM per device.

```python
import math
import jax
import jax.numpy as jnp
from jax import lax

CHANNELS = 4096
SEQ_LEN = 1024
BATCH = 4


def draw_filter_taps(key, part):
    rate_key, noise_key = jax.random.split(jax.random.fold_in(key, 11))
    positions = jnp.arange(SEQ_LEN, dtype=jnp.float32)[:, None]
    log_decay = jax.random.uniform(rate_key, (1, CHANNELS), jnp.float32, math.log(30.0), math.log(SEQ_LEN * 4.0))
    noise = jnp.clip(jax.random.normal(noise_key, (SEQ_LEN, CHANNELS), jnp.float32), -4.0, 4.0)
    decay_length = jnp.exp(log_decay)
    normalizer = jnp.sqrt((1.0 - jnp.exp(-2.0 / decay_length)) / (1.0 - jnp.exp(-2.0 * SEQ_LEN / decay_length)))
    return noise * jnp.exp(-positions / decay_length) * normalizer


def block_scale(key, extent, cuts, smallest, high):
    level = 1.0
    for axis_at, shards_of in cuts:
        steps = jax.random.uniform(jax.random.fold_in(jax.random.fold_in(key, 6), axis_at), (shards_of,), jnp.float32, smallest / len(cuts), high / len(cuts))
        level = level * jnp.repeat(jnp.exp(steps), extent[axis_at] // shards_of).reshape((-1,) + (1,) * (len(extent) - 1 - axis_at))
    return level


def scatter_about(stream_key, shape, spread, reach, cuts=(), kind=jnp.bfloat16):
    values = jax.random.normal(stream_key, shape, jnp.float32) * spread
    if len(cuts) > 0:
        values = block_scale(stream_key, shape, cuts, -0.22, 0.18) * values
    return jnp.clip(values, min=-reach, max=reach).astype(kind)


def setup_inputs(seed: int = 0) -> dict:
    key_list = jax.random.split(jax.random.key(seed), 5)
    gate_input = scatter_about(key_list[0], (BATCH, SEQ_LEN, CHANNELS), 1.0, 6.0, ((0, 4), (1, 8)))
    values = scatter_about(key_list[1], (BATCH, SEQ_LEN, CHANNELS), 1.0, 6.0, ((0, 4), (1, 8)))
    cotangent = scatter_about(key_list[2], (BATCH, SEQ_LEN, CHANNELS), 1.0, 6.0, ((0, 4), (1, 8)))
    filter_taps = draw_filter_taps(jax.random.fold_in(key_list[4], 71), 0)
    return dict(gate_input=gate_input, values=values, cotangent=cotangent, filter_taps=filter_taps)


def dft_tables(blocks, freq_len):
    half_blocks = blocks // 2
    row_index = jnp.arange(half_blocks, dtype=jnp.int32)[:, None]
    freq_index = jnp.arange(blocks, dtype=jnp.int32)[None, :]
    angles = ((row_index * freq_index) % blocks).astype(jnp.float32) * (2.0 * math.pi / blocks)
    first_forward = jnp.stack([jnp.cos(angles), -jnp.sin(angles)], axis=1).astype(jnp.bfloat16)
    first_inverse = jnp.stack([jnp.cos(angles).T, -jnp.sin(angles).T], axis=0).astype(jnp.bfloat16)
    block_index = jnp.arange(blocks, dtype=jnp.int32)[:, None]
    lane_index = jnp.arange(128, dtype=jnp.int32)[None, :]
    twist_angles = ((block_index * lane_index) % freq_len).astype(jnp.float32) * (2.0 * math.pi / freq_len)
    twist_cosine = jnp.cos(twist_angles)[:, :, None]
    twist_sine = jnp.sin(twist_angles)[:, :, None]
    inner_index = jnp.arange(128, dtype=jnp.int32)
    inner_angles = ((inner_index[:, None] * inner_index[None, :]) % 128).astype(jnp.float32) * (2.0 * math.pi / 128)
    cosine = jnp.cos(inner_angles)
    sine_part = jnp.sin(inner_angles)
    second_forward = jnp.stack([jnp.stack([cosine, -sine_part], axis=1), jnp.stack([sine_part, cosine], axis=1)], axis=0).astype(jnp.bfloat16)
    second_inverse = jnp.stack([jnp.stack([cosine, sine_part], axis=1), jnp.stack([-sine_part, cosine], axis=1)], axis=0).astype(jnp.bfloat16)
    return (first_forward, first_inverse, twist_cosine, twist_sine, second_forward, second_inverse)


def product(einsum_form, left_side, right_side):
    return jnp.einsum(einsum_form, left_side.astype(jnp.float32), right_side.astype(jnp.float32), precision=lax.Precision.HIGHEST)


def spectrum(signal, tables):
    grouped = signal.reshape(-1, 128, signal.shape[-1])
    first = product("abc,arp->rpbc", grouped, tables[0])
    twisted = jnp.stack([first[0] * tables[2] + first[1] * tables[3], first[1] * tables[2] - first[0] * tables[3]]).astype(jnp.bfloat16)
    return product("rpbc,rbsq->spqc", twisted, tables[4])


def inverse(spectrum_half, tables, norm_scale):
    mixture = product("rpqc,rqsb->spbc", spectrum_half, tables[5])
    twisted = jnp.stack([mixture[0] * tables[2] - mixture[1] * tables[3], mixture[1] * tables[2] + mixture[0] * tables[3]]).astype(jnp.bfloat16)
    rows = product("rpbc,rpa->abc", twisted, tables[1]) * norm_scale
    return rows.reshape(-1, rows.shape[-1])


def times_spec(left_spec, right_spec):
    return jnp.stack([left_spec[0] * right_spec[0] - left_spec[1] * right_spec[1], left_spec[0] * right_spec[1] + left_spec[1] * right_spec[0]]).astype(jnp.bfloat16)


def times_conj(left_spec, right_spec):
    return jnp.stack([left_spec[0] * right_spec[0] + left_spec[1] * right_spec[1], left_spec[1] * right_spec[0] - left_spec[0] * right_spec[1]]).astype(jnp.bfloat16)


def reference(gate_input, values, cotangent, filter_taps):
    batch_size = gate_input.shape[0]
    seq_len = gate_input.shape[1]
    channels = gate_input.shape[2]
    freq_len = 2 * seq_len
    blocks = seq_len // 64
    tables = dft_tables(blocks, freq_len)
    norm_scale = 1.0 / freq_len
    conv_grad = (cotangent.astype(jnp.float32) * gate_input.astype(jnp.float32)).astype(jnp.bfloat16)
    group_width = min(128, channels)
    group_count = channels // group_width
    value_groups = values.reshape(batch_size, seq_len, group_count, group_width).transpose(2, 0, 1, 3)
    grad_groups = conv_grad.reshape(batch_size, seq_len, group_count, group_width).transpose(2, 0, 1, 3)
    filter_groups = filter_taps.astype(jnp.bfloat16).reshape(seq_len, group_count, group_width).transpose(1, 0, 2)

    def per_group(inputs):
        value_block, grad_block, filter_block = inputs
        filter_spec = spectrum(filter_block, tables)
        conv_list = []
        back_list = []
        taps_sum = jnp.zeros((seq_len, group_width), jnp.float32)
        for member in range(batch_size):
            value_spec = spectrum(value_block[member], tables)
            conv_list.append(inverse(times_spec(value_spec, filter_spec), tables, norm_scale).astype(jnp.bfloat16))
            grad_spec = spectrum(grad_block[member], tables)
            back_list.append(inverse(times_conj(grad_spec, filter_spec), tables, norm_scale).astype(jnp.bfloat16))
            taps_sum = taps_sum + inverse(times_conj(grad_spec, value_spec), tables, norm_scale)
        return jnp.stack(conv_list), jnp.stack(back_list), taps_sum

    conv_groups, back_groups, taps_groups = lax.map(per_group, (value_groups, grad_groups, filter_groups))
    conv = conv_groups.transpose(1, 2, 0, 3).reshape(batch_size, seq_len, channels)
    values_grad = back_groups.transpose(1, 2, 0, 3).reshape(batch_size, seq_len, channels)
    filter_grad = taps_groups.transpose(1, 0, 2).reshape(seq_len, channels)
    output = (gate_input.astype(jnp.float32) * conv.astype(jnp.float32)).astype(jnp.bfloat16)
    gate_grad = (cotangent.astype(jnp.float32) * conv.astype(jnp.float32)).astype(jnp.bfloat16)
    return (output, gate_grad, values_grad, filter_grad)
```

```python
import functools
import math

import jax
import jax.numpy as jnp
import numpy as np
from jax import lax
from jax.experimental import pallas as pl
from jax.experimental.pallas import tpu as pltpu
from jax.sharding import PartitionSpec as P

MESH = pl.DeviceIdType.MESH
WIDTH = 256
TABLE_LIMIT = 8 * 2**20


def odd_tables(seq_len):
    turns = np.outer(2 * np.arange(seq_len) + 1, np.arange(seq_len)) % (4 * seq_len)
    angles = turns * (2.0 * math.pi / (4 * seq_len))
    forward = np.concatenate([np.cos(angles), -np.sin(angles)], axis=0)
    inverse = forward.T / seq_len
    return jnp.asarray(forward, jnp.bfloat16), jnp.asarray(inverse, jnp.bfloat16)


def dot(left, right):
    return jnp.dot(left, right, preferred_element_type=jnp.float32)


def kernel(
    dims,
    gate_hbm, values_hbm, cot_hbm, taps_hbm, forward_hbm, inverse_hbm,
    out_ref, gate_grad_ref, values_grad_ref, filter_grad_ref,
    gate, cot, taps, forward, inverse, taps_half, grad_rows,
    value_cols, grad_cols, taps_cols, filter_spec, value_spec, mixed, mixed_taps,
    conv_cols, back_cols, partial, partial_in, summed, conv_rows, back_rows, summed_rows,
    load_sem, h_sem, hg_sem, v_sem, g_sem, c_sem, b_sem, t_sem, f_sem,
):
    ctx, dp, rows, seq_len, local, chunks = dims
    width = local // chunks
    part = seq_len // dp
    own_rows = part // ctx
    me = lax.axis_index("ctx")
    group = lax.axis_index("dp")

    def columns(owner, chunk):
        return pl.ds(pl.multiple_of(owner * local + chunk * width, width), width)

    def block(index, size):
        return pl.ds(pl.multiple_of(index * size, size), size)

    def remote(src, dst, sems, device):
        return pltpu.make_async_remote_copy(
            src_ref=src, dst_ref=dst, send_sem=sems[0], recv_sem=sems[1],
            device_id=device, device_id_type=MESH,
        )

    def over(count, body):
        def step(index, carry):
            body(index)
            return carry

        lax.fori_loop(1, count, step, 0)

    def exchange(source, target, sems, pick):
        def sent(offset):
            peer = lax.rem(me + offset, ctx)
            return remote(source(peer), target(me), pick(sems, offset), {"ctx": peer})

        def received(offset):
            peer = lax.rem(me + ctx - offset, ctx)
            return remote(source(me), target(peer), pick(sems, offset), {"ctx": peer})

        own = pltpu.make_async_copy(source(me), target(me), pick(sems, 0)[0])

        def start():
            own.start()
            over(ctx, lambda offset: sent(offset).start())

        def arrive():
            own.wait()
            over(ctx, lambda offset: received(offset).wait_recv())

        def leave():
            over(ctx, lambda offset: sent(offset).wait_send())

        return start, arrive, leave

    def picker(chunk):
        return lambda sems, offset: (sems.at[0, chunk, offset], sems.at[1, chunk, offset])

    loads = [
        pltpu.make_async_copy(src, dst, load_sem.at[at])
        for at, (src, dst) in enumerate(
            [(taps_hbm, taps), (gate_hbm, gate), (cot_hbm, cot),
             (forward_hbm, forward), (inverse_hbm, inverse)]
        )
    ]
    for load in loads:
        load.start()

    barrier = pltpu.get_barrier_semaphore()
    over(ctx, lambda offset: pl.semaphore_signal(
        barrier, inc=1, device_id={"ctx": lax.rem(me + offset, ctx)}, device_id_type=MESH))
    over(dp, lambda offset: pl.semaphore_signal(
        barrier, inc=1, device_id={"dp": lax.rem(group + offset, dp)}, device_id_type=MESH))
    pl.semaphore_wait(barrier, ctx + dp - 2)

    span = range(chunks)
    taps_way = [
        exchange(
            lambda peer, j=j: taps_half.at[:, columns(peer, j)],
            lambda owner, j=j: taps_cols.at[
                j, pl.ds(pl.multiple_of(group * part + owner * own_rows, own_rows), own_rows), :],
            h_sem, picker(j),
        ) for j in span
    ]
    values_way = [
        exchange(
            lambda peer, j=j: values_hbm.at[:, columns(peer, j)],
            lambda owner, j=j: value_cols.at[j, block(owner, rows), :],
            v_sem, picker(j),
        ) for j in span
    ]
    grad_way = [
        exchange(
            lambda peer, j=j: grad_rows.at[:, columns(peer, j)],
            lambda owner, j=j: grad_cols.at[j, block(owner, rows), :],
            g_sem, picker(j),
        ) for j in span
    ]
    conv_way = [
        exchange(
            lambda peer, j=j: conv_cols.at[j, block(peer, rows), :],
            lambda owner, j=j: conv_rows.at[:, columns(owner, j)],
            c_sem, picker(j),
        ) for j in span
    ]
    back_way = [
        exchange(
            lambda peer, j=j: back_cols.at[j, block(peer, rows), :],
            lambda owner, j=j: back_rows.at[:, columns(owner, j)],
            b_sem, picker(j),
        ) for j in span
    ]
    summed_way = [
        exchange(
            lambda peer, j=j: summed.at[j, block(peer, own_rows), :],
            lambda owner, j=j: summed_rows.at[:, columns(owner, j)],
            f_sem, picker(j),
        ) for j in span
    ]

    loads[0].wait()
    taps_half[...] = taps[...].astype(jnp.bfloat16)
    for start, _, _ in taps_way:
        start()
    for start, _, _ in values_way:
        start()
    loads[1].wait()
    loads[2].wait()

    def grad_band(index, carry):
        band = block(index, 16)
        product = gate[band, :].astype(jnp.float32) * cot[band, :].astype(jnp.float32)
        grad_rows[band, :] = product.astype(jnp.bfloat16)
        return carry

    lax.fori_loop(0, rows // 16, grad_band, 0)
    for start, _, _ in grad_way:
        start()

    for _, arrive, _ in taps_way:
        arrive()

    def gathered(offset, owner):
        peer = lax.rem(group + offset, dp)
        held = taps_cols.at[:, block(owner, part), :]
        return remote(held, held, (hg_sem.at[0, offset], hg_sem.at[1, offset]), {"dp": peer})

    over(dp, lambda offset: gathered(offset, group).start())
    loads[3].wait()
    over(dp, lambda offset: gathered(offset, lax.rem(group + dp - offset, dp)).wait_recv())

    tile = 256
    tiles = seq_len // tile

    def spectrum_tile(index, signal):
        real = dot(forward[block(index, tile), :], signal)
        imag = dot(forward[pl.ds(pl.multiple_of(seq_len + index * tile, tile), tile), :], signal)
        return real, imag

    def halves(index):
        return block(index, tile), pl.ds(pl.multiple_of(seq_len + index * tile, tile), tile)

    for j in span:
        def filter_tile(index, carry, j=j):
            upper, lower = halves(index)
            real, imag = spectrum_tile(index, taps_cols[j])
            filter_spec[j, upper, :] = real
            filter_spec[j, lower, :] = imag
            return carry

        lax.fori_loop(0, tiles, filter_tile, 0)

    for j in span:
        values_way[j][1]()

        def value_tile(index, carry, j=j):
            upper, lower = halves(index)
            real, imag = spectrum_tile(index, value_cols[j])
            value_spec[j, upper, :] = real
            value_spec[j, lower, :] = imag
            taps_real, taps_imag = filter_spec[j, upper, :], filter_spec[j, lower, :]
            mixed[upper, :] = (real * taps_real - imag * taps_imag).astype(jnp.bfloat16)
            mixed[lower, :] = (real * taps_imag + imag * taps_real).astype(jnp.bfloat16)
            return carry

        lax.fori_loop(0, tiles, value_tile, 0)
        if j == 0:
            loads[4].wait()

        def conv_tile(index, carry, j=j):
            band = block(index, tile)
            conv_cols[j, band, :] = dot(inverse[band, :], mixed[...]).astype(jnp.bfloat16)
            return carry

        lax.fori_loop(0, tiles, conv_tile, 0)
        conv_way[j][0]()

    def reduced(j, offset, owner, slot_of):
        peer = lax.rem(group + offset, dp)
        return remote(
            partial.at[j, block(owner, part), :], partial_in.at[j, offset],
            (t_sem.at[0, j, offset], t_sem.at[1, j, offset]), {"dp": peer})

    def finish(j):
        over(dp, lambda offset: reduced(j, offset, group, 0).wait_recv())
        total = partial[j, block(group, part), :].astype(jnp.float32)
        for offset in range(1, dp):
            total = total + partial_in[j, offset].astype(jnp.float32)
        summed[j] = total.astype(jnp.bfloat16)
        summed_way[j][0]()

    for j in span:
        grad_way[j][1]()

        def grad_tile(index, carry, j=j):
            upper, lower = halves(index)
            real, imag = spectrum_tile(index, grad_cols[j])
            value_real, value_imag = value_spec[j, upper, :], value_spec[j, lower, :]
            mixed_taps[upper, :] = (real * value_real + imag * value_imag).astype(jnp.bfloat16)
            mixed_taps[lower, :] = (imag * value_real - real * value_imag).astype(jnp.bfloat16)
            taps_real, taps_imag = filter_spec[j, upper, :], filter_spec[j, lower, :]
            mixed[upper, :] = (real * taps_real + imag * taps_imag).astype(jnp.bfloat16)
            mixed[lower, :] = (imag * taps_real - real * taps_imag).astype(jnp.bfloat16)
            return carry

        lax.fori_loop(0, tiles, grad_tile, 0)

        def taps_tile(index, carry, j=j):
            band = block(index, tile)
            partial[j, band, :] = dot(inverse[band, :], mixed_taps[...]).astype(jnp.bfloat16)
            return carry

        lax.fori_loop(0, tiles, taps_tile, 0)
        over(dp, lambda offset, j=j: reduced(
            j, offset, lax.rem(group + offset, dp), 0).start())

        def back_tile(index, carry, j=j):
            band = block(index, tile)
            back_cols[j, band, :] = dot(inverse[band, :], mixed[...]).astype(jnp.bfloat16)
            return carry

        lax.fori_loop(0, tiles, back_tile, 0)
        back_way[j][0]()
        if j > 0:
            finish(j - 1)
    finish(chunks - 1)

    for _, arrive, _ in conv_way:
        arrive()

    def gate_band(index, carry):
        band = block(index, 16)
        conv = conv_rows[band, :].astype(jnp.float32)
        out_ref[band, :] = (gate[band, :].astype(jnp.float32) * conv).astype(jnp.bfloat16)
        gate_grad_ref[band, :] = (cot[band, :].astype(jnp.float32) * conv).astype(jnp.bfloat16)
        return carry

    lax.fori_loop(0, rows // 16, gate_band, 0)
    for _, arrive, _ in summed_way:
        arrive()
    filter_grad_ref[...] = summed_rows[...].astype(jnp.float32)
    for _, arrive, _ in back_way:
        arrive()
    values_grad_ref[...] = back_rows[...]

    for ways in (taps_way, values_way, grad_way, conv_way, back_way, summed_way):
        for _, _, leave in ways:
            leave()
    over(dp, lambda offset: gathered(offset, group).wait_send())
    for j in span:
        over(dp, lambda offset, j=j: reduced(
            j, offset, lax.rem(group + offset, dp), 0).wait_send())


def in_one_kernel(gate_input, values, cotangent, filter_taps):
    ctx = lax.axis_size("ctx")
    dp = lax.axis_size("dp")
    rows, channels = values.shape[1:]
    seq_len = rows * ctx
    local = channels // ctx
    chunks = local // WIDTH
    width = local // chunks
    own_rows = filter_taps.shape[0]
    part = seq_len // dp
    forward, inverse = odd_tables(seq_len)
    half, full = jnp.bfloat16, jnp.float32
    cols = pltpu.VMEM((chunks, seq_len, width), half)
    spec = pltpu.VMEM((chunks, 2 * seq_len, width), full)
    mix = pltpu.VMEM((2 * seq_len, width), half)
    block = pltpu.VMEM((rows, channels), half)
    sems = pltpu.SemaphoreType.DMA((2, chunks, ctx))
    anywhere = pl.BlockSpec(memory_space=pl.ANY)
    vmem = pl.BlockSpec(memory_space=pltpu.VMEM)
    shape = jax.ShapeDtypeStruct((rows, channels), half)
    flops = 6 * 2 * 2 * seq_len * seq_len * local
    output, gate_grad, values_grad, filter_grad = pl.pallas_call(
        functools.partial(kernel, (ctx, dp, rows, seq_len, local, chunks)),
        out_shape=(shape, shape, shape, jax.ShapeDtypeStruct((own_rows, channels), full)),
        in_specs=[anywhere] * 6,
        out_specs=(vmem,) * 4,
        scratch_shapes=[
            block, block, pltpu.VMEM((own_rows, channels), full),
            pltpu.VMEM(forward.shape, half), pltpu.VMEM(inverse.shape, half),
            pltpu.VMEM((own_rows, channels), half), block,
            cols, cols, cols, spec, spec, mix, mix,
            cols, cols, cols, pltpu.VMEM((chunks, dp, part, width), half),
            pltpu.VMEM((chunks, part, width), half),
            block, block, pltpu.VMEM((own_rows, channels), half),
            pltpu.SemaphoreType.DMA((5,)), sems, pltpu.SemaphoreType.DMA((2, dp)),
            sems, sems, sems, sems, pltpu.SemaphoreType.DMA((2, chunks, dp)), sems,
        ],
        compiler_params=pltpu.CompilerParams(
            collective_id=0, has_side_effects=True, vmem_limit_bytes=56 * 2**20
        ),
        cost_estimate=pl.CostEstimate(
            flops=flops, bytes_accessed=16 * rows * channels, transcendentals=0
        ),
    )(gate_input[0], values[0], cotangent[0], filter_taps, forward, inverse)
    return output[None], gate_grad[None], values_grad[None], filter_grad


def dft_tables(blocks, freq_len):
    half_blocks = blocks // 2
    row_index = jnp.arange(half_blocks, dtype=jnp.int32)[:, None]
    freq_index = jnp.arange(blocks, dtype=jnp.int32)[None, :]
    angles = (row_index * freq_index % blocks).astype(jnp.float32) * (2.0 * math.pi / blocks)
    first_forward = jnp.stack([jnp.cos(angles), -jnp.sin(angles)], axis=1).astype(jnp.bfloat16)
    first_inverse = jnp.stack([jnp.cos(angles).T, -jnp.sin(angles).T], axis=0).astype(jnp.bfloat16)
    block_index = jnp.arange(blocks, dtype=jnp.int32)[:, None]
    lane_index = jnp.arange(128, dtype=jnp.int32)[None, :]
    twist_angles = (block_index * lane_index % freq_len).astype(jnp.float32) * (
        2.0 * math.pi / freq_len
    )
    twist_cosine = jnp.cos(twist_angles)[:, :, None]
    twist_sine = jnp.sin(twist_angles)[:, :, None]
    inner_index = jnp.arange(128, dtype=jnp.int32)
    inner_angles = (inner_index[:, None] * inner_index[None, :] % 128).astype(jnp.float32) * (
        2.0 * math.pi / 128
    )
    cosine = jnp.cos(inner_angles)
    sine_part = jnp.sin(inner_angles)
    second_forward = jnp.stack(
        [jnp.stack([cosine, -sine_part], axis=1), jnp.stack([sine_part, cosine], axis=1)], axis=0
    ).astype(jnp.bfloat16)
    second_inverse = jnp.stack(
        [jnp.stack([cosine, sine_part], axis=1), jnp.stack([-sine_part, cosine], axis=1)], axis=0
    ).astype(jnp.bfloat16)
    return (first_forward, first_inverse, twist_cosine, twist_sine, second_forward, second_inverse)


def first_section(signal, matrix):
    grouped = signal.reshape(-1, 128, signal.shape[-1])
    return jnp.einsum("abc,arp->rpbc", grouped, matrix, preferred_element_type=jnp.float32)


def second_section(first, tables):
    twisted = jnp.stack(
        [first[0] * tables[2] + first[1] * tables[3], first[1] * tables[2] - first[0] * tables[3]]
    ).astype(jnp.bfloat16)
    return jnp.einsum("rpbc,rbsq->spqc", twisted, tables[4], preferred_element_type=jnp.float32)


def spectrum(signal, tables):
    return second_section(first_section(signal, tables[0]), tables)


def inverse_prepare(spectrum_half, tables):
    mixture = jnp.einsum(
        "rpqc,rqsb->spbc", spectrum_half, tables[5], preferred_element_type=jnp.float32
    )
    return jnp.stack(
        [
            mixture[0] * tables[2] - mixture[1] * tables[3],
            mixture[1] * tables[2] + mixture[0] * tables[3],
        ]
    ).astype(jnp.bfloat16)


def inverse_rows(twisted, matrix, norm_scale):
    rows = (
        jnp.einsum("rpbc,rpa->abc", twisted, matrix, preferred_element_type=jnp.float32)
        * norm_scale
    )
    return rows.reshape(-1, rows.shape[-1])


def times_spec(left_spec, right_spec):
    return jnp.stack(
        [
            left_spec[0] * right_spec[0] - left_spec[1] * right_spec[1],
            left_spec[0] * right_spec[1] + left_spec[1] * right_spec[0],
        ]
    ).astype(jnp.bfloat16)


def times_conj(left_spec, right_spec):
    return jnp.stack(
        [
            left_spec[0] * right_spec[0] + left_spec[1] * right_spec[1],
            left_spec[1] * right_spec[0] - left_spec[0] * right_spec[1],
        ]
    ).astype(jnp.bfloat16)


def multiply_round(left_side, right_side):
    return (left_side.astype(jnp.float32) * right_side.astype(jnp.float32)).astype(jnp.bfloat16)


def in_steps(gate_input, values, cotangent, filter_taps):
    context_size = lax.axis_size("ctx")
    data_size = lax.axis_size("dp")
    tok_rows = values.shape[1]
    channels = values.shape[2]
    seq_len = tok_rows * context_size
    local_channels = channels // context_size
    blocks = seq_len // 64
    freq_len = 2 * seq_len
    norm_scale = 1.0 / freq_len
    tables = dft_tables(blocks, freq_len)
    filter_half = filter_taps.astype(jnp.bfloat16)
    filter_columns = lax.all_to_all(filter_half, "ctx", split_axis=1, concat_axis=0, tiled=True)
    matrix = tables[0]
    filter_first = first_section(lax.all_gather(filter_columns, "dp", axis=0, tiled=True), matrix)
    filter_spec = second_section(filter_first, tables)
    value_columns = lax.all_to_all(values[0], "ctx", split_axis=1, concat_axis=0, tiled=True)
    value_spec = spectrum(value_columns, tables)
    conv_columns = inverse_rows(
        inverse_prepare(times_spec(value_spec, filter_spec), tables), tables[1], norm_scale
    ).astype(jnp.bfloat16)
    conv_rows = lax.all_to_all(conv_columns, "ctx", split_axis=0, concat_axis=1, tiled=True)
    output = multiply_round(gate_input[0], conv_rows)
    gate_grad = multiply_round(cotangent[0], conv_rows)
    grad_rows = multiply_round(cotangent[0], gate_input[0])
    grad_columns = lax.all_to_all(grad_rows, "ctx", split_axis=1, concat_axis=0, tiled=True)
    grad_spec = spectrum(grad_columns, tables)
    back_columns = inverse_rows(
        inverse_prepare(times_conj(grad_spec, filter_spec), tables), tables[1], norm_scale
    ).astype(jnp.bfloat16)
    values_grad = lax.all_to_all(back_columns, "ctx", split_axis=0, concat_axis=1, tiled=True)
    filter_twisted = inverse_prepare(times_conj(grad_spec, value_spec), tables)
    whole_rows = inverse_rows(filter_twisted, tables[1], norm_scale)
    reordered = whole_rows.reshape(data_size, context_size, tok_rows // data_size, local_channels)
    reordered = reordered.transpose(1, 0, 2, 3).reshape(seq_len, local_channels)
    received_rows = lax.all_to_all(
        reordered.astype(jnp.bfloat16), "ctx", split_axis=0, concat_axis=1, tiled=True
    ).astype(reordered.dtype)
    filter_grad = lax.psum_scatter(
        received_rows.astype(jnp.bfloat16), "dp", scatter_dimension=0, tiled=True
    ).astype(jnp.float32)
    return (output[None], gate_grad[None], values_grad[None], filter_grad)


def on_device(gate_input, values, cotangent, filter_taps):
    rows, channels = values.shape[1:]
    context_size = lax.axis_size("ctx")
    seq_len = rows * context_size
    table_bytes = 2 * 2 * 2 * seq_len * seq_len
    if table_bytes <= TABLE_LIMIT and channels % (WIDTH * context_size) == 0:
        return in_one_kernel(gate_input, values, cotangent, filter_taps)
    return in_steps(gate_input, values, cotangent, filter_taps)


def solution(mesh):
    in_specs = (
        P("dp", "ctx", None),
        P("dp", "ctx", None),
        P("dp", "ctx", None),
        P(("dp", "ctx"), None),
    )
    out_specs = (
        P("dp", "ctx", None),
        P("dp", "ctx", None),
        P("dp", "ctx", None),
        P(("dp", "ctx"), None),
    )
    return jax.shard_map(
        on_device, mesh=mesh, in_specs=in_specs, out_specs=out_specs, check_vma=False
    )
```

```python
import functools
import math

import jax
import jax.numpy as jnp
import numpy as np
from jax import lax
from jax.experimental import pallas as pl
from jax.experimental.pallas import tpu as pltpu
from jax.sharding import PartitionSpec as P

MESH = pl.DeviceIdType.MESH
WIDTH = 256
TABLE_LIMIT = 8 * 2**20
TILE = 256
OUTER_EIGHTHS = 2


def odd_tables(seq_len):
    turns = np.outer(2 * np.arange(seq_len) + 1, np.arange(seq_len)) % (4 * seq_len)
    angles = turns * (2.0 * math.pi / (4 * seq_len))
    forward = np.concatenate([np.cos(angles), -np.sin(angles)], axis=0)
    inverse = forward.T / seq_len
    forward = np.stack([forward[:, : seq_len // 2], forward[:, seq_len // 2 :]])
    return jnp.asarray(forward, jnp.bfloat16), jnp.asarray(inverse, jnp.bfloat16)


def dot(left, right):
    return jnp.dot(left, right, preferred_element_type=jnp.float32)


def loop(first, last, body):
    def step(index, carry):
        body(index)
        return carry

    lax.fori_loop(first, last, step, 0)


def kernel(
    dims,
    gate_hbm, values_hbm, cot_hbm, taps_hbm, forward_hbm, inverse_hbm,
    out_ref, gate_grad_ref, values_grad_ref, filter_grad_ref,
    gate, cot, taps, forward, inverse, taps_half, signal_rows,
    near, whole, taps_cols, mixed_near, mixed_far, mixed_taps,
    near_cols, far_cols, partial, partial_in, summed, result_rows, summed_rows,
    load_sem, gather_sem, reduce_sem,
    near_sem, cross_sem, far_sem, taps_sem, taps_cross_sem, back_near_sem, back_far_sem,
    summed_sem, summed_cross_sem,
):
    ctx, dp, rows, seq_len, outer, inner = dims
    side = ctx // 2
    most = max(outer, inner)
    part = seq_len // dp
    own_rows = part // ctx
    half_len = seq_len // 2
    me = lax.axis_index("ctx")
    group = lax.axis_index("dp")
    half = me // side
    place = lax.rem(me, side)
    low = half == 0
    early = group * part < half_len

    def counts(owner):
        first = outer + (owner // side) * (inner - outer)
        second = outer + inner - first
        return first, second, lax.rem(owner, side) // (side // 2)

    def count(owner):
        first, second, late = counts(owner)
        return first + late * (second - first)

    def columns(owner, chunk):
        first, second, late = counts(owner)
        at = lax.rem(owner, side)
        early_at = at - late * (at - side // 2)
        base = early_at * first + (at - early_at) * second
        return pl.ds(pl.multiple_of((base + chunk) * WIDTH, WIDTH), WIDTH)

    def block(index, size):
        return pl.ds(pl.multiple_of(index * size, size), size)

    def remote(src, dst, send_sem, recv_sem, device):
        return pltpu.make_async_remote_copy(
            src_ref=src, dst_ref=dst, send_sem=send_sem, recv_sem=recv_sem,
            device_id=device, device_id_type=MESH,
        )

    def peer_at(offset, crossing):
        where = lax.rem(place + offset + side, side)
        return (1 - half if crossing else half) * side + where

    class Exchange:
        def __init__(self, refs, sems, crossing, inbound):
            self.refs, self.sems, self.crossing, self.inbound = refs, sems, crossing, inbound

        def own(self, chunk):
            source, target = self.refs(chunk, me, me)
            return pltpu.make_async_copy(source, target, self.sems.at[1, chunk, 0])

        def to(self, chunk, offset):
            peer = peer_at(offset, self.crossing)
            source, target = self.refs(chunk, me, peer)
            return remote(source, target, self.sems.at[0, chunk, offset],
                          self.sems.at[1, chunk, offset], {"ctx": peer})

        def back(self, chunk, offset):
            peer = peer_at(-offset, self.crossing)
            source, target = self.refs(chunk, peer, me)
            return remote(source, target, self.sems.at[0, chunk, offset],
                          self.sems.at[1, chunk, offset], {"ctx": peer})

        def each(self, chunk, sending, act):
            def one(offset):
                peer = peer_at(offset if sending else -offset, self.crossing)
                counted = peer if sending == self.inbound else me

                @pl.when(chunk < count(counted))
                def _():
                    act(offset)

            loop(0 if self.crossing else 1, side, one)

        def start(self, chunk):
            self.each(chunk, True, lambda offset: self.to(chunk, offset).start())
            if not self.crossing:
                @pl.when(chunk < count(me))
                def _():
                    self.own(chunk).start()

        def arrive(self, chunk):
            self.each(chunk, False, lambda offset: self.back(chunk, offset).wait_recv())
            if not self.crossing:
                @pl.when(chunk < count(me))
                def _():
                    self.own(chunk).wait()

        def leave(self, chunk):
            self.each(chunk, True, lambda offset: self.to(chunk, offset).wait_send())

    def near_refs(chunk, sender, receiver):
        return (signal_rows.at[0, :, columns(receiver, chunk)],
                near.at[chunk, block(lax.rem(sender, side), rows), :])

    def cross_refs(chunk, sender, receiver):
        return (signal_rows.at[0, :, columns(receiver, chunk)],
                whole.at[chunk, block(sender, rows), :])

    def far_refs(chunk, sender, receiver):
        return (signal_rows.at[1, :, columns(receiver, chunk)],
                whole.at[chunk, block(sender, rows), :])

    def taps_refs(chunk, sender, receiver):
        return (taps_half.at[:, columns(receiver, chunk)],
                taps_cols.at[chunk, block(group * ctx + sender, own_rows), :])

    def back_near_refs(chunk, sender, receiver):
        return (near_cols.at[chunk, block(lax.rem(receiver, side), rows), :],
                result_rows.at[half, :, columns(sender, chunk)])

    def back_far_refs(chunk, sender, receiver):
        return (far_cols.at[chunk, block(lax.rem(receiver, side), rows), :],
                result_rows.at[1 - half, :, columns(sender, chunk)])

    def summed_refs(chunk, sender, receiver):
        return (summed.at[chunk, block(receiver, own_rows), :],
                summed_rows.at[sender // side, :, columns(sender, chunk)])

    near_way = Exchange(near_refs, near_sem, False, True)
    cross_way = Exchange(cross_refs, cross_sem, True, True)
    far_way = Exchange(far_refs, far_sem, False, True)
    taps_way = Exchange(taps_refs, taps_sem, False, True)
    taps_cross_way = Exchange(taps_refs, taps_cross_sem, True, True)
    back_near_way = Exchange(back_near_refs, back_near_sem, False, False)
    back_far_way = Exchange(back_far_refs, back_far_sem, False, False)
    summed_way = Exchange(summed_refs, summed_sem, False, False)
    summed_cross_way = Exchange(summed_refs, summed_cross_sem, True, False)

    loads = [
        pltpu.make_async_copy(src, dst, load_sem.at[at])
        for at, (src, dst) in enumerate(
            [(taps_hbm, taps), (values_hbm, signal_rows.at[half]), (gate_hbm, gate),
             (cot_hbm, cot), (forward_hbm, forward), (inverse_hbm, inverse)]
        )
    ]
    for load in loads:
        load.start()

    barrier = pltpu.get_barrier_semaphore()
    loop(1, ctx, lambda offset: pl.semaphore_signal(
        barrier, inc=1, device_id={"ctx": lax.rem(me + offset, ctx)}, device_id_type=MESH))
    loop(1, dp, lambda offset: pl.semaphore_signal(
        barrier, inc=1, device_id={"dp": lax.rem(group + offset, dp)}, device_id_type=MESH))
    loads[0].wait()
    taps_half[...] = taps[...].astype(jnp.bfloat16)
    loads[2].wait()
    loads[3].wait()

    def grad_band(index):
        band = block(index, 16)
        product = gate[band, :].astype(jnp.float32) * cot[band, :].astype(jnp.float32)
        signal_rows[1 - half, band, :] = product.astype(jnp.bfloat16)

    loop(0, rows // 16, grad_band)
    loads[1].wait()
    pl.semaphore_wait(barrier, ctx + dp - 2)

    def send_in(chunk):
        taps_cross_way.start(chunk)
        taps_way.start(chunk)
        cross_way.start(chunk)
        near_way.start(chunk)
        far_way.start(chunk)

    loop(0, most, send_in)
    mine = count(me)

    def gathered(chunk, offset, owner):
        peer = lax.rem(group + offset, dp)
        held = taps_cols.at[chunk, block(owner, part), :]
        return remote(held, held, gather_sem.at[0, chunk, offset], gather_sem.at[1, chunk, offset],
                      {"dp": peer})

    def gather(chunk):
        taps_cross_way.arrive(chunk)
        taps_way.arrive(chunk)
        loop(1, dp, lambda offset: gathered(chunk, offset, group).start())

    loop(0, mine, gather)
    loads[4].wait()
    loads[5].wait()
    sign = jnp.where(low, 1.0, -1.0).astype(jnp.float32)
    keep = jnp.where(low, 1.0, 0.0).astype(jnp.float32)

    def reduces(owner):
        return jnp.logical_or(low, owner * part < half_len)

    def reduced(chunk, offset, owner):
        return remote(
            partial.at[chunk, block(owner, part), :], partial_in.at[chunk, offset],
            reduce_sem.at[0, chunk, offset], reduce_sem.at[1, chunk, offset],
            {"dp": lax.rem(group + offset, dp)})

    def reduce_each(chunk, act):
        def one(offset):
            owner = lax.rem(group + offset, dp)

            @pl.when(reduces(owner))
            def _():
                act(reduced(chunk, offset, owner))

        loop(1, dp, one)

    def finish(chunk):
        @pl.when(reduces(group))
        def _():
            loop(1, dp, lambda offset: reduced(chunk, offset, group).wait_recv())
            total = partial[chunk, block(group, part), :].astype(jnp.float32)
            for offset in range(1, dp):
                total = total + partial_in[chunk, offset].astype(jnp.float32)
            summed[chunk] = total.astype(jnp.bfloat16)
            summed_cross_way.start(chunk)
            summed_way.start(chunk)

    def work(chunk):
        cross_way.arrive(chunk)
        near_way.arrive(chunk)
        far_way.arrive(chunk)
        loop(1, dp, lambda offset: gathered(
            chunk, offset, lax.rem(group + dp - offset, dp)).wait_recv())
        first, second = pl.ds(0, half_len), pl.ds(half_len, half_len)

        def frequencies(index):
            upper = block(index, TILE)
            lower = pl.ds(pl.multiple_of(seq_len + index * TILE, TILE), TILE)

            def split(band):
                taps_part = dot(forward[0, band, :], taps_cols[chunk, first, :]) + dot(
                    forward[1, band, :], taps_cols[chunk, second, :])
                near_part = dot(forward[half, band, :], near[chunk])
                return (taps_part, near_part, dot(forward[0, band, :], whole[chunk, first, :]),
                        dot(forward[1, band, :], whole[chunk, second, :]))

            taps_real, near_real, early_real, late_real = split(upper)
            taps_imag, near_imag, early_imag, late_imag = split(lower)
            taps_imag = taps_imag * sign
            far_real, far_imag = early_real + late_real, early_imag + late_imag
            half_type = jnp.bfloat16
            mixed_near[upper, :] = (near_real * taps_real - near_imag * taps_imag).astype(half_type)
            mixed_near[lower, :] = (near_real * taps_imag + near_imag * taps_real).astype(half_type)
            mixed_far[upper, :] = (far_real * taps_real + far_imag * taps_imag).astype(half_type)
            mixed_far[lower, :] = (far_imag * taps_real - far_real * taps_imag).astype(half_type)
            part_real, part_imag = early_real * keep + late_real, early_imag * keep + late_imag
            mixed_taps[upper, :] = (part_real * near_real + part_imag * near_imag).astype(half_type)
            mixed_taps[lower, :] = (
                (part_imag * near_real - part_real * near_imag) * sign).astype(half_type)

        loop(0, seq_len // TILE, frequencies)

        def inverse_rows(index):
            return inverse[pl.ds(pl.multiple_of(half * half_len + index * TILE, TILE), TILE), :]

        def near_tile(index):
            near_cols[chunk, block(index, TILE), :] = dot(
                inverse_rows(index), mixed_near[...]).astype(jnp.bfloat16)

        def far_tile(index):
            far_cols[chunk, block(index, TILE), :] = dot(
                inverse_rows(index), mixed_far[...]).astype(jnp.bfloat16)

        def taps_tile(index):
            band = block(index, TILE)
            partial[chunk, band, :] = dot(inverse[band, :], mixed_taps[...]).astype(jnp.bfloat16)

        loop(0, half_len // TILE, near_tile)
        back_near_way.start(chunk)
        loop(0, (2 - half) * (half_len // TILE), taps_tile)
        reduce_each(chunk, lambda copy: copy.start())
        loop(0, half_len // TILE, far_tile)
        back_far_way.start(chunk)

        @pl.when(chunk > 0)
        def _():
            finish(chunk - 1)

    loop(0, mine, work)
    finish(mine - 1)

    def results(chunk):
        back_near_way.arrive(chunk)
        back_far_way.arrive(chunk)

    loop(0, most, results)

    def gate_band(index):
        band = block(index, 16)
        conv = result_rows[0, band, :].astype(jnp.float32)
        out_ref[band, :] = (gate[band, :].astype(jnp.float32) * conv).astype(jnp.bfloat16)
        gate_grad_ref[band, :] = (cot[band, :].astype(jnp.float32) * conv).astype(jnp.bfloat16)

    loop(0, rows // 16, gate_band)
    values_grad_ref[...] = result_rows[1]

    @pl.when(low)
    def _():
        loop(0, most, summed_way.arrive)

    @pl.when(jnp.logical_not(low))
    def _():
        loop(0, most, summed_cross_way.arrive)

    filter_grad_ref[...] = summed_rows[0].astype(jnp.float32)

    @pl.when(early)
    def _():
        @pl.when(low)
        def _():
            loop(0, most, summed_cross_way.arrive)

        @pl.when(jnp.logical_not(low))
        def _():
            loop(0, most, summed_way.arrive)

        filter_grad_ref[...] += summed_rows[1].astype(jnp.float32)

    def sent(chunk):
        for way in (taps_cross_way, taps_way, cross_way, near_way, far_way,
                    back_near_way, back_far_way):
            way.leave(chunk)

    loop(0, most, sent)

    def sent_sums(chunk):
        loop(1, dp, lambda offset: gathered(chunk, offset, group).wait_send())
        reduce_each(chunk, lambda copy: copy.wait_send())

        @pl.when(reduces(group))
        def _():
            summed_cross_way.leave(chunk)
            summed_way.leave(chunk)

    loop(0, mine, sent_sums)


def in_one_kernel(gate_input, values, cotangent, filter_taps):
    ctx = lax.axis_size("ctx")
    dp = lax.axis_size("dp")
    rows, channels = values.shape[1:]
    seq_len = rows * ctx
    own_rows = filter_taps.shape[0]
    part = seq_len // dp
    pair = channels // WIDTH // (ctx // 4)
    outer = max(1, pair * OUTER_EIGHTHS // 8)
    inner = pair - outer
    most = max(outer, inner)
    forward, inverse = odd_tables(seq_len)
    half, full = jnp.bfloat16, jnp.float32
    whole = pltpu.VMEM((most, seq_len, WIDTH), half)
    halves = pltpu.VMEM((most, seq_len // 2, WIDTH), half)
    mix = pltpu.VMEM((2 * seq_len, WIDTH), half)
    block = pltpu.VMEM((rows, channels), half)
    pair_rows = pltpu.VMEM((2, rows, channels), half)
    sems = pltpu.SemaphoreType.DMA((2, most, ctx // 2))
    groups = pltpu.SemaphoreType.DMA((2, most, dp))
    anywhere = pl.BlockSpec(memory_space=pl.ANY)
    vmem = pl.BlockSpec(memory_space=pltpu.VMEM)
    shape = jax.ShapeDtypeStruct((rows, channels), half)
    flops = 12 * seq_len * seq_len * (channels // ctx) * 2
    output, gate_grad, values_grad, filter_grad = pl.pallas_call(
        functools.partial(kernel, (ctx, dp, rows, seq_len, outer, inner)),
        out_shape=(shape, shape, shape, jax.ShapeDtypeStruct((own_rows, channels), full)),
        in_specs=[anywhere] * 6,
        out_specs=(vmem,) * 4,
        scratch_shapes=[
            block, block, pltpu.VMEM((own_rows, channels), full),
            pltpu.VMEM(forward.shape, half), pltpu.VMEM(inverse.shape, half),
            pltpu.VMEM((own_rows, channels), half), pair_rows,
            halves, whole, whole, mix, mix, mix,
            halves, halves, whole, pltpu.VMEM((most, dp, part, WIDTH), half),
            pltpu.VMEM((most, part, WIDTH), half),
            pair_rows, pltpu.VMEM((2, own_rows, channels), half),
            pltpu.SemaphoreType.DMA((6,)), groups, groups,
        ] + [sems] * 9,
        compiler_params=pltpu.CompilerParams(
            collective_id=0, has_side_effects=True, vmem_limit_bytes=58 * 2**20
        ),
        cost_estimate=pl.CostEstimate(
            flops=flops, bytes_accessed=16 * rows * channels, transcendentals=0
        ),
    )(gate_input[0], values[0], cotangent[0], filter_taps, forward, inverse)
    return output[None], gate_grad[None], values_grad[None], filter_grad


def dft_tables(blocks, freq_len):
    half_blocks = blocks // 2
    row_index = jnp.arange(half_blocks, dtype=jnp.int32)[:, None]
    freq_index = jnp.arange(blocks, dtype=jnp.int32)[None, :]
    angles = (row_index * freq_index % blocks).astype(jnp.float32) * (2.0 * math.pi / blocks)
    first_forward = jnp.stack([jnp.cos(angles), -jnp.sin(angles)], axis=1).astype(jnp.bfloat16)
    first_inverse = jnp.stack([jnp.cos(angles).T, -jnp.sin(angles).T], axis=0).astype(jnp.bfloat16)
    block_index = jnp.arange(blocks, dtype=jnp.int32)[:, None]
    lane_index = jnp.arange(128, dtype=jnp.int32)[None, :]
    twist_angles = (block_index * lane_index % freq_len).astype(jnp.float32) * (
        2.0 * math.pi / freq_len
    )
    twist_cosine = jnp.cos(twist_angles)[:, :, None]
    twist_sine = jnp.sin(twist_angles)[:, :, None]
    inner_index = jnp.arange(128, dtype=jnp.int32)
    inner_angles = (inner_index[:, None] * inner_index[None, :] % 128).astype(jnp.float32) * (
        2.0 * math.pi / 128
    )
    cosine = jnp.cos(inner_angles)
    sine_part = jnp.sin(inner_angles)
    second_forward = jnp.stack(
        [jnp.stack([cosine, -sine_part], axis=1), jnp.stack([sine_part, cosine], axis=1)], axis=0
    ).astype(jnp.bfloat16)
    second_inverse = jnp.stack(
        [jnp.stack([cosine, sine_part], axis=1), jnp.stack([-sine_part, cosine], axis=1)], axis=0
    ).astype(jnp.bfloat16)
    return (first_forward, first_inverse, twist_cosine, twist_sine, second_forward, second_inverse)


def first_section(signal, matrix):
    grouped = signal.reshape(-1, 128, signal.shape[-1])
    return jnp.einsum("abc,arp->rpbc", grouped, matrix, preferred_element_type=jnp.float32)


def second_section(first, tables):
    twisted = jnp.stack(
        [first[0] * tables[2] + first[1] * tables[3], first[1] * tables[2] - first[0] * tables[3]]
    ).astype(jnp.bfloat16)
    return jnp.einsum("rpbc,rbsq->spqc", twisted, tables[4], preferred_element_type=jnp.float32)


def spectrum(signal, tables):
    return second_section(first_section(signal, tables[0]), tables)


def inverse_prepare(spectrum_half, tables):
    mixture = jnp.einsum(
        "rpqc,rqsb->spbc", spectrum_half, tables[5], preferred_element_type=jnp.float32
    )
    return jnp.stack(
        [
            mixture[0] * tables[2] - mixture[1] * tables[3],
            mixture[1] * tables[2] + mixture[0] * tables[3],
        ]
    ).astype(jnp.bfloat16)


def inverse_rows(twisted, matrix, norm_scale):
    rows = (
        jnp.einsum("rpbc,rpa->abc", twisted, matrix, preferred_element_type=jnp.float32)
        * norm_scale
    )
    return rows.reshape(-1, rows.shape[-1])


def times_spec(left_spec, right_spec):
    return jnp.stack(
        [
            left_spec[0] * right_spec[0] - left_spec[1] * right_spec[1],
            left_spec[0] * right_spec[1] + left_spec[1] * right_spec[0],
        ]
    ).astype(jnp.bfloat16)


def times_conj(left_spec, right_spec):
    return jnp.stack(
        [
            left_spec[0] * right_spec[0] + left_spec[1] * right_spec[1],
            left_spec[1] * right_spec[0] - left_spec[0] * right_spec[1],
        ]
    ).astype(jnp.bfloat16)


def multiply_round(left_side, right_side):
    return (left_side.astype(jnp.float32) * right_side.astype(jnp.float32)).astype(jnp.bfloat16)


def in_steps(gate_input, values, cotangent, filter_taps):
    context_size = lax.axis_size("ctx")
    data_size = lax.axis_size("dp")
    tok_rows = values.shape[1]
    channels = values.shape[2]
    seq_len = tok_rows * context_size
    local_channels = channels // context_size
    blocks = seq_len // 64
    freq_len = 2 * seq_len
    norm_scale = 1.0 / freq_len
    tables = dft_tables(blocks, freq_len)
    filter_half = filter_taps.astype(jnp.bfloat16)
    filter_columns = lax.all_to_all(filter_half, "ctx", split_axis=1, concat_axis=0, tiled=True)
    matrix = tables[0]
    filter_first = first_section(lax.all_gather(filter_columns, "dp", axis=0, tiled=True), matrix)
    filter_spec = second_section(filter_first, tables)
    value_columns = lax.all_to_all(values[0], "ctx", split_axis=1, concat_axis=0, tiled=True)
    value_spec = spectrum(value_columns, tables)
    conv_columns = inverse_rows(
        inverse_prepare(times_spec(value_spec, filter_spec), tables), tables[1], norm_scale
    ).astype(jnp.bfloat16)
    conv_rows = lax.all_to_all(conv_columns, "ctx", split_axis=0, concat_axis=1, tiled=True)
    output = multiply_round(gate_input[0], conv_rows)
    gate_grad = multiply_round(cotangent[0], conv_rows)
    grad_rows = multiply_round(cotangent[0], gate_input[0])
    grad_columns = lax.all_to_all(grad_rows, "ctx", split_axis=1, concat_axis=0, tiled=True)
    grad_spec = spectrum(grad_columns, tables)
    back_columns = inverse_rows(
        inverse_prepare(times_conj(grad_spec, filter_spec), tables), tables[1], norm_scale
    ).astype(jnp.bfloat16)
    values_grad = lax.all_to_all(back_columns, "ctx", split_axis=0, concat_axis=1, tiled=True)
    filter_twisted = inverse_prepare(times_conj(grad_spec, value_spec), tables)
    whole_rows = inverse_rows(filter_twisted, tables[1], norm_scale)
    reordered = whole_rows.reshape(data_size, context_size, tok_rows // data_size, local_channels)
    reordered = reordered.transpose(1, 0, 2, 3).reshape(seq_len, local_channels)
    received_rows = lax.all_to_all(
        reordered.astype(jnp.bfloat16), "ctx", split_axis=0, concat_axis=1, tiled=True
    ).astype(reordered.dtype)
    filter_grad = lax.psum_scatter(
        received_rows.astype(jnp.bfloat16), "dp", scatter_dimension=0, tiled=True
    ).astype(jnp.float32)
    return (output[None], gate_grad[None], values_grad[None], filter_grad)


def on_device(gate_input, values, cotangent, filter_taps):
    rows, channels = values.shape[1:]
    context_size = lax.axis_size("ctx")
    seq_len = rows * context_size
    table_bytes = 2 * 2 * 2 * seq_len * seq_len
    if table_bytes <= TABLE_LIMIT and context_size % 4 == 0 and channels % (WIDTH * context_size) == 0:
        return in_one_kernel(gate_input, values, cotangent, filter_taps)
    return in_steps(gate_input, values, cotangent, filter_taps)


def solution(mesh):
    in_specs = (
        P("dp", "ctx", None),
        P("dp", "ctx", None),
        P("dp", "ctx", None),
        P(("dp", "ctx"), None),
    )
    out_specs = (
        P("dp", "ctx", None),
        P("dp", "ctx", None),
        P("dp", "ctx", None),
        P(("dp", "ctx"), None),
    )
    return jax.shard_map(
        on_device, mesh=mesh, in_specs=in_specs, out_specs=out_specs, check_vma=False
    )
```

```python
import functools
import math

import jax
import jax.numpy as jnp
import numpy as np
from jax import lax
from jax.experimental import pallas as pl
from jax.experimental.pallas import tpu as pltpu
from jax.sharding import PartitionSpec as P

MESH = pl.DeviceIdType.MESH
WIDTH = 256
TABLE_LIMIT = 8 * 2**20
TILE = 256
OUTER_EIGHTHS = 4


def odd_tables(seq_len):
    turns = np.outer(2 * np.arange(seq_len) + 1, np.arange(seq_len)) % (4 * seq_len)
    angles = turns * (2.0 * math.pi / (4 * seq_len))
    forward = np.concatenate([np.cos(angles), -np.sin(angles)], axis=0)
    inverse = forward.T / seq_len
    forward = np.stack([forward[:, : seq_len // 2], forward[:, seq_len // 2 :]])
    return jnp.asarray(forward, jnp.bfloat16), jnp.asarray(inverse, jnp.bfloat16)


def dot(left, right):
    return jnp.dot(left, right, preferred_element_type=jnp.float32)


def loop(first, last, body):
    def step(index, carry):
        body(index)
        return carry

    lax.fori_loop(first, last, step, 0)


def kernel(
    dims,
    gate_hbm, values_hbm, cot_hbm, taps_hbm, forward_hbm, inverse_hbm,
    out_ref, gate_grad_ref, values_grad_ref, filter_grad_ref,
    gate, cot, taps, forward, inverse, taps_half, signal_rows,
    near, whole, taps_cols, mixed_near, mixed_far, mixed_taps,
    near_cols, far_cols, partial, partial_in, summed, result_rows, summed_rows,
    load_sem, gather_sem, reduce_sem,
    near_sem, cross_sem, far_sem, taps_sem, taps_cross_sem, back_near_sem, back_far_sem,
    summed_sem, summed_cross_sem,
):
    ctx, dp, rows, seq_len, outer, inner = dims
    side = ctx // 2
    most = max(outer, inner)
    part = seq_len // dp
    own_rows = part // ctx
    half_len = seq_len // 2
    me = lax.axis_index("ctx")
    group = lax.axis_index("dp")
    half = me // side
    place = lax.rem(me, side)
    low = half == 0
    early = group * part < half_len

    def counts(owner):
        first = outer + (owner // side) * (inner - outer)
        second = outer + inner - first
        return first, second, lax.rem(owner, side) // (side // 2)

    def count(owner):
        first, second, late = counts(owner)
        return first + late * (second - first)

    def columns(owner, chunk):
        first, second, late = counts(owner)
        at = lax.rem(owner, side)
        early_at = at - late * (at - side // 2)
        base = early_at * first + (at - early_at) * second
        return pl.ds(pl.multiple_of((base + chunk) * WIDTH, WIDTH), WIDTH)

    def block(index, size):
        return pl.ds(pl.multiple_of(index * size, size), size)

    def remote(src, dst, send_sem, recv_sem, device):
        return pltpu.make_async_remote_copy(
            src_ref=src, dst_ref=dst, send_sem=send_sem, recv_sem=recv_sem,
            device_id=device, device_id_type=MESH,
        )

    def peer_at(offset, crossing):
        where = lax.rem(place + offset + side, side)
        return (1 - half if crossing else half) * side + where

    class Exchange:
        def __init__(self, refs, sems, crossing, inbound):
            self.refs, self.sems, self.crossing, self.inbound = refs, sems, crossing, inbound

        def own(self, chunk):
            source, target = self.refs(chunk, me, me)
            return pltpu.make_async_copy(source, target, self.sems.at[1, chunk, 0])

        def to(self, chunk, offset):
            peer = peer_at(offset, self.crossing)
            source, target = self.refs(chunk, me, peer)
            return remote(source, target, self.sems.at[0, chunk, offset],
                          self.sems.at[1, chunk, offset], {"ctx": peer})

        def back(self, chunk, offset):
            peer = peer_at(-offset, self.crossing)
            source, target = self.refs(chunk, peer, me)
            return remote(source, target, self.sems.at[0, chunk, offset],
                          self.sems.at[1, chunk, offset], {"ctx": peer})

        def each(self, chunk, sending, act):
            def one(offset):
                peer = peer_at(offset if sending else -offset, self.crossing)
                counted = peer if sending == self.inbound else me

                @pl.when(chunk < count(counted))
                def _():
                    act(offset)

            loop(0 if self.crossing else 1, side, one)

        def start(self, chunk):
            self.each(chunk, True, lambda offset: self.to(chunk, offset).start())
            if not self.crossing:
                @pl.when(chunk < count(me))
                def _():
                    self.own(chunk).start()

        def arrive(self, chunk):
            self.each(chunk, False, lambda offset: self.back(chunk, offset).wait_recv())
            if not self.crossing:
                @pl.when(chunk < count(me))
                def _():
                    self.own(chunk).wait()

        def leave(self, chunk):
            self.each(chunk, True, lambda offset: self.to(chunk, offset).wait_send())

    def near_refs(chunk, sender, receiver):
        return (signal_rows.at[0, :, columns(receiver, chunk)],
                near.at[chunk, block(lax.rem(sender, side), rows), :])

    def cross_refs(chunk, sender, receiver):
        return (signal_rows.at[0, :, columns(receiver, chunk)],
                whole.at[chunk, block(sender, rows), :])

    def far_refs(chunk, sender, receiver):
        return (signal_rows.at[1, :, columns(receiver, chunk)],
                whole.at[chunk, block(sender, rows), :])

    def taps_refs(chunk, sender, receiver):
        return (taps_half.at[:, columns(receiver, chunk)],
                taps_cols.at[chunk, block(group * ctx + sender, own_rows), :])

    def back_near_refs(chunk, sender, receiver):
        return (near_cols.at[chunk, block(lax.rem(receiver, side), rows), :],
                result_rows.at[half, :, columns(sender, chunk)])

    def back_far_refs(chunk, sender, receiver):
        return (far_cols.at[chunk, block(lax.rem(receiver, side), rows), :],
                result_rows.at[1 - half, :, columns(sender, chunk)])

    def summed_refs(chunk, sender, receiver):
        return (summed.at[chunk, block(receiver, own_rows), :],
                summed_rows.at[sender // side, :, columns(sender, chunk)])

    near_way = Exchange(near_refs, near_sem, False, True)
    cross_way = Exchange(cross_refs, cross_sem, True, True)
    far_way = Exchange(far_refs, far_sem, False, True)
    taps_way = Exchange(taps_refs, taps_sem, False, True)
    taps_cross_way = Exchange(taps_refs, taps_cross_sem, True, True)
    back_near_way = Exchange(back_near_refs, back_near_sem, False, False)
    back_far_way = Exchange(back_far_refs, back_far_sem, False, False)
    summed_way = Exchange(summed_refs, summed_sem, False, False)
    summed_cross_way = Exchange(summed_refs, summed_cross_sem, True, False)

    loads = [
        pltpu.make_async_copy(src, dst, load_sem.at[at])
        for at, (src, dst) in enumerate(
            [(taps_hbm, taps), (values_hbm, signal_rows.at[half]), (gate_hbm, gate),
             (cot_hbm, cot), (forward_hbm, forward), (inverse_hbm, inverse)]
        )
    ]
    for load in loads:
        load.start()

    barrier = pltpu.get_barrier_semaphore()
    loop(1, ctx, lambda offset: pl.semaphore_signal(
        barrier, inc=1, device_id={"ctx": lax.rem(me + offset, ctx)}, device_id_type=MESH))
    loop(1, dp, lambda offset: pl.semaphore_signal(
        barrier, inc=1, device_id={"dp": lax.rem(group + offset, dp)}, device_id_type=MESH))
    loads[0].wait()
    taps_half[...] = taps[...].astype(jnp.bfloat16)
    loads[2].wait()
    loads[3].wait()

    def grad_band(index):
        band = block(index, 16)
        product = gate[band, :].astype(jnp.float32) * cot[band, :].astype(jnp.float32)
        signal_rows[1 - half, band, :] = product.astype(jnp.bfloat16)

    loop(0, rows // 16, grad_band)
    loads[1].wait()
    pl.semaphore_wait(barrier, ctx + dp - 2)

    def send_in(chunk):
        taps_cross_way.start(chunk)
        taps_way.start(chunk)
        cross_way.start(chunk)
        near_way.start(chunk)
        far_way.start(chunk)

    loop(0, most, send_in)
    mine = count(me)

    def gathered(chunk, offset, owner):
        peer = lax.rem(group + offset, dp)
        held = taps_cols.at[chunk, block(owner, part), :]
        return remote(held, held, gather_sem.at[0, chunk, offset], gather_sem.at[1, chunk, offset],
                      {"dp": peer})

    def gather(chunk):
        taps_cross_way.arrive(chunk)
        taps_way.arrive(chunk)
        loop(1, dp, lambda offset: gathered(chunk, offset, group).start())

    loop(0, mine, gather)
    loads[4].wait()
    loads[5].wait()
    sign = jnp.where(low, 1.0, -1.0).astype(jnp.float32)
    keep = jnp.where(low, 1.0, 0.0).astype(jnp.float32)

    def reduces(owner):
        return jnp.logical_or(low, owner * part < half_len)

    def reduced(chunk, offset, owner):
        return remote(
            partial.at[chunk, block(owner, part), :], partial_in.at[chunk, offset],
            reduce_sem.at[0, chunk, offset], reduce_sem.at[1, chunk, offset],
            {"dp": lax.rem(group + offset, dp)})

    def reduce_each(chunk, act):
        def one(offset):
            owner = lax.rem(group + offset, dp)

            @pl.when(reduces(owner))
            def _():
                act(reduced(chunk, offset, owner))

        loop(1, dp, one)

    def finish(chunk):
        @pl.when(reduces(group))
        def _():
            loop(1, dp, lambda offset: reduced(chunk, offset, group).wait_recv())
            total = partial[chunk, block(group, part), :].astype(jnp.float32)
            for offset in range(1, dp):
                total = total + partial_in[chunk, offset].astype(jnp.float32)
            summed[chunk] = total.astype(jnp.bfloat16)
            summed_cross_way.start(chunk)
            summed_way.start(chunk)

    def work(chunk):
        cross_way.arrive(chunk)
        near_way.arrive(chunk)
        far_way.arrive(chunk)
        loop(1, dp, lambda offset: gathered(
            chunk, offset, lax.rem(group + dp - offset, dp)).wait_recv())
        first, second = pl.ds(0, half_len), pl.ds(half_len, half_len)

        def frequencies(index):
            upper = block(index, TILE)
            lower = pl.ds(pl.multiple_of(seq_len + index * TILE, TILE), TILE)

            def split(band):
                taps_part = dot(forward[0, band, :], taps_cols[chunk, first, :]) + dot(
                    forward[1, band, :], taps_cols[chunk, second, :])
                near_part = dot(forward[half, band, :], near[chunk])
                return (taps_part, near_part, dot(forward[0, band, :], whole[chunk, first, :]),
                        dot(forward[1, band, :], whole[chunk, second, :]))

            taps_real, near_real, early_real, late_real = split(upper)
            taps_imag, near_imag, early_imag, late_imag = split(lower)
            taps_imag = taps_imag * sign
            far_real, far_imag = early_real + late_real, early_imag + late_imag
            half_type = jnp.bfloat16
            mixed_near[upper, :] = (near_real * taps_real - near_imag * taps_imag).astype(half_type)
            mixed_near[lower, :] = (near_real * taps_imag + near_imag * taps_real).astype(half_type)
            mixed_far[upper, :] = (far_real * taps_real + far_imag * taps_imag).astype(half_type)
            mixed_far[lower, :] = (far_imag * taps_real - far_real * taps_imag).astype(half_type)
            part_real, part_imag = early_real * keep + late_real, early_imag * keep + late_imag
            mixed_taps[upper, :] = (part_real * near_real + part_imag * near_imag).astype(half_type)
            mixed_taps[lower, :] = (
                (part_imag * near_real - part_real * near_imag) * sign).astype(half_type)

        loop(0, seq_len // TILE, frequencies)

        def inverse_rows(index):
            return inverse[pl.ds(pl.multiple_of(half * half_len + index * TILE, TILE), TILE), :]

        def near_tile(index):
            near_cols[chunk, block(index, TILE), :] = dot(
                inverse_rows(index), mixed_near[...]).astype(jnp.bfloat16)

        def far_tile(index):
            far_cols[chunk, block(index, TILE), :] = dot(
                inverse_rows(index), mixed_far[...]).astype(jnp.bfloat16)

        def taps_tile(index):
            band = block(index, TILE)
            partial[chunk, band, :] = dot(inverse[band, :], mixed_taps[...]).astype(jnp.bfloat16)

        loop(0, half_len // TILE, near_tile)
        back_near_way.start(chunk)
        loop(0, (2 - half) * (half_len // TILE), taps_tile)
        reduce_each(chunk, lambda copy: copy.start())
        loop(0, half_len // TILE, far_tile)
        back_far_way.start(chunk)

        @pl.when(chunk > 0)
        def _():
            finish(chunk - 1)

    loop(0, mine, work)
    finish(mine - 1)

    def results(chunk):
        back_near_way.arrive(chunk)
        back_far_way.arrive(chunk)

    loop(0, most, results)

    def gate_band(index):
        band = block(index, 16)
        conv = result_rows[0, band, :].astype(jnp.float32)
        out_ref[band, :] = (gate[band, :].astype(jnp.float32) * conv).astype(jnp.bfloat16)
        gate_grad_ref[band, :] = (cot[band, :].astype(jnp.float32) * conv).astype(jnp.bfloat16)

    loop(0, rows // 16, gate_band)
    values_grad_ref[...] = result_rows[1]

    @pl.when(low)
    def _():
        loop(0, most, summed_way.arrive)

    @pl.when(jnp.logical_not(low))
    def _():
        loop(0, most, summed_cross_way.arrive)

    filter_grad_ref[...] = summed_rows[0].astype(jnp.float32)

    @pl.when(early)
    def _():
        @pl.when(low)
        def _():
            loop(0, most, summed_cross_way.arrive)

        @pl.when(jnp.logical_not(low))
        def _():
            loop(0, most, summed_way.arrive)

        filter_grad_ref[...] += summed_rows[1].astype(jnp.float32)

    def sent(chunk):
        for way in (taps_cross_way, taps_way, cross_way, near_way, far_way,
                    back_near_way, back_far_way):
            way.leave(chunk)

    loop(0, most, sent)

    def sent_sums(chunk):
        loop(1, dp, lambda offset: gathered(chunk, offset, group).wait_send())
        reduce_each(chunk, lambda copy: copy.wait_send())

        @pl.when(reduces(group))
        def _():
            summed_cross_way.leave(chunk)
            summed_way.leave(chunk)

    loop(0, mine, sent_sums)


def in_one_kernel(gate_input, values, cotangent, filter_taps):
    ctx = lax.axis_size("ctx")
    dp = lax.axis_size("dp")
    rows, channels = values.shape[1:]
    seq_len = rows * ctx
    own_rows = filter_taps.shape[0]
    part = seq_len // dp
    pair = channels // WIDTH // (ctx // 4)
    outer = max(1, pair * OUTER_EIGHTHS // 8)
    inner = pair - outer
    most = max(outer, inner)
    forward, inverse = odd_tables(seq_len)
    half, full = jnp.bfloat16, jnp.float32
    whole = pltpu.VMEM((most, seq_len, WIDTH), half)
    halves = pltpu.VMEM((most, seq_len // 2, WIDTH), half)
    mix = pltpu.VMEM((2 * seq_len, WIDTH), half)
    block = pltpu.VMEM((rows, channels), half)
    pair_rows = pltpu.VMEM((2, rows, channels), half)
    sems = pltpu.SemaphoreType.DMA((2, most, ctx // 2))
    groups = pltpu.SemaphoreType.DMA((2, most, dp))
    anywhere = pl.BlockSpec(memory_space=pl.ANY)
    vmem = pl.BlockSpec(memory_space=pltpu.VMEM)
    shape = jax.ShapeDtypeStruct((rows, channels), half)
    flops = 12 * seq_len * seq_len * (channels // ctx) * 2
    output, gate_grad, values_grad, filter_grad = pl.pallas_call(
        functools.partial(kernel, (ctx, dp, rows, seq_len, outer, inner)),
        out_shape=(shape, shape, shape, jax.ShapeDtypeStruct((own_rows, channels), full)),
        in_specs=[anywhere] * 6,
        out_specs=(vmem,) * 4,
        scratch_shapes=[
            block, block, pltpu.VMEM((own_rows, channels), full),
            pltpu.VMEM(forward.shape, half), pltpu.VMEM(inverse.shape, half),
            pltpu.VMEM((own_rows, channels), half), pair_rows,
            halves, whole, whole, mix, mix, mix,
            halves, halves, whole, pltpu.VMEM((most, dp, part, WIDTH), half),
            pltpu.VMEM((most, part, WIDTH), half),
            pair_rows, pltpu.VMEM((2, own_rows, channels), half),
            pltpu.SemaphoreType.DMA((6,)), groups, groups,
        ] + [sems] * 9,
        compiler_params=pltpu.CompilerParams(
            collective_id=0, has_side_effects=True, vmem_limit_bytes=58 * 2**20
        ),
        cost_estimate=pl.CostEstimate(
            flops=flops, bytes_accessed=16 * rows * channels, transcendentals=0
        ),
    )(gate_input[0], values[0], cotangent[0], filter_taps, forward, inverse)
    return output[None], gate_grad[None], values_grad[None], filter_grad


def dft_tables(blocks, freq_len):
    half_blocks = blocks // 2
    row_index = jnp.arange(half_blocks, dtype=jnp.int32)[:, None]
    freq_index = jnp.arange(blocks, dtype=jnp.int32)[None, :]
    angles = (row_index * freq_index % blocks).astype(jnp.float32) * (2.0 * math.pi / blocks)
    first_forward = jnp.stack([jnp.cos(angles), -jnp.sin(angles)], axis=1).astype(jnp.bfloat16)
    first_inverse = jnp.stack([jnp.cos(angles).T, -jnp.sin(angles).T], axis=0).astype(jnp.bfloat16)
    block_index = jnp.arange(blocks, dtype=jnp.int32)[:, None]
    lane_index = jnp.arange(128, dtype=jnp.int32)[None, :]
    twist_angles = (block_index * lane_index % freq_len).astype(jnp.float32) * (
        2.0 * math.pi / freq_len
    )
    twist_cosine = jnp.cos(twist_angles)[:, :, None]
    twist_sine = jnp.sin(twist_angles)[:, :, None]
    inner_index = jnp.arange(128, dtype=jnp.int32)
    inner_angles = (inner_index[:, None] * inner_index[None, :] % 128).astype(jnp.float32) * (
        2.0 * math.pi / 128
    )
    cosine = jnp.cos(inner_angles)
    sine_part = jnp.sin(inner_angles)
    second_forward = jnp.stack(
        [jnp.stack([cosine, -sine_part], axis=1), jnp.stack([sine_part, cosine], axis=1)], axis=0
    ).astype(jnp.bfloat16)
    second_inverse = jnp.stack(
        [jnp.stack([cosine, sine_part], axis=1), jnp.stack([-sine_part, cosine], axis=1)], axis=0
    ).astype(jnp.bfloat16)
    return (first_forward, first_inverse, twist_cosine, twist_sine, second_forward, second_inverse)


def first_section(signal, matrix):
    grouped = signal.reshape(-1, 128, signal.shape[-1])
    return jnp.einsum("abc,arp->rpbc", grouped, matrix, preferred_element_type=jnp.float32)


def second_section(first, tables):
    twisted = jnp.stack(
        [first[0] * tables[2] + first[1] * tables[3], first[1] * tables[2] - first[0] * tables[3]]
    ).astype(jnp.bfloat16)
    return jnp.einsum("rpbc,rbsq->spqc", twisted, tables[4], preferred_element_type=jnp.float32)


def spectrum(signal, tables):
    return second_section(first_section(signal, tables[0]), tables)


def inverse_prepare(spectrum_half, tables):
    mixture = jnp.einsum(
        "rpqc,rqsb->spbc", spectrum_half, tables[5], preferred_element_type=jnp.float32
    )
    return jnp.stack(
        [
            mixture[0] * tables[2] - mixture[1] * tables[3],
            mixture[1] * tables[2] + mixture[0] * tables[3],
        ]
    ).astype(jnp.bfloat16)


def inverse_rows(twisted, matrix, norm_scale):
    rows = (
        jnp.einsum("rpbc,rpa->abc", twisted, matrix, preferred_element_type=jnp.float32)
        * norm_scale
    )
    return rows.reshape(-1, rows.shape[-1])


def times_spec(left_spec, right_spec):
    return jnp.stack(
        [
            left_spec[0] * right_spec[0] - left_spec[1] * right_spec[1],
            left_spec[0] * right_spec[1] + left_spec[1] * right_spec[0],
        ]
    ).astype(jnp.bfloat16)


def times_conj(left_spec, right_spec):
    return jnp.stack(
        [
            left_spec[0] * right_spec[0] + left_spec[1] * right_spec[1],
            left_spec[1] * right_spec[0] - left_spec[0] * right_spec[1],
        ]
    ).astype(jnp.bfloat16)


def multiply_round(left_side, right_side):
    return (left_side.astype(jnp.float32) * right_side.astype(jnp.float32)).astype(jnp.bfloat16)


def in_steps(gate_input, values, cotangent, filter_taps):
    context_size = lax.axis_size("ctx")
    data_size = lax.axis_size("dp")
    tok_rows = values.shape[1]
    channels = values.shape[2]
    seq_len = tok_rows * context_size
    local_channels = channels // context_size
    blocks = seq_len // 64
    freq_len = 2 * seq_len
    norm_scale = 1.0 / freq_len
    tables = dft_tables(blocks, freq_len)
    filter_half = filter_taps.astype(jnp.bfloat16)
    filter_columns = lax.all_to_all(filter_half, "ctx", split_axis=1, concat_axis=0, tiled=True)
    matrix = tables[0]
    filter_first = first_section(lax.all_gather(filter_columns, "dp", axis=0, tiled=True), matrix)
    filter_spec = second_section(filter_first, tables)
    value_columns = lax.all_to_all(values[0], "ctx", split_axis=1, concat_axis=0, tiled=True)
    value_spec = spectrum(value_columns, tables)
    conv_columns = inverse_rows(
        inverse_prepare(times_spec(value_spec, filter_spec), tables), tables[1], norm_scale
    ).astype(jnp.bfloat16)
    conv_rows = lax.all_to_all(conv_columns, "ctx", split_axis=0, concat_axis=1, tiled=True)
    output = multiply_round(gate_input[0], conv_rows)
    gate_grad = multiply_round(cotangent[0], conv_rows)
    grad_rows = multiply_round(cotangent[0], gate_input[0])
    grad_columns = lax.all_to_all(grad_rows, "ctx", split_axis=1, concat_axis=0, tiled=True)
    grad_spec = spectrum(grad_columns, tables)
    back_columns = inverse_rows(
        inverse_prepare(times_conj(grad_spec, filter_spec), tables), tables[1], norm_scale
    ).astype(jnp.bfloat16)
    values_grad = lax.all_to_all(back_columns, "ctx", split_axis=0, concat_axis=1, tiled=True)
    filter_twisted = inverse_prepare(times_conj(grad_spec, value_spec), tables)
    whole_rows = inverse_rows(filter_twisted, tables[1], norm_scale)
    reordered = whole_rows.reshape(data_size, context_size, tok_rows // data_size, local_channels)
    reordered = reordered.transpose(1, 0, 2, 3).reshape(seq_len, local_channels)
    received_rows = lax.all_to_all(
        reordered.astype(jnp.bfloat16), "ctx", split_axis=0, concat_axis=1, tiled=True
    ).astype(reordered.dtype)
    filter_grad = lax.psum_scatter(
        received_rows.astype(jnp.bfloat16), "dp", scatter_dimension=0, tiled=True
    ).astype(jnp.float32)
    return (output[None], gate_grad[None], values_grad[None], filter_grad)


def on_device(gate_input, values, cotangent, filter_taps):
    rows, channels = values.shape[1:]
    context_size = lax.axis_size("ctx")
    seq_len = rows * context_size
    table_bytes = 2 * 2 * 2 * seq_len * seq_len
    if table_bytes <= TABLE_LIMIT and context_size % 4 == 0 and channels % (WIDTH * context_size) == 0:
        return in_one_kernel(gate_input, values, cotangent, filter_taps)
    return in_steps(gate_input, values, cotangent, filter_taps)


def solution(mesh):
    in_specs = (
        P("dp", "ctx", None),
        P("dp", "ctx", None),
        P("dp", "ctx", None),
        P(("dp", "ctx"), None),
    )
    out_specs = (
        P("dp", "ctx", None),
        P("dp", "ctx", None),
        P("dp", "ctx", None),
        P(("dp", "ctx"), None),
    )
    return jax.shard_map(
        on_device, mesh=mesh, in_specs=in_specs, out_specs=out_specs, check_vma=False
    )
```

```python
import functools
import math

import jax
import jax.numpy as jnp
import numpy as np
from jax import lax
from jax.experimental import pallas as pl
from jax.experimental.pallas import tpu as pltpu
from jax.sharding import PartitionSpec as P

MESH = pl.DeviceIdType.MESH
WIDTH = 256
TABLE_LIMIT = 8 * 2**20
TILE = 512
OUTER_EIGHTHS = 4


def odd_tables(seq_len):
    turns = np.outer(2 * np.arange(seq_len) + 1, np.arange(seq_len)) % (4 * seq_len)
    angles = turns * (2.0 * math.pi / (4 * seq_len))
    forward = np.concatenate([np.cos(angles), -np.sin(angles)], axis=0)
    inverse = forward.T / seq_len
    tiled = forward.reshape(2, seq_len // TILE, TILE, 2, seq_len // 2)
    forward = tiled.transpose(3, 1, 0, 2, 4).reshape(2, 2 * seq_len, seq_len // 2)
    return jnp.asarray(forward, jnp.bfloat16), jnp.asarray(inverse, jnp.bfloat16)


def dot(left, right):
    return jnp.dot(left, right, preferred_element_type=jnp.float32)


def loop(first, last, body):
    def step(index, carry):
        body(index)
        return carry

    lax.fori_loop(first, last, step, 0)


def kernel(
    dims,
    gate_hbm, values_hbm, cot_hbm, taps_hbm, forward_hbm, inverse_hbm,
    result_rows_ref, filter_grad_ref,
    gate, cot, taps, forward, inverse, taps_half, signal_rows,
    near, whole, taps_cols, mixed_near, mixed_far, mixed_taps,
    near_cols, far_cols, partial, partial_in, summed, result_rows, summed_rows,
    load_sem, gather_sem, reduce_sem,
    near_sem, cross_sem, far_sem, taps_sem, taps_cross_sem, back_near_sem, back_far_sem,
    summed_sem, summed_cross_sem,
):
    ctx, dp, rows, seq_len, outer, inner = dims
    side = ctx // 2
    most = max(outer, inner)
    part = seq_len // dp
    own_rows = part // ctx
    half_len = seq_len // 2
    me = lax.axis_index("ctx")
    group = lax.axis_index("dp")
    half = me // side
    place = lax.rem(me, side)
    low = half == 0
    early = group * part < half_len

    def counts(owner):
        first = outer + (owner // side) * (inner - outer)
        second = outer + inner - first
        return first, second, lax.rem(owner, side) // (side // 2)

    def count(owner):
        first, second, late = counts(owner)
        return first + late * (second - first)

    def columns(owner, chunk):
        first, second, late = counts(owner)
        at = lax.rem(owner, side)
        early_at = at - late * (at - side // 2)
        base = early_at * first + (at - early_at) * second
        return pl.ds(pl.multiple_of((base + chunk) * WIDTH, WIDTH), WIDTH)

    def block(index, size):
        return pl.ds(pl.multiple_of(index * size, size), size)

    def remote(src, dst, send_sem, recv_sem, device):
        return pltpu.make_async_remote_copy(
            src_ref=src, dst_ref=dst, send_sem=send_sem, recv_sem=recv_sem,
            device_id=device, device_id_type=MESH,
        )

    def peer_at(offset, crossing):
        where = lax.rem(place + offset + side, side)
        return (1 - half if crossing else half) * side + where

    class Exchange:
        def __init__(self, refs, sems, crossing, inbound):
            self.refs, self.sems, self.crossing, self.inbound = refs, sems, crossing, inbound

        def own(self, chunk):
            source, target = self.refs(chunk, me, me)
            return pltpu.make_async_copy(source, target, self.sems.at[1, chunk, 0])

        def to(self, chunk, offset):
            peer = peer_at(offset, self.crossing)
            source, target = self.refs(chunk, me, peer)
            return remote(source, target, self.sems.at[0, chunk, offset],
                          self.sems.at[1, chunk, offset], {"ctx": peer})

        def back(self, chunk, offset):
            peer = peer_at(-offset, self.crossing)
            source, target = self.refs(chunk, peer, me)
            return remote(source, target, self.sems.at[0, chunk, offset],
                          self.sems.at[1, chunk, offset], {"ctx": peer})

        def each(self, chunk, sending, act):
            def one(offset):
                peer = peer_at(offset if sending else -offset, self.crossing)
                counted = peer if sending == self.inbound else me

                @pl.when(chunk < count(counted))
                def _():
                    act(offset)

            loop(0 if self.crossing else 1, side, one)

        def start(self, chunk):
            self.each(chunk, True, lambda offset: self.to(chunk, offset).start())
            if not self.crossing:
                @pl.when(chunk < count(me))
                def _():
                    self.own(chunk).start()

        def arrive(self, chunk):
            self.each(chunk, False, lambda offset: self.back(chunk, offset).wait_recv())
            if not self.crossing:
                @pl.when(chunk < count(me))
                def _():
                    self.own(chunk).wait()

        def leave(self, chunk):
            self.each(chunk, True, lambda offset: self.to(chunk, offset).wait_send())

    def near_refs(chunk, sender, receiver):
        return (signal_rows.at[0, :, columns(receiver, chunk)],
                near.at[chunk, block(lax.rem(sender, side), rows), :])

    def cross_refs(chunk, sender, receiver):
        return (signal_rows.at[0, :, columns(receiver, chunk)],
                whole.at[chunk, block(sender, rows), :])

    def far_refs(chunk, sender, receiver):
        return (signal_rows.at[1, :, columns(receiver, chunk)],
                whole.at[chunk, block(sender, rows), :])

    def taps_refs(chunk, sender, receiver):
        return (taps_half.at[:, columns(receiver, chunk)],
                taps_cols.at[chunk, block(group * ctx + sender, own_rows), :])

    def back_near_refs(chunk, sender, receiver):
        return (near_cols.at[chunk, block(lax.rem(receiver, side), rows), :],
                result_rows.at[half, :, columns(sender, chunk)])

    def back_far_refs(chunk, sender, receiver):
        return (far_cols.at[chunk, block(lax.rem(receiver, side), rows), :],
                result_rows.at[1 - half, :, columns(sender, chunk)])

    def summed_refs(chunk, sender, receiver):
        return (summed.at[chunk, block(receiver, own_rows), :],
                summed_rows.at[sender // side, :, columns(sender, chunk)])

    near_way = Exchange(near_refs, near_sem, False, True)
    cross_way = Exchange(cross_refs, cross_sem, True, True)
    far_way = Exchange(far_refs, far_sem, False, True)
    taps_way = Exchange(taps_refs, taps_sem, False, True)
    taps_cross_way = Exchange(taps_refs, taps_cross_sem, True, True)
    back_near_way = Exchange(back_near_refs, back_near_sem, False, False)
    back_far_way = Exchange(back_far_refs, back_far_sem, False, False)
    summed_way = Exchange(summed_refs, summed_sem, False, False)
    summed_cross_way = Exchange(summed_refs, summed_cross_sem, True, False)

    loads = [
        pltpu.make_async_copy(src, dst, load_sem.at[at])
        for at, (src, dst) in enumerate(
            [(taps_hbm, taps), (values_hbm, signal_rows.at[half]), (gate_hbm, gate),
             (cot_hbm, cot), (forward_hbm, forward), (inverse_hbm, inverse)]
        )
    ]
    for load in loads:
        load.start()

    barrier = pltpu.get_barrier_semaphore()
    loop(1, ctx, lambda offset: pl.semaphore_signal(
        barrier, inc=1, device_id={"ctx": lax.rem(me + offset, ctx)}, device_id_type=MESH))
    loop(1, dp, lambda offset: pl.semaphore_signal(
        barrier, inc=1, device_id={"dp": lax.rem(group + offset, dp)}, device_id_type=MESH))
    loads[0].wait()
    taps_half[...] = taps[...].astype(jnp.bfloat16)
    pl.semaphore_wait(barrier, ctx + dp - 2)

    def send_taps(chunk):
        taps_cross_way.start(chunk)
        taps_way.start(chunk)

    loop(0, most, send_taps)
    loads[2].wait()
    loads[3].wait()

    def grad_band(index):
        band = block(index, 16)
        product = gate[band, :].astype(jnp.float32) * cot[band, :].astype(jnp.float32)
        signal_rows[1 - half, band, :] = product.astype(jnp.bfloat16)

    loop(0, rows // 16, grad_band)
    loads[1].wait()

    def send_signals(chunk):
        cross_way.start(chunk)
        near_way.start(chunk)
        far_way.start(chunk)

    send_signals(0)
    mine = count(me)

    def gathered(chunk, offset, owner):
        peer = lax.rem(group + offset, dp)
        held = taps_cols.at[chunk, block(owner, part), :]
        return remote(held, held, gather_sem.at[0, chunk, offset], gather_sem.at[1, chunk, offset],
                      {"dp": peer})

    def gather(chunk):
        taps_cross_way.arrive(chunk)
        taps_way.arrive(chunk)
        loop(1, dp, lambda offset: gathered(chunk, offset, group).start())

    loop(0, mine, gather)
    loop(1, most, send_signals)
    loads[4].wait()
    loads[5].wait()
    sign = jnp.where(low, 1.0, -1.0).astype(jnp.float32)
    keep = jnp.where(low, 1.0, 0.0).astype(jnp.float32)

    def reduces(owner):
        return jnp.logical_or(low, owner * part < half_len)

    def reduced(chunk, offset, owner):
        return remote(
            partial.at[chunk, block(owner, part), :], partial_in.at[chunk, offset],
            reduce_sem.at[0, chunk, offset], reduce_sem.at[1, chunk, offset],
            {"dp": lax.rem(group + offset, dp)})

    def reduce_each(chunk, act):
        def one(offset):
            owner = lax.rem(group + offset, dp)

            @pl.when(reduces(owner))
            def _():
                act(reduced(chunk, offset, owner))

        loop(1, dp, one)

    def finish(chunk):
        @pl.when(reduces(group))
        def _():
            loop(1, dp, lambda offset: reduced(chunk, offset, group).wait_recv())
            total = partial[chunk, block(group, part), :].astype(jnp.float32)
            for offset in range(1, dp):
                total = total + partial_in[chunk, offset].astype(jnp.float32)
            summed[chunk] = total.astype(jnp.bfloat16)
            summed_cross_way.start(chunk)
            summed_way.start(chunk)

    def work(chunk):
        cross_way.arrive(chunk)
        near_way.arrive(chunk)
        far_way.arrive(chunk)
        loop(1, dp, lambda offset: gathered(
            chunk, offset, lax.rem(group + dp - offset, dp)).wait_recv())
        first, second = pl.ds(0, half_len), pl.ds(half_len, half_len)

        def frequencies(index):
            upper = block(index, TILE)
            lower = pl.ds(pl.multiple_of(seq_len + index * TILE, TILE), TILE)
            band = block(index, 2 * TILE)

            def parts(both):
                return both[:TILE], both[TILE:]

            taps_real, taps_imag = parts(
                dot(forward[0, band, :], taps_cols[chunk, first, :])
                + dot(forward[1, band, :], taps_cols[chunk, second, :]))
            near_real, near_imag = parts(dot(forward[half, band, :], near[chunk]))
            early_real, early_imag = parts(dot(forward[0, band, :], whole[chunk, first, :]))
            late_real, late_imag = parts(dot(forward[1, band, :], whole[chunk, second, :]))
            taps_imag = taps_imag * sign
            far_real, far_imag = early_real + late_real, early_imag + late_imag
            half_type = jnp.bfloat16
            mixed_near[upper, :] = (near_real * taps_real - near_imag * taps_imag).astype(half_type)
            mixed_near[lower, :] = (near_real * taps_imag + near_imag * taps_real).astype(half_type)
            mixed_far[upper, :] = (far_real * taps_real + far_imag * taps_imag).astype(half_type)
            mixed_far[lower, :] = (far_imag * taps_real - far_real * taps_imag).astype(half_type)
            part_real, part_imag = early_real * keep + late_real, early_imag * keep + late_imag
            mixed_taps[upper, :] = (part_real * near_real + part_imag * near_imag).astype(half_type)
            mixed_taps[lower, :] = (
                (part_imag * near_real - part_real * near_imag) * sign).astype(half_type)

        loop(0, seq_len // TILE, frequencies)

        def inverse_rows(index):
            return inverse[pl.ds(pl.multiple_of(half * half_len + index * TILE, TILE), TILE), :]

        def near_tile(index):
            near_cols[chunk, block(index, TILE), :] = dot(
                inverse_rows(index), mixed_near[...]).astype(jnp.bfloat16)

        def far_tile(index):
            far_cols[chunk, block(index, TILE), :] = dot(
                inverse_rows(index), mixed_far[...]).astype(jnp.bfloat16)

        def taps_tile(index):
            band = block(index, TILE)
            partial[chunk, band, :] = dot(inverse[band, :], mixed_taps[...]).astype(jnp.bfloat16)

        loop(0, half_len // TILE, near_tile)
        back_near_way.start(chunk)
        loop(0, (2 - half) * (half_len // TILE), taps_tile)
        reduce_each(chunk, lambda copy: copy.start())
        loop(0, half_len // TILE, far_tile)
        back_far_way.start(chunk)

        @pl.when(chunk > 0)
        def _():
            finish(chunk - 1)

    loop(0, mine, work)
    finish(mine - 1)

    def results(chunk):
        back_near_way.arrive(chunk)
        back_far_way.arrive(chunk)

    loop(0, most, results)

    result_rows_ref[...] = result_rows[...]

    @pl.when(low)
    def _():
        loop(0, most, summed_way.arrive)

    @pl.when(jnp.logical_not(low))
    def _():
        loop(0, most, summed_cross_way.arrive)

    filter_grad_ref[...] = summed_rows[0].astype(jnp.float32)

    @pl.when(early)
    def _():
        @pl.when(low)
        def _():
            loop(0, most, summed_cross_way.arrive)

        @pl.when(jnp.logical_not(low))
        def _():
            loop(0, most, summed_way.arrive)

        filter_grad_ref[...] += summed_rows[1].astype(jnp.float32)

    def sent(chunk):
        for way in (taps_cross_way, taps_way, cross_way, near_way, far_way,
                    back_near_way, back_far_way):
            way.leave(chunk)

    loop(0, most, sent)

    def sent_sums(chunk):
        loop(1, dp, lambda offset: gathered(chunk, offset, group).wait_send())
        reduce_each(chunk, lambda copy: copy.wait_send())

        @pl.when(reduces(group))
        def _():
            summed_cross_way.leave(chunk)
            summed_way.leave(chunk)

    loop(0, mine, sent_sums)


def gate_kernel(gate, cot, rows, sums, out_ref, gate_grad_ref, values_grad_ref, filter_grad_ref):
    conv = rows[0].astype(jnp.float32)
    out_ref[...] = (gate[...].astype(jnp.float32) * conv).astype(jnp.bfloat16)
    gate_grad_ref[...] = (cot[...].astype(jnp.float32) * conv).astype(jnp.bfloat16)
    values_grad_ref[...] = rows[1]
    filter_grad_ref[...] = sums[...]


def gate_results(gate_input, cotangent, result_rows, sums):
    rows, channels = gate_input.shape
    own_rows = sums.shape[0]
    steps = own_rows // 8
    block = pl.BlockSpec((rows // steps, channels), lambda i: (i, 0))
    pair = pl.BlockSpec((2, rows // steps, channels), lambda i: (0, i, 0))
    few = pl.BlockSpec((8, channels), lambda i: (i, 0))
    shape = jax.ShapeDtypeStruct((rows, channels), jnp.bfloat16)
    return pl.pallas_call(
        gate_kernel,
        grid=(steps,),
        in_specs=[block, block, pair, few],
        out_specs=(block, block, block, few),
        out_shape=(shape, shape, shape, jax.ShapeDtypeStruct(sums.shape, jnp.float32)),
        compiler_params=pltpu.CompilerParams(vmem_limit_bytes=24 * 2**20),
    )(gate_input, cotangent, result_rows, sums)


def in_one_kernel(gate_input, values, cotangent, filter_taps):
    ctx = lax.axis_size("ctx")
    dp = lax.axis_size("dp")
    rows, channels = values.shape[1:]
    seq_len = rows * ctx
    own_rows = filter_taps.shape[0]
    part = seq_len // dp
    pair = channels // WIDTH // (ctx // 4)
    outer = max(1, pair * OUTER_EIGHTHS // 8)
    inner = pair - outer
    most = max(outer, inner)
    forward, inverse = odd_tables(seq_len)
    half, full = jnp.bfloat16, jnp.float32
    whole = pltpu.VMEM((most, seq_len, WIDTH), half)
    halves = pltpu.VMEM((most, seq_len // 2, WIDTH), half)
    mix = pltpu.VMEM((2 * seq_len, WIDTH), half)
    block = pltpu.VMEM((rows, channels), half)
    pair_rows = pltpu.VMEM((2, rows, channels), half)
    sems = pltpu.SemaphoreType.DMA((2, most, ctx // 2))
    groups = pltpu.SemaphoreType.DMA((2, most, dp))
    anywhere = pl.BlockSpec(memory_space=pl.ANY)
    vmem = pl.BlockSpec(memory_space=pltpu.VMEM)
    flops = 12 * seq_len * seq_len * (channels // ctx) * 2
    result_rows, sums = pl.pallas_call(
        functools.partial(kernel, (ctx, dp, rows, seq_len, outer, inner)),
        out_shape=(
            jax.ShapeDtypeStruct((2, rows, channels), half),
            jax.ShapeDtypeStruct((own_rows, channels), full),
        ),
        in_specs=[anywhere] * 6,
        out_specs=(vmem,) * 2,
        scratch_shapes=[
            block, block, pltpu.VMEM((own_rows, channels), full),
            pltpu.VMEM(forward.shape, half), pltpu.VMEM(inverse.shape, half),
            pltpu.VMEM((own_rows, channels), half), pair_rows,
            halves, whole, whole, mix, mix, mix,
            halves, halves, whole, pltpu.VMEM((most, dp, part, WIDTH), half),
            pltpu.VMEM((most, part, WIDTH), half),
            pair_rows, pltpu.VMEM((2, own_rows, channels), half),
            pltpu.SemaphoreType.DMA((6,)), groups, groups,
        ] + [sems] * 9,
        compiler_params=pltpu.CompilerParams(
            collective_id=0, has_side_effects=True, vmem_limit_bytes=58 * 2**20
        ),
        cost_estimate=pl.CostEstimate(
            flops=flops, bytes_accessed=16 * rows * channels, transcendentals=0
        ),
    )(gate_input[0], values[0], cotangent[0], filter_taps, forward, inverse)
    output, gate_grad, values_grad, filter_grad = gate_results(
        gate_input[0], cotangent[0], result_rows, sums
    )
    return output[None], gate_grad[None], values_grad[None], filter_grad


def dft_tables(blocks, freq_len):
    half_blocks = blocks // 2
    row_index = jnp.arange(half_blocks, dtype=jnp.int32)[:, None]
    freq_index = jnp.arange(blocks, dtype=jnp.int32)[None, :]
    angles = (row_index * freq_index % blocks).astype(jnp.float32) * (2.0 * math.pi / blocks)
    first_forward = jnp.stack([jnp.cos(angles), -jnp.sin(angles)], axis=1).astype(jnp.bfloat16)
    first_inverse = jnp.stack([jnp.cos(angles).T, -jnp.sin(angles).T], axis=0).astype(jnp.bfloat16)
    block_index = jnp.arange(blocks, dtype=jnp.int32)[:, None]
    lane_index = jnp.arange(128, dtype=jnp.int32)[None, :]
    twist_angles = (block_index * lane_index % freq_len).astype(jnp.float32) * (
        2.0 * math.pi / freq_len
    )
    twist_cosine = jnp.cos(twist_angles)[:, :, None]
    twist_sine = jnp.sin(twist_angles)[:, :, None]
    inner_index = jnp.arange(128, dtype=jnp.int32)
    inner_angles = (inner_index[:, None] * inner_index[None, :] % 128).astype(jnp.float32) * (
        2.0 * math.pi / 128
    )
    cosine = jnp.cos(inner_angles)
    sine_part = jnp.sin(inner_angles)
    second_forward = jnp.stack(
        [jnp.stack([cosine, -sine_part], axis=1), jnp.stack([sine_part, cosine], axis=1)], axis=0
    ).astype(jnp.bfloat16)
    second_inverse = jnp.stack(
        [jnp.stack([cosine, sine_part], axis=1), jnp.stack([-sine_part, cosine], axis=1)], axis=0
    ).astype(jnp.bfloat16)
    return (first_forward, first_inverse, twist_cosine, twist_sine, second_forward, second_inverse)


def first_section(signal, matrix):
    grouped = signal.reshape(-1, 128, signal.shape[-1])
    return jnp.einsum("abc,arp->rpbc", grouped, matrix, preferred_element_type=jnp.float32)


def second_section(first, tables):
    twisted = jnp.stack(
        [first[0] * tables[2] + first[1] * tables[3], first[1] * tables[2] - first[0] * tables[3]]
    ).astype(jnp.bfloat16)
    return jnp.einsum("rpbc,rbsq->spqc", twisted, tables[4], preferred_element_type=jnp.float32)


def spectrum(signal, tables):
    return second_section(first_section(signal, tables[0]), tables)


def inverse_prepare(spectrum_half, tables):
    mixture = jnp.einsum(
        "rpqc,rqsb->spbc", spectrum_half, tables[5], preferred_element_type=jnp.float32
    )
    return jnp.stack(
        [
            mixture[0] * tables[2] - mixture[1] * tables[3],
            mixture[1] * tables[2] + mixture[0] * tables[3],
        ]
    ).astype(jnp.bfloat16)


def inverse_rows(twisted, matrix, norm_scale):
    rows = (
        jnp.einsum("rpbc,rpa->abc", twisted, matrix, preferred_element_type=jnp.float32)
        * norm_scale
    )
    return rows.reshape(-1, rows.shape[-1])


def times_spec(left_spec, right_spec):
    return jnp.stack(
        [
            left_spec[0] * right_spec[0] - left_spec[1] * right_spec[1],
            left_spec[0] * right_spec[1] + left_spec[1] * right_spec[0],
        ]
    ).astype(jnp.bfloat16)


def times_conj(left_spec, right_spec):
    return jnp.stack(
        [
            left_spec[0] * right_spec[0] + left_spec[1] * right_spec[1],
            left_spec[1] * right_spec[0] - left_spec[0] * right_spec[1],
        ]
    ).astype(jnp.bfloat16)


def multiply_round(left_side, right_side):
    return (left_side.astype(jnp.float32) * right_side.astype(jnp.float32)).astype(jnp.bfloat16)


def in_steps(gate_input, values, cotangent, filter_taps):
    context_size = lax.axis_size("ctx")
    data_size = lax.axis_size("dp")
    tok_rows = values.shape[1]
    channels = values.shape[2]
    seq_len = tok_rows * context_size
    local_channels = channels // context_size
    blocks = seq_len // 64
    freq_len = 2 * seq_len
    norm_scale = 1.0 / freq_len
    tables = dft_tables(blocks, freq_len)
    filter_half = filter_taps.astype(jnp.bfloat16)
    filter_columns = lax.all_to_all(filter_half, "ctx", split_axis=1, concat_axis=0, tiled=True)
    matrix = tables[0]
    filter_first = first_section(lax.all_gather(filter_columns, "dp", axis=0, tiled=True), matrix)
    filter_spec = second_section(filter_first, tables)
    value_columns = lax.all_to_all(values[0], "ctx", split_axis=1, concat_axis=0, tiled=True)
    value_spec = spectrum(value_columns, tables)
    conv_columns = inverse_rows(
        inverse_prepare(times_spec(value_spec, filter_spec), tables), tables[1], norm_scale
    ).astype(jnp.bfloat16)
    conv_rows = lax.all_to_all(conv_columns, "ctx", split_axis=0, concat_axis=1, tiled=True)
    output = multiply_round(gate_input[0], conv_rows)
    gate_grad = multiply_round(cotangent[0], conv_rows)
    grad_rows = multiply_round(cotangent[0], gate_input[0])
    grad_columns = lax.all_to_all(grad_rows, "ctx", split_axis=1, concat_axis=0, tiled=True)
    grad_spec = spectrum(grad_columns, tables)
    back_columns = inverse_rows(
        inverse_prepare(times_conj(grad_spec, filter_spec), tables), tables[1], norm_scale
    ).astype(jnp.bfloat16)
    values_grad = lax.all_to_all(back_columns, "ctx", split_axis=0, concat_axis=1, tiled=True)
    filter_twisted = inverse_prepare(times_conj(grad_spec, value_spec), tables)
    whole_rows = inverse_rows(filter_twisted, tables[1], norm_scale)
    reordered = whole_rows.reshape(data_size, context_size, tok_rows // data_size, local_channels)
    reordered = reordered.transpose(1, 0, 2, 3).reshape(seq_len, local_channels)
    received_rows = lax.all_to_all(
        reordered.astype(jnp.bfloat16), "ctx", split_axis=0, concat_axis=1, tiled=True
    ).astype(reordered.dtype)
    filter_grad = lax.psum_scatter(
        received_rows.astype(jnp.bfloat16), "dp", scatter_dimension=0, tiled=True
    ).astype(jnp.float32)
    return (output[None], gate_grad[None], values_grad[None], filter_grad)


def on_device(gate_input, values, cotangent, filter_taps):
    rows, channels = values.shape[1:]
    context_size = lax.axis_size("ctx")
    seq_len = rows * context_size
    table_bytes = 2 * 2 * 2 * seq_len * seq_len
    if table_bytes <= TABLE_LIMIT and context_size % 4 == 0 and channels % (WIDTH * context_size) == 0:
        return in_one_kernel(gate_input, values, cotangent, filter_taps)
    return in_steps(gate_input, values, cotangent, filter_taps)


def solution(mesh):
    in_specs = (
        P("dp", "ctx", None),
        P("dp", "ctx", None),
        P("dp", "ctx", None),
        P(("dp", "ctx"), None),
    )
    out_specs = (
        P("dp", "ctx", None),
        P("dp", "ctx", None),
        P("dp", "ctx", None),
        P(("dp", "ctx"), None),
    )
    return jax.shard_map(
        on_device, mesh=mesh, in_specs=in_specs, out_specs=out_specs, check_vma=False
    )
```

```python
import functools
import math

import jax
import jax.numpy as jnp
import numpy as np
from jax import lax
from jax.experimental import pallas as pl
from jax.experimental.pallas import tpu as pltpu
from jax.sharding import PartitionSpec as P

MESH = pl.DeviceIdType.MESH
WIDTH = 256
TABLE_LIMIT = 8 * 2**20
TILE = 512
OUTER_EIGHTHS = 4


def odd_tables(seq_len):
    turns = np.outer(2 * np.arange(seq_len) + 1, np.arange(seq_len)) % (4 * seq_len)
    angles = turns * (2.0 * math.pi / (4 * seq_len))
    forward = np.concatenate([np.cos(angles), -np.sin(angles)], axis=0)
    inverse = forward.T / seq_len
    tiled = forward.reshape(2, seq_len // TILE, TILE, 2, seq_len // 2)
    forward = tiled.transpose(3, 1, 0, 2, 4).reshape(2, 2 * seq_len, seq_len // 2)
    return jnp.asarray(forward, jnp.bfloat16), jnp.asarray(inverse, jnp.bfloat16)


def dot(left, right):
    return jnp.dot(left, right, preferred_element_type=jnp.float32)


def loop(first, last, body):
    def step(index, carry):
        body(index)
        return carry

    lax.fori_loop(first, last, step, 0)


def kernel(
    dims,
    gate_hbm, values_hbm, cot_hbm, taps_hbm, forward_hbm, inverse_hbm,
    result_rows_ref, filter_grad_ref,
    gate, cot, taps, forward, inverse, taps_half, signal_rows,
    near, whole, taps_cols, taps_spec, near_spec, mixed_near, mixed_far, mixed_taps,
    near_cols, far_cols, partial, partial_in, summed, result_rows, summed_rows,
    load_sem, gather_sem, reduce_sem,
    near_sem, cross_sem, far_sem, taps_sem, taps_cross_sem, back_near_sem, back_far_sem,
    summed_sem, summed_cross_sem,
):
    ctx, dp, rows, seq_len, outer, inner = dims
    side = ctx // 2
    most = max(outer, inner)
    part = seq_len // dp
    own_rows = part // ctx
    half_len = seq_len // 2
    me = lax.axis_index("ctx")
    group = lax.axis_index("dp")
    half = me // side
    place = lax.rem(me, side)
    low = half == 0
    early = group * part < half_len

    def counts(owner):
        first = outer + (owner // side) * (inner - outer)
        second = outer + inner - first
        return first, second, lax.rem(owner, side) // (side // 2)

    def count(owner):
        first, second, late = counts(owner)
        return first + late * (second - first)

    def columns(owner, chunk):
        first, second, late = counts(owner)
        at = lax.rem(owner, side)
        early_at = at - late * (at - side // 2)
        base = early_at * first + (at - early_at) * second
        return pl.ds(pl.multiple_of((base + chunk) * WIDTH, WIDTH), WIDTH)

    def block(index, size):
        return pl.ds(pl.multiple_of(index * size, size), size)

    def remote(src, dst, send_sem, recv_sem, device):
        return pltpu.make_async_remote_copy(
            src_ref=src, dst_ref=dst, send_sem=send_sem, recv_sem=recv_sem,
            device_id=device, device_id_type=MESH,
        )

    def peer_at(offset, crossing):
        where = lax.rem(place + offset + side, side)
        return (1 - half if crossing else half) * side + where

    class Exchange:
        def __init__(self, refs, sems, crossing, inbound):
            self.refs, self.sems, self.crossing, self.inbound = refs, sems, crossing, inbound

        def own(self, chunk):
            source, target = self.refs(chunk, me, me)
            return pltpu.make_async_copy(source, target, self.sems.at[1, chunk, 0])

        def to(self, chunk, offset):
            peer = peer_at(offset, self.crossing)
            source, target = self.refs(chunk, me, peer)
            return remote(source, target, self.sems.at[0, chunk, offset],
                          self.sems.at[1, chunk, offset], {"ctx": peer})

        def back(self, chunk, offset):
            peer = peer_at(-offset, self.crossing)
            source, target = self.refs(chunk, peer, me)
            return remote(source, target, self.sems.at[0, chunk, offset],
                          self.sems.at[1, chunk, offset], {"ctx": peer})

        def each(self, chunk, sending, act):
            def one(offset):
                peer = peer_at(offset if sending else -offset, self.crossing)
                counted = peer if sending == self.inbound else me

                @pl.when(chunk < count(counted))
                def _():
                    act(offset)

            loop(0 if self.crossing else 1, side, one)

        def start(self, chunk):
            self.each(chunk, True, lambda offset: self.to(chunk, offset).start())
            if not self.crossing:
                @pl.when(chunk < count(me))
                def _():
                    self.own(chunk).start()

        def arrive(self, chunk):
            self.each(chunk, False, lambda offset: self.back(chunk, offset).wait_recv())
            if not self.crossing:
                @pl.when(chunk < count(me))
                def _():
                    self.own(chunk).wait()

        def leave(self, chunk):
            self.each(chunk, True, lambda offset: self.to(chunk, offset).wait_send())

    def near_refs(chunk, sender, receiver):
        return (signal_rows.at[0, :, columns(receiver, chunk)],
                near.at[chunk, block(lax.rem(sender, side), rows), :])

    def cross_refs(chunk, sender, receiver):
        return (signal_rows.at[0, :, columns(receiver, chunk)],
                whole.at[chunk, block(sender, rows), :])

    def far_refs(chunk, sender, receiver):
        return (signal_rows.at[1, :, columns(receiver, chunk)],
                whole.at[chunk, block(sender, rows), :])

    def taps_refs(chunk, sender, receiver):
        return (taps_half.at[:, columns(receiver, chunk)],
                taps_cols.at[chunk, block(group * ctx + sender, own_rows), :])

    def back_near_refs(chunk, sender, receiver):
        return (near_cols.at[chunk, block(lax.rem(receiver, side), rows), :],
                result_rows.at[half, :, columns(sender, chunk)])

    def back_far_refs(chunk, sender, receiver):
        return (far_cols.at[chunk, block(lax.rem(receiver, side), rows), :],
                result_rows.at[1 - half, :, columns(sender, chunk)])

    def summed_refs(chunk, sender, receiver):
        return (summed.at[chunk, block(receiver, own_rows), :],
                summed_rows.at[sender // side, :, columns(sender, chunk)])

    near_way = Exchange(near_refs, near_sem, False, True)
    cross_way = Exchange(cross_refs, cross_sem, True, True)
    far_way = Exchange(far_refs, far_sem, False, True)
    taps_way = Exchange(taps_refs, taps_sem, False, True)
    taps_cross_way = Exchange(taps_refs, taps_cross_sem, True, True)
    back_near_way = Exchange(back_near_refs, back_near_sem, False, False)
    back_far_way = Exchange(back_far_refs, back_far_sem, False, False)
    summed_way = Exchange(summed_refs, summed_sem, False, False)
    summed_cross_way = Exchange(summed_refs, summed_cross_sem, True, False)

    loads = [
        pltpu.make_async_copy(src, dst, load_sem.at[at])
        for at, (src, dst) in enumerate(
            [(taps_hbm, taps), (gate_hbm, gate), (cot_hbm, cot),
             (values_hbm, signal_rows.at[half]), (forward_hbm, forward), (inverse_hbm, inverse)]
        )
    ]
    for load in loads[:4]:
        load.start()

    barrier = pltpu.get_barrier_semaphore()
    loop(1, ctx, lambda offset: pl.semaphore_signal(
        barrier, inc=1, device_id={"ctx": lax.rem(me + offset, ctx)}, device_id_type=MESH))
    loop(1, dp, lambda offset: pl.semaphore_signal(
        barrier, inc=1, device_id={"dp": lax.rem(group + offset, dp)}, device_id_type=MESH))
    loads[0].wait()
    taps_half[...] = taps[...].astype(jnp.bfloat16)
    pl.semaphore_wait(barrier, ctx + dp - 2)

    def send_taps(chunk):
        taps_cross_way.start(chunk)
        taps_way.start(chunk)

    loop(0, most, send_taps)
    loads[1].wait()
    loads[2].wait()

    def grad_band(index):
        band = block(index, 16)
        product = gate[band, :].astype(jnp.float32) * cot[band, :].astype(jnp.float32)
        signal_rows[1 - half, band, :] = product.astype(jnp.bfloat16)

    loop(0, rows // 16, grad_band)
    loads[3].wait()

    def send_signals(chunk):
        near_way.start(chunk)
        cross_way.start(chunk)
        far_way.start(chunk)

    send_signals(0)
    loads[4].start()
    loads[5].start()
    mine = count(me)

    def gathered(chunk, offset, owner):
        peer = lax.rem(group + offset, dp)
        held = taps_cols.at[chunk, block(owner, part), :]
        return remote(held, held, gather_sem.at[0, chunk, offset], gather_sem.at[1, chunk, offset],
                      {"dp": peer})

    def gather(chunk):
        taps_cross_way.arrive(chunk)
        taps_way.arrive(chunk)
        loop(1, dp, lambda offset: gathered(chunk, offset, group).start())

    loop(0, mine, gather)
    loop(1, most, send_signals)
    loads[4].wait()
    loads[5].wait()
    sign = jnp.where(low, 1.0, -1.0).astype(jnp.float32)
    keep = jnp.where(low, 1.0, 0.0).astype(jnp.float32)

    def reduces(owner):
        return jnp.logical_or(low, owner * part < half_len)

    def reduced(chunk, offset, owner):
        return remote(
            partial.at[chunk, block(owner, part), :], partial_in.at[chunk, offset],
            reduce_sem.at[0, chunk, offset], reduce_sem.at[1, chunk, offset],
            {"dp": lax.rem(group + offset, dp)})

    def reduce_each(chunk, act):
        def one(offset):
            owner = lax.rem(group + offset, dp)

            @pl.when(reduces(owner))
            def _():
                act(reduced(chunk, offset, owner))

        loop(1, dp, one)

    def finish(chunk):
        @pl.when(reduces(group))
        def _():
            loop(1, dp, lambda offset: reduced(chunk, offset, group).wait_recv())
            total = partial[chunk, block(group, part), :].astype(jnp.float32)
            for offset in range(1, dp):
                total = total + partial_in[chunk, offset].astype(jnp.float32)
            summed[chunk] = total.astype(jnp.bfloat16)
            summed_cross_way.start(chunk)
            summed_way.start(chunk)

    def work(chunk):
        loop(1, dp, lambda offset: gathered(
            chunk, offset, lax.rem(group + dp - offset, dp)).wait_recv())
        first, second = pl.ds(0, half_len), pl.ds(half_len, half_len)
        half_type = jnp.bfloat16

        def places(index):
            upper = block(index, TILE)
            lower = pl.ds(pl.multiple_of(seq_len + index * TILE, TILE), TILE)
            return upper, lower, block(index, 2 * TILE)

        def parts(both):
            return both[:TILE], both[TILE:]

        def taps_frequencies(index):
            band = places(index)[2]
            taps_spec[band, :] = dot(forward[0, band, :], taps_cols[chunk, first, :]) + dot(
                forward[1, band, :], taps_cols[chunk, second, :])

        loop(0, seq_len // TILE, taps_frequencies)
        near_way.arrive(chunk)

        def near_frequencies(index):
            upper, lower, band = places(index)
            both = dot(forward[half, band, :], near[chunk])
            near_spec[band, :] = both
            near_real, near_imag = parts(both)
            taps_real, taps_imag = parts(taps_spec[band, :])
            taps_imag = taps_imag * sign
            mixed_near[upper, :] = (near_real * taps_real - near_imag * taps_imag).astype(half_type)
            mixed_near[lower, :] = (near_real * taps_imag + near_imag * taps_real).astype(half_type)

        loop(0, seq_len // TILE, near_frequencies)

        def inverse_rows(index):
            return inverse[pl.ds(pl.multiple_of(half * half_len + index * TILE, TILE), TILE), :]

        def near_tile(index):
            near_cols[chunk, block(index, TILE), :] = dot(
                inverse_rows(index), mixed_near[...]).astype(half_type)

        def far_tile(index):
            far_cols[chunk, block(index, TILE), :] = dot(
                inverse_rows(index), mixed_far[...]).astype(half_type)

        def taps_tile(index):
            band = block(index, TILE)
            partial[chunk, band, :] = dot(inverse[band, :], mixed_taps[...]).astype(half_type)

        loop(0, half_len // TILE, near_tile)
        back_near_way.start(chunk)
        cross_way.arrive(chunk)
        far_way.arrive(chunk)

        def far_frequencies(index):
            upper, lower, band = places(index)
            early_real, early_imag = parts(dot(forward[0, band, :], whole[chunk, first, :]))
            late_real, late_imag = parts(dot(forward[1, band, :], whole[chunk, second, :]))
            near_real, near_imag = parts(near_spec[band, :])
            part_real, part_imag = early_real * keep + late_real, early_imag * keep + late_imag
            mixed_taps[upper, :] = (part_real * near_real + part_imag * near_imag).astype(half_type)
            mixed_taps[lower, :] = (
                (part_imag * near_real - part_real * near_imag) * sign).astype(half_type)
            far_real, far_imag = early_real + late_real, early_imag + late_imag
            taps_real, taps_imag = parts(taps_spec[band, :])
            taps_imag = taps_imag * sign
            mixed_far[upper, :] = (far_real * taps_real + far_imag * taps_imag).astype(half_type)
            mixed_far[lower, :] = (far_imag * taps_real - far_real * taps_imag).astype(half_type)

        loop(0, seq_len // TILE, far_frequencies)
        loop(0, (2 - half) * (half_len // TILE), taps_tile)
        reduce_each(chunk, lambda copy: copy.start())

        @pl.when(chunk > 0)
        def _():
            finish(chunk - 1)

        loop(0, half_len // TILE, far_tile)
        back_far_way.start(chunk)

    loop(0, mine, work)
    finish(mine - 1)

    def results(chunk):
        back_near_way.arrive(chunk)
        back_far_way.arrive(chunk)

    loop(0, most, results)

    result_rows_ref[...] = result_rows[...]

    @pl.when(low)
    def _():
        loop(0, most, summed_way.arrive)

    @pl.when(jnp.logical_not(low))
    def _():
        loop(0, most, summed_cross_way.arrive)

    filter_grad_ref[...] = summed_rows[0].astype(jnp.float32)

    @pl.when(early)
    def _():
        @pl.when(low)
        def _():
            loop(0, most, summed_cross_way.arrive)

        @pl.when(jnp.logical_not(low))
        def _():
            loop(0, most, summed_way.arrive)

        filter_grad_ref[...] += summed_rows[1].astype(jnp.float32)

    def sent(chunk):
        for way in (taps_cross_way, taps_way, cross_way, near_way, far_way,
                    back_near_way, back_far_way):
            way.leave(chunk)

    loop(0, most, sent)

    def sent_sums(chunk):
        loop(1, dp, lambda offset: gathered(chunk, offset, group).wait_send())
        reduce_each(chunk, lambda copy: copy.wait_send())

        @pl.when(reduces(group))
        def _():
            summed_cross_way.leave(chunk)
            summed_way.leave(chunk)

    loop(0, mine, sent_sums)


def gate_kernel(gate, cot, rows, sums, out_ref, gate_grad_ref, values_grad_ref, filter_grad_ref):
    conv = rows[0].astype(jnp.float32)
    out_ref[...] = (gate[...].astype(jnp.float32) * conv).astype(jnp.bfloat16)
    gate_grad_ref[...] = (cot[...].astype(jnp.float32) * conv).astype(jnp.bfloat16)
    values_grad_ref[...] = rows[1]
    filter_grad_ref[...] = sums[...]


def gate_results(gate_input, cotangent, result_rows, sums):
    rows, channels = gate_input.shape
    own_rows = sums.shape[0]
    steps = own_rows // 8
    block = pl.BlockSpec((rows // steps, channels), lambda i: (i, 0))
    pair = pl.BlockSpec((2, rows // steps, channels), lambda i: (0, i, 0))
    few = pl.BlockSpec((8, channels), lambda i: (i, 0))
    shape = jax.ShapeDtypeStruct((rows, channels), jnp.bfloat16)
    return pl.pallas_call(
        gate_kernel,
        grid=(steps,),
        in_specs=[block, block, pair, few],
        out_specs=(block, block, block, few),
        out_shape=(shape, shape, shape, jax.ShapeDtypeStruct(sums.shape, jnp.float32)),
        compiler_params=pltpu.CompilerParams(vmem_limit_bytes=60 * 2**20),
    )(gate_input, cotangent, result_rows, sums)


def in_one_kernel(gate_input, values, cotangent, filter_taps):
    ctx = lax.axis_size("ctx")
    dp = lax.axis_size("dp")
    rows, channels = values.shape[1:]
    seq_len = rows * ctx
    own_rows = filter_taps.shape[0]
    part = seq_len // dp
    pair = channels // WIDTH // (ctx // 4)
    outer = max(1, pair * OUTER_EIGHTHS // 8)
    inner = pair - outer
    most = max(outer, inner)
    forward, inverse = odd_tables(seq_len)
    half, full = jnp.bfloat16, jnp.float32
    whole = pltpu.VMEM((most, seq_len, WIDTH), half)
    halves = pltpu.VMEM((most, seq_len // 2, WIDTH), half)
    mix = pltpu.VMEM((2 * seq_len, WIDTH), half)
    spec = pltpu.VMEM((2 * seq_len, WIDTH), full)
    block = pltpu.VMEM((rows, channels), half)
    pair_rows = pltpu.VMEM((2, rows, channels), half)
    sems = pltpu.SemaphoreType.DMA((2, most, ctx // 2))
    groups = pltpu.SemaphoreType.DMA((2, most, dp))
    anywhere = pl.BlockSpec(memory_space=pl.ANY)
    vmem = pl.BlockSpec(memory_space=pltpu.VMEM)
    flops = 12 * seq_len * seq_len * (channels // ctx) * 2
    result_rows, sums = pl.pallas_call(
        functools.partial(kernel, (ctx, dp, rows, seq_len, outer, inner)),
        out_shape=(
            jax.ShapeDtypeStruct((2, rows, channels), half),
            jax.ShapeDtypeStruct((own_rows, channels), full),
        ),
        in_specs=[anywhere] * 6,
        out_specs=(vmem,) * 2,
        scratch_shapes=[
            block, block, pltpu.VMEM((own_rows, channels), full),
            pltpu.VMEM(forward.shape, half), pltpu.VMEM(inverse.shape, half),
            pltpu.VMEM((own_rows, channels), half), pair_rows,
            halves, whole, whole, spec, spec, mix, mix, mix,
            halves, halves, whole, pltpu.VMEM((most, dp, part, WIDTH), half),
            pltpu.VMEM((most, part, WIDTH), half),
            pair_rows, pltpu.VMEM((2, own_rows, channels), half),
            pltpu.SemaphoreType.DMA((6,)), groups, groups,
        ] + [sems] * 9,
        compiler_params=pltpu.CompilerParams(
            collective_id=0, has_side_effects=True, vmem_limit_bytes=58 * 2**20
        ),
        cost_estimate=pl.CostEstimate(
            flops=flops, bytes_accessed=16 * rows * channels, transcendentals=0
        ),
    )(gate_input[0], values[0], cotangent[0], filter_taps, forward, inverse)
    output, gate_grad, values_grad, filter_grad = gate_results(
        gate_input[0], cotangent[0], result_rows, sums
    )
    return output[None], gate_grad[None], values_grad[None], filter_grad


def dft_tables(blocks, freq_len):
    half_blocks = blocks // 2
    row_index = jnp.arange(half_blocks, dtype=jnp.int32)[:, None]
    freq_index = jnp.arange(blocks, dtype=jnp.int32)[None, :]
    angles = (row_index * freq_index % blocks).astype(jnp.float32) * (2.0 * math.pi / blocks)
    first_forward = jnp.stack([jnp.cos(angles), -jnp.sin(angles)], axis=1).astype(jnp.bfloat16)
    first_inverse = jnp.stack([jnp.cos(angles).T, -jnp.sin(angles).T], axis=0).astype(jnp.bfloat16)
    block_index = jnp.arange(blocks, dtype=jnp.int32)[:, None]
    lane_index = jnp.arange(128, dtype=jnp.int32)[None, :]
    twist_angles = (block_index * lane_index % freq_len).astype(jnp.float32) * (
        2.0 * math.pi / freq_len
    )
    twist_cosine = jnp.cos(twist_angles)[:, :, None]
    twist_sine = jnp.sin(twist_angles)[:, :, None]
    inner_index = jnp.arange(128, dtype=jnp.int32)
    inner_angles = (inner_index[:, None] * inner_index[None, :] % 128).astype(jnp.float32) * (
        2.0 * math.pi / 128
    )
    cosine = jnp.cos(inner_angles)
    sine_part = jnp.sin(inner_angles)
    second_forward = jnp.stack(
        [jnp.stack([cosine, -sine_part], axis=1), jnp.stack([sine_part, cosine], axis=1)], axis=0
    ).astype(jnp.bfloat16)
    second_inverse = jnp.stack(
        [jnp.stack([cosine, sine_part], axis=1), jnp.stack([-sine_part, cosine], axis=1)], axis=0
    ).astype(jnp.bfloat16)
    return (first_forward, first_inverse, twist_cosine, twist_sine, second_forward, second_inverse)


def first_section(signal, matrix):
    grouped = signal.reshape(-1, 128, signal.shape[-1])
    return jnp.einsum("abc,arp->rpbc", grouped, matrix, preferred_element_type=jnp.float32)


def second_section(first, tables):
    twisted = jnp.stack(
        [first[0] * tables[2] + first[1] * tables[3], first[1] * tables[2] - first[0] * tables[3]]
    ).astype(jnp.bfloat16)
    return jnp.einsum("rpbc,rbsq->spqc", twisted, tables[4], preferred_element_type=jnp.float32)


def spectrum(signal, tables):
    return second_section(first_section(signal, tables[0]), tables)


def inverse_prepare(spectrum_half, tables):
    mixture = jnp.einsum(
        "rpqc,rqsb->spbc", spectrum_half, tables[5], preferred_element_type=jnp.float32
    )
    return jnp.stack(
        [
            mixture[0] * tables[2] - mixture[1] * tables[3],
            mixture[1] * tables[2] + mixture[0] * tables[3],
        ]
    ).astype(jnp.bfloat16)


def inverse_rows(twisted, matrix, norm_scale):
    rows = (
        jnp.einsum("rpbc,rpa->abc", twisted, matrix, preferred_element_type=jnp.float32)
        * norm_scale
    )
    return rows.reshape(-1, rows.shape[-1])


def times_spec(left_spec, right_spec):
    return jnp.stack(
        [
            left_spec[0] * right_spec[0] - left_spec[1] * right_spec[1],
            left_spec[0] * right_spec[1] + left_spec[1] * right_spec[0],
        ]
    ).astype(jnp.bfloat16)


def times_conj(left_spec, right_spec):
    return jnp.stack(
        [
            left_spec[0] * right_spec[0] + left_spec[1] * right_spec[1],
            left_spec[1] * right_spec[0] - left_spec[0] * right_spec[1],
        ]
    ).astype(jnp.bfloat16)


def multiply_round(left_side, right_side):
    return (left_side.astype(jnp.float32) * right_side.astype(jnp.float32)).astype(jnp.bfloat16)


def in_steps(gate_input, values, cotangent, filter_taps):
    context_size = lax.axis_size("ctx")
    data_size = lax.axis_size("dp")
    tok_rows = values.shape[1]
    channels = values.shape[2]
    seq_len = tok_rows * context_size
    local_channels = channels // context_size
    blocks = seq_len // 64
    freq_len = 2 * seq_len
    norm_scale = 1.0 / freq_len
    tables = dft_tables(blocks, freq_len)
    filter_half = filter_taps.astype(jnp.bfloat16)
    filter_columns = lax.all_to_all(filter_half, "ctx", split_axis=1, concat_axis=0, tiled=True)
    matrix = tables[0]
    filter_first = first_section(lax.all_gather(filter_columns, "dp", axis=0, tiled=True), matrix)
    filter_spec = second_section(filter_first, tables)
    value_columns = lax.all_to_all(values[0], "ctx", split_axis=1, concat_axis=0, tiled=True)
    value_spec = spectrum(value_columns, tables)
    conv_columns = inverse_rows(
        inverse_prepare(times_spec(value_spec, filter_spec), tables), tables[1], norm_scale
    ).astype(jnp.bfloat16)
    conv_rows = lax.all_to_all(conv_columns, "ctx", split_axis=0, concat_axis=1, tiled=True)
    output = multiply_round(gate_input[0], conv_rows)
    gate_grad = multiply_round(cotangent[0], conv_rows)
    grad_rows = multiply_round(cotangent[0], gate_input[0])
    grad_columns = lax.all_to_all(grad_rows, "ctx", split_axis=1, concat_axis=0, tiled=True)
    grad_spec = spectrum(grad_columns, tables)
    back_columns = inverse_rows(
        inverse_prepare(times_conj(grad_spec, filter_spec), tables), tables[1], norm_scale
    ).astype(jnp.bfloat16)
    values_grad = lax.all_to_all(back_columns, "ctx", split_axis=0, concat_axis=1, tiled=True)
    filter_twisted = inverse_prepare(times_conj(grad_spec, value_spec), tables)
    whole_rows = inverse_rows(filter_twisted, tables[1], norm_scale)
    reordered = whole_rows.reshape(data_size, context_size, tok_rows // data_size, local_channels)
    reordered = reordered.transpose(1, 0, 2, 3).reshape(seq_len, local_channels)
    received_rows = lax.all_to_all(
        reordered.astype(jnp.bfloat16), "ctx", split_axis=0, concat_axis=1, tiled=True
    ).astype(reordered.dtype)
    filter_grad = lax.psum_scatter(
        received_rows.astype(jnp.bfloat16), "dp", scatter_dimension=0, tiled=True
    ).astype(jnp.float32)
    return (output[None], gate_grad[None], values_grad[None], filter_grad)


def on_device(gate_input, values, cotangent, filter_taps):
    rows, channels = values.shape[1:]
    context_size = lax.axis_size("ctx")
    seq_len = rows * context_size
    table_bytes = 2 * 2 * 2 * seq_len * seq_len
    if table_bytes <= TABLE_LIMIT and context_size % 4 == 0 and channels % (WIDTH * context_size) == 0:
        return in_one_kernel(gate_input, values, cotangent, filter_taps)
    return in_steps(gate_input, values, cotangent, filter_taps)


def solution(mesh):
    in_specs = (
        P("dp", "ctx", None),
        P("dp", "ctx", None),
        P("dp", "ctx", None),
        P(("dp", "ctx"), None),
    )
    out_specs = (
        P("dp", "ctx", None),
        P("dp", "ctx", None),
        P("dp", "ctx", None),
        P(("dp", "ctx"), None),
    )
    return jax.shard_map(
        on_device, mesh=mesh, in_specs=in_specs, out_specs=out_specs, check_vma=False
    )
```

```python
import functools
import math

import jax
import jax.numpy as jnp
import numpy as np
from jax import lax
from jax.experimental import pallas as pl
from jax.experimental.pallas import tpu as pltpu
from jax.sharding import PartitionSpec as P

MESH = pl.DeviceIdType.MESH
WIDTH = 256
TABLE_LIMIT = 8 * 2**20
OUTER_EIGHTHS = 4


def odd_tables(seq_len):
    half_len = seq_len // 2
    turns = np.outer(2 * np.arange(half_len) + 1, np.arange(half_len)) % (2 * seq_len)
    angles = turns * (math.pi / seq_len)
    forward = np.concatenate([np.cos(angles), -np.sin(angles)], axis=0)
    inverse = forward.T / seq_len
    forward = np.stack([forward[:, : half_len // 2], forward[:, half_len // 2 :]])
    steps = (2 * np.arange(half_len) + 1)[:, None] * (math.pi / (2 * seq_len)) * np.ones((1, WIDTH))
    twist = np.stack([np.cos(steps), np.sin(steps)])
    return (jnp.asarray(forward, jnp.bfloat16), jnp.asarray(inverse, jnp.bfloat16),
            jnp.asarray(twist, jnp.float32))


def parting(rows):
    row = lax.broadcasted_iota(jnp.int32, (rows, rows), 0)
    column = lax.broadcasted_iota(jnp.int32, (rows, rows), 1)
    source = jnp.where(row < rows // 2, 2 * row, 2 * row + 1 - rows)
    return jnp.where(column == source, 1.0, 0.0).astype(jnp.bfloat16)


def joining(rows):
    row = lax.broadcasted_iota(jnp.int32, (rows, rows), 0)
    column = lax.broadcasted_iota(jnp.int32, (rows, rows), 1)
    source = jnp.where(column < rows // 2, 2 * column, 2 * column + 1 - rows)
    return jnp.where(row == source, 1.0, 0.0).astype(jnp.bfloat16)


def dot(left, right):
    return jnp.dot(left, right, preferred_element_type=jnp.float32)


def loop(first, last, body):
    def step(index, carry):
        body(index)
        return carry

    lax.fori_loop(first, last, step, 0)


def kernel(
    dims,
    gate_hbm, values_hbm, cot_hbm, taps_hbm, forward_hbm, inverse_hbm, twist_hbm,
    result_rows_ref, sums_ref,
    gate, cot, values, taps, forward, inverse, twist, taps_half, signal_rows,
    near, whole, taps_cols, taps_spec, near_spec, mixed_near, mixed_far, mixed_taps,
    near_cols, far_cols, partial, partial_in, summed, result_rows, summed_rows,
    load_sem, gather_sem, reduce_sem,
    near_sem, cross_sem, far_sem, taps_sem, taps_cross_sem, back_near_sem, back_far_sem,
    summed_sem, summed_cross_sem,
):
    ctx, dp, rows, seq_len, outer, inner = dims
    side = ctx // 2
    most = max(outer, inner)
    part = seq_len // dp
    own_rows = part // ctx
    half_len = seq_len // 2
    me = lax.axis_index("ctx")
    group = lax.axis_index("dp")
    half = me // side
    place = lax.rem(me, side)
    low = half == 0
    early = group * part < half_len

    def counts(owner):
        first = outer + (owner // side) * (inner - outer)
        second = outer + inner - first
        return first, second, lax.rem(owner, side) // (side // 2)

    def count(owner):
        first, second, late = counts(owner)
        return first + late * (second - first)

    def columns(owner, chunk):
        first, second, late = counts(owner)
        at = lax.rem(owner, side)
        early_at = at - late * (at - side // 2)
        base = early_at * first + (at - early_at) * second
        return pl.ds(pl.multiple_of((base + chunk) * WIDTH, WIDTH), WIDTH)

    def block(index, size):
        return pl.ds(pl.multiple_of(index * size, size), size)

    def remote(src, dst, send_sem, recv_sem, device):
        return pltpu.make_async_remote_copy(
            src_ref=src, dst_ref=dst, send_sem=send_sem, recv_sem=recv_sem,
            device_id=device, device_id_type=MESH,
        )

    def peer_at(offset, crossing):
        where = lax.rem(place + offset + side, side)
        return (1 - half if crossing else half) * side + where

    class Exchange:
        def __init__(self, refs, sems, crossing, inbound):
            self.refs, self.sems, self.crossing, self.inbound = refs, sems, crossing, inbound

        def own(self, chunk):
            source, target = self.refs(chunk, me, me)
            return pltpu.make_async_copy(source, target, self.sems.at[1, chunk, 0])

        def to(self, chunk, offset):
            peer = peer_at(offset, self.crossing)
            source, target = self.refs(chunk, me, peer)
            return remote(source, target, self.sems.at[0, chunk, offset],
                          self.sems.at[1, chunk, offset], {"ctx": peer})

        def back(self, chunk, offset):
            peer = peer_at(-offset, self.crossing)
            source, target = self.refs(chunk, peer, me)
            return remote(source, target, self.sems.at[0, chunk, offset],
                          self.sems.at[1, chunk, offset], {"ctx": peer})

        def each(self, chunk, sending, act):
            def one(offset):
                peer = peer_at(offset if sending else -offset, self.crossing)
                counted = peer if sending == self.inbound else me

                @pl.when(chunk < count(counted))
                def _():
                    act(offset)

            loop(0 if self.crossing else 1, side, one)

        def start(self, chunk):
            self.each(chunk, True, lambda offset: self.to(chunk, offset).start())
            if not self.crossing:
                @pl.when(chunk < count(me))
                def _():
                    self.own(chunk).start()

        def arrive(self, chunk):
            self.each(chunk, False, lambda offset: self.back(chunk, offset).wait_recv())
            if not self.crossing:
                @pl.when(chunk < count(me))
                def _():
                    self.own(chunk).wait()

        def leave(self, chunk):
            self.each(chunk, True, lambda offset: self.to(chunk, offset).wait_send())

    def near_refs(chunk, sender, receiver):
        return (signal_rows.at[0, :, :, columns(receiver, chunk)],
                near.at[chunk, :, block(lax.rem(sender, side), rows // 2), :])

    def cross_refs(chunk, sender, receiver):
        return (signal_rows.at[0, :, :, columns(receiver, chunk)],
                whole.at[chunk, :, block(sender, rows // 2), :])

    def far_refs(chunk, sender, receiver):
        return (signal_rows.at[1, :, :, columns(receiver, chunk)],
                whole.at[chunk, :, block(sender, rows // 2), :])

    def taps_refs(chunk, sender, receiver):
        return (taps_half.at[:, :, columns(receiver, chunk)],
                taps_cols.at[chunk, :, block(group * ctx + sender, own_rows // 2), :])

    def back_near_refs(chunk, sender, receiver):
        return (near_cols.at[chunk, :, block(lax.rem(receiver, side), rows // 2), :],
                result_rows.at[half, :, :, columns(sender, chunk)])

    def back_far_refs(chunk, sender, receiver):
        return (far_cols.at[chunk, :, block(lax.rem(receiver, side), rows // 2), :],
                result_rows.at[1 - half, :, :, columns(sender, chunk)])

    def summed_refs(chunk, sender, receiver):
        return (summed.at[chunk, :, block(receiver, own_rows // 2), :],
                summed_rows.at[sender // side, :, :, columns(sender, chunk)])

    near_way = Exchange(near_refs, near_sem, False, True)
    cross_way = Exchange(cross_refs, cross_sem, True, True)
    far_way = Exchange(far_refs, far_sem, False, True)
    taps_way = Exchange(taps_refs, taps_sem, False, True)
    taps_cross_way = Exchange(taps_refs, taps_cross_sem, True, True)
    back_near_way = Exchange(back_near_refs, back_near_sem, False, False)
    back_far_way = Exchange(back_far_refs, back_far_sem, False, False)
    summed_way = Exchange(summed_refs, summed_sem, False, False)
    summed_cross_way = Exchange(summed_refs, summed_cross_sem, True, False)

    loads = [
        pltpu.make_async_copy(src, dst, load_sem.at[at])
        for at, (src, dst) in enumerate(
            [(taps_hbm, taps), (gate_hbm, gate), (cot_hbm, cot),
             (values_hbm, values), (forward_hbm, forward), (inverse_hbm, inverse),
             (twist_hbm, twist)]
        )
    ]
    for load in loads[:4]:
        load.start()

    barrier = pltpu.get_barrier_semaphore()
    loop(1, ctx, lambda offset: pl.semaphore_signal(
        barrier, inc=1, device_id={"ctx": lax.rem(me + offset, ctx)}, device_id_type=MESH))
    loop(1, dp, lambda offset: pl.semaphore_signal(
        barrier, inc=1, device_id={"dp": lax.rem(group + offset, dp)}, device_id_type=MESH))
    loads[0].wait()

    def apart(target, source, order):
        both = dot(order, source).astype(jnp.bfloat16)
        target[0], target[1] = both[: both.shape[0] // 2], both[both.shape[0] // 2 :]

    channels = gate.shape[1]
    span = 512

    def taps_band(index):
        band = block(index, span)
        apart(taps_half.at[:, :, band], taps[:, band].astype(jnp.bfloat16), parting(own_rows))

    loop(0, channels // span, taps_band)
    pl.semaphore_wait(barrier, ctx + dp - 2)

    def send_taps(chunk):
        taps_cross_way.start(chunk)
        taps_way.start(chunk)

    loop(0, most, send_taps)
    loads[1].wait()
    loads[2].wait()

    def grad_band(index):
        band = block(index, span)
        product = gate[:, band].astype(jnp.float32) * cot[:, band].astype(jnp.float32)
        apart(signal_rows.at[1 - half, :, :, band], product.astype(jnp.bfloat16), parting(rows))

    loop(0, channels // span, grad_band)
    loads[3].wait()

    def value_band(index):
        band = block(index, span)
        apart(signal_rows.at[half, :, :, band], values[:, band], parting(rows))

    loop(0, channels // span, value_band)

    def send_signals(chunk):
        near_way.start(chunk)
        cross_way.start(chunk)
        far_way.start(chunk)

    send_signals(0)
    loads[4].start()
    loads[5].start()
    loads[6].start()
    mine = count(me)

    def gathered(chunk, offset, owner):
        peer = lax.rem(group + offset, dp)
        held = taps_cols.at[chunk, :, block(owner, part // 2), :]
        return remote(held, held, gather_sem.at[0, chunk, offset], gather_sem.at[1, chunk, offset],
                      {"dp": peer})

    def gather(chunk):
        taps_cross_way.arrive(chunk)
        taps_way.arrive(chunk)
        loop(1, dp, lambda offset: gathered(chunk, offset, group).start())

    loop(0, mine, gather)
    loop(1, most, send_signals)
    loads[4].wait()
    loads[5].wait()
    loads[6].wait()
    sign = jnp.where(low, 1.0, -1.0).astype(jnp.float32)
    keep = jnp.where(low, 1.0, 0.0).astype(jnp.float32)

    def reduces(owner):
        return jnp.logical_or(low, owner * part < half_len)

    def reduced(chunk, offset, owner):
        return remote(
            partial.at[chunk, :, block(owner, part // 2), :], partial_in.at[chunk, offset],
            reduce_sem.at[0, chunk, offset], reduce_sem.at[1, chunk, offset],
            {"dp": lax.rem(group + offset, dp)})

    def reduce_each(chunk, act):
        def one(offset):
            owner = lax.rem(group + offset, dp)

            @pl.when(reduces(owner))
            def _():
                act(reduced(chunk, offset, owner))

        loop(1, dp, one)

    def finish(chunk):
        @pl.when(reduces(group))
        def _():
            loop(1, dp, lambda offset: reduced(chunk, offset, group).wait_recv())
            total = partial[chunk, :, block(group, part // 2), :].astype(jnp.float32)
            for offset in range(1, dp):
                total = total + partial_in[chunk, offset].astype(jnp.float32)
            summed[chunk] = total.astype(jnp.bfloat16)
            summed_cross_way.start(chunk)
            summed_way.start(chunk)

    def work(chunk):
        loop(1, dp, lambda offset: gathered(
            chunk, offset, lax.rem(group + dp - offset, dp)).wait_recv())
        quarter = half_len // 2
        first, second = pl.ds(0, quarter), pl.ds(quarter, quarter)

        def parts(both):
            return both[:half_len], both[half_len:]

        def turned(odd):
            real, imag = parts(odd)
            return twist[0] * real + twist[1] * imag, twist[0] * imag - twist[1] * real

        def butterfly(even, odd):
            real, imag = parts(even)
            turned_real, turned_imag = turned(odd)
            return (real + turned_real, imag + turned_imag, real - turned_real, imag - turned_imag)

        def unmix(target, real, imag, mirror_real, mirror_imag):
            target[0, :half_len, :] = (real + mirror_real).astype(jnp.bfloat16)
            target[0, half_len:, :] = (imag + mirror_imag).astype(jnp.bfloat16)
            real, imag = real - mirror_real, imag - mirror_imag
            target[1, :half_len, :] = (twist[0] * real - twist[1] * imag).astype(jnp.bfloat16)
            target[1, half_len:, :] = (twist[0] * imag + twist[1] * real).astype(jnp.bfloat16)

        def times(left, right):
            return left[0] * right[0] - left[1] * right[1], left[0] * right[1] + left[1] * right[0]

        def times_conjugate(left, right):
            return left[0] * right[0] + left[1] * right[1], left[1] * right[0] - left[0] * right[1]

        def of_taps(parity):
            return dot(forward[0], taps_cols[chunk, parity, first, :]) + dot(
                forward[1], taps_cols[chunk, parity, second, :])

        spectrum = butterfly(of_taps(0), of_taps(1))
        taps_spec[0], taps_spec[1] = spectrum[0], spectrum[1] * sign
        taps_spec[2], taps_spec[3] = spectrum[2], spectrum[3] * sign
        near_way.arrive(chunk)
        spectrum = butterfly(dot(forward[half], near[chunk, 0]), dot(forward[half], near[chunk, 1]))
        for at in range(4):
            near_spec[at] = spectrum[at]
        unmix(mixed_near,
              *times(spectrum[:2], (taps_spec[0], taps_spec[1])),
              *times(spectrum[2:], (taps_spec[2], taps_spec[3])))
        own_half = pl.ds(pl.multiple_of(half * quarter, quarter), quarter)
        for parity in range(2):
            near_cols[chunk, parity] = dot(
                inverse[own_half, :], mixed_near[parity]).astype(jnp.bfloat16)
        back_near_way.start(chunk)
        cross_way.arrive(chunk)
        far_way.arrive(chunk)
        early_spec = butterfly(*(dot(forward[0], whole[chunk, parity, first, :]) for parity in (0, 1)))
        late_spec = butterfly(*(dot(forward[1], whole[chunk, parity, second, :]) for parity in (0, 1)))
        wide = [one + two for one, two in zip(early_spec, late_spec)]
        some = [one * keep + two for one, two in zip(early_spec, late_spec)]
        unmix(mixed_far,
              *times_conjugate(wide[:2], (taps_spec[0], taps_spec[1])),
              *times_conjugate(wide[2:], (taps_spec[2], taps_spec[3])))
        real, imag = times_conjugate(some[:2], (near_spec[0], near_spec[1]))
        mirror_real, mirror_imag = times_conjugate(some[2:], (near_spec[2], near_spec[3]))
        unmix(mixed_taps, real, imag * sign, mirror_real, mirror_imag * sign)

        def taps_tile(index):
            band = block(index, quarter)
            for parity in range(2):
                partial[chunk, parity, band, :] = dot(
                    inverse[band, :], mixed_taps[parity]).astype(jnp.bfloat16)

        loop(0, 2 - half, taps_tile)
        reduce_each(chunk, lambda copy: copy.start())

        @pl.when(chunk > 0)
        def _():
            finish(chunk - 1)

        for parity in range(2):
            far_cols[chunk, parity] = dot(
                inverse[own_half, :], mixed_far[parity]).astype(jnp.bfloat16)
        back_far_way.start(chunk)

    loop(0, mine, work)
    finish(mine - 1)

    def results(chunk):
        back_near_way.arrive(chunk)
        back_far_way.arrive(chunk)

    loop(0, most, results)

    result_rows_ref[...] = result_rows[...]

    @pl.when(low)
    def _():
        loop(0, most, summed_way.arrive)

    @pl.when(jnp.logical_not(low))
    def _():
        loop(0, most, summed_cross_way.arrive)

    sums_ref[0] = summed_rows[0]
    sums_ref[1] = jnp.zeros_like(summed_rows[1])

    @pl.when(early)
    def _():
        @pl.when(low)
        def _():
            loop(0, most, summed_cross_way.arrive)

        @pl.when(jnp.logical_not(low))
        def _():
            loop(0, most, summed_way.arrive)

        sums_ref[1] = summed_rows[1]

    def sent(chunk):
        for way in (taps_cross_way, taps_way, cross_way, near_way, far_way,
                    back_near_way, back_far_way):
            way.leave(chunk)

    loop(0, most, sent)

    def sent_sums(chunk):
        loop(1, dp, lambda offset: gathered(chunk, offset, group).wait_send())
        reduce_each(chunk, lambda copy: copy.wait_send())

        @pl.when(reduces(group))
        def _():
            summed_cross_way.leave(chunk)
            summed_way.leave(chunk)

    loop(0, mine, sent_sums)


def gate_kernel(gate, cot, rows, sums, out_ref, gate_grad_ref, values_grad_ref, filter_grad_ref):
    def whole(parted):
        return dot(joining(2 * parted.shape[1]), parted.reshape(-1, parted.shape[2]))

    conv = whole(rows[0])
    out_ref[...] = (gate[...].astype(jnp.float32) * conv).astype(jnp.bfloat16)
    gate_grad_ref[...] = (cot[...].astype(jnp.float32) * conv).astype(jnp.bfloat16)
    values_grad_ref[...] = whole(rows[1]).astype(jnp.bfloat16)
    filter_grad_ref[...] = whole(sums[0]) + whole(sums[1])


def gate_results(gate_input, cotangent, result_rows, sums):
    rows, channels = gate_input.shape
    own_rows = 2 * sums.shape[2]
    width = 512
    block = pl.BlockSpec((rows, width), lambda i: (0, i))
    pair = pl.BlockSpec((2, 2, rows // 2, width), lambda i: (0, 0, 0, i))
    few = pl.BlockSpec((2, 2, own_rows // 2, width), lambda i: (0, 0, 0, i))
    shape = jax.ShapeDtypeStruct((rows, channels), jnp.bfloat16)
    return pl.pallas_call(
        gate_kernel,
        grid=(channels // width,),
        in_specs=[block, block, pair, few],
        out_specs=(block, block, block, pl.BlockSpec((own_rows, width), lambda i: (0, i))),
        out_shape=(shape, shape, shape, jax.ShapeDtypeStruct((own_rows, channels), jnp.float32)),
        compiler_params=pltpu.CompilerParams(vmem_limit_bytes=60 * 2**20),
    )(gate_input, cotangent, result_rows, sums)


def in_one_kernel(gate_input, values, cotangent, filter_taps):
    ctx = lax.axis_size("ctx")
    dp = lax.axis_size("dp")
    rows, channels = values.shape[1:]
    seq_len = rows * ctx
    own_rows = filter_taps.shape[0]
    part = seq_len // dp
    pair = channels // WIDTH // (ctx // 4)
    outer = max(1, pair * OUTER_EIGHTHS // 8)
    inner = pair - outer
    most = max(outer, inner)
    forward, inverse, twist = odd_tables(seq_len)
    half, full = jnp.bfloat16, jnp.float32
    whole = pltpu.VMEM((most, 2, seq_len // 2, WIDTH), half)
    halves = pltpu.VMEM((most, 2, seq_len // 4, WIDTH), half)
    mix = pltpu.VMEM((2, seq_len, WIDTH), half)
    spec = pltpu.VMEM((4, seq_len // 2, WIDTH), full)
    block = pltpu.VMEM((rows, channels), half)
    pair_rows = pltpu.VMEM((2, 2, rows // 2, channels), half)
    sems = pltpu.SemaphoreType.DMA((2, most, ctx // 2))
    groups = pltpu.SemaphoreType.DMA((2, most, dp))
    anywhere = pl.BlockSpec(memory_space=pl.ANY)
    vmem = pl.BlockSpec(memory_space=pltpu.VMEM)
    flops = 12 * seq_len * seq_len * (channels // ctx) * 2
    result_rows, sums = pl.pallas_call(
        functools.partial(kernel, (ctx, dp, rows, seq_len, outer, inner)),
        out_shape=(
            jax.ShapeDtypeStruct((2, 2, rows // 2, channels), half),
            jax.ShapeDtypeStruct((2, 2, own_rows // 2, channels), half),
        ),
        in_specs=[anywhere] * 7,
        out_specs=(vmem,) * 2,
        scratch_shapes=[
            block, block, block, pltpu.VMEM((own_rows, channels), full),
            pltpu.VMEM(forward.shape, half), pltpu.VMEM(inverse.shape, half),
            pltpu.VMEM(twist.shape, full), pltpu.VMEM((2, own_rows // 2, channels), half), pair_rows,
            halves, whole, whole, spec, spec, mix, mix, mix,
            halves, halves, whole, pltpu.VMEM((most, dp, 2, part // 2, WIDTH), half),
            pltpu.VMEM((most, 2, part // 2, WIDTH), half),
            pair_rows, pltpu.VMEM((2, 2, own_rows // 2, channels), half),
            pltpu.SemaphoreType.DMA((7,)), groups, groups,
        ] + [sems] * 9,
        compiler_params=pltpu.CompilerParams(
            collective_id=0, has_side_effects=True, vmem_limit_bytes=58 * 2**20
        ),
        cost_estimate=pl.CostEstimate(
            flops=flops, bytes_accessed=16 * rows * channels, transcendentals=0
        ),
    )(gate_input[0], values[0], cotangent[0], filter_taps, forward, inverse, twist)
    output, gate_grad, values_grad, filter_grad = gate_results(
        gate_input[0], cotangent[0], result_rows, sums
    )
    return output[None], gate_grad[None], values_grad[None], filter_grad


def dft_tables(blocks, freq_len):
    half_blocks = blocks // 2
    row_index = jnp.arange(half_blocks, dtype=jnp.int32)[:, None]
    freq_index = jnp.arange(blocks, dtype=jnp.int32)[None, :]
    angles = (row_index * freq_index % blocks).astype(jnp.float32) * (2.0 * math.pi / blocks)
    first_forward = jnp.stack([jnp.cos(angles), -jnp.sin(angles)], axis=1).astype(jnp.bfloat16)
    first_inverse = jnp.stack([jnp.cos(angles).T, -jnp.sin(angles).T], axis=0).astype(jnp.bfloat16)
    block_index = jnp.arange(blocks, dtype=jnp.int32)[:, None]
    lane_index = jnp.arange(128, dtype=jnp.int32)[None, :]
    twist_angles = (block_index * lane_index % freq_len).astype(jnp.float32) * (
        2.0 * math.pi / freq_len
    )
    twist_cosine = jnp.cos(twist_angles)[:, :, None]
    twist_sine = jnp.sin(twist_angles)[:, :, None]
    inner_index = jnp.arange(128, dtype=jnp.int32)
    inner_angles = (inner_index[:, None] * inner_index[None, :] % 128).astype(jnp.float32) * (
        2.0 * math.pi / 128
    )
    cosine = jnp.cos(inner_angles)
    sine_part = jnp.sin(inner_angles)
    second_forward = jnp.stack(
        [jnp.stack([cosine, -sine_part], axis=1), jnp.stack([sine_part, cosine], axis=1)], axis=0
    ).astype(jnp.bfloat16)
    second_inverse = jnp.stack(
        [jnp.stack([cosine, sine_part], axis=1), jnp.stack([-sine_part, cosine], axis=1)], axis=0
    ).astype(jnp.bfloat16)
    return (first_forward, first_inverse, twist_cosine, twist_sine, second_forward, second_inverse)


def first_section(signal, matrix):
    grouped = signal.reshape(-1, 128, signal.shape[-1])
    return jnp.einsum("abc,arp->rpbc", grouped, matrix, preferred_element_type=jnp.float32)


def second_section(first, tables):
    twisted = jnp.stack(
        [first[0] * tables[2] + first[1] * tables[3], first[1] * tables[2] - first[0] * tables[3]]
    ).astype(jnp.bfloat16)
    return jnp.einsum("rpbc,rbsq->spqc", twisted, tables[4], preferred_element_type=jnp.float32)


def spectrum(signal, tables):
    return second_section(first_section(signal, tables[0]), tables)


def inverse_prepare(spectrum_half, tables):
    mixture = jnp.einsum(
        "rpqc,rqsb->spbc", spectrum_half, tables[5], preferred_element_type=jnp.float32
    )
    return jnp.stack(
        [
            mixture[0] * tables[2] - mixture[1] * tables[3],
            mixture[1] * tables[2] + mixture[0] * tables[3],
        ]
    ).astype(jnp.bfloat16)


def inverse_rows(twisted, matrix, norm_scale):
    rows = (
        jnp.einsum("rpbc,rpa->abc", twisted, matrix, preferred_element_type=jnp.float32)
        * norm_scale
    )
    return rows.reshape(-1, rows.shape[-1])


def times_spec(left_spec, right_spec):
    return jnp.stack(
        [
            left_spec[0] * right_spec[0] - left_spec[1] * right_spec[1],
            left_spec[0] * right_spec[1] + left_spec[1] * right_spec[0],
        ]
    ).astype(jnp.bfloat16)


def times_conj(left_spec, right_spec):
    return jnp.stack(
        [
            left_spec[0] * right_spec[0] + left_spec[1] * right_spec[1],
            left_spec[1] * right_spec[0] - left_spec[0] * right_spec[1],
        ]
    ).astype(jnp.bfloat16)


def multiply_round(left_side, right_side):
    return (left_side.astype(jnp.float32) * right_side.astype(jnp.float32)).astype(jnp.bfloat16)


def in_steps(gate_input, values, cotangent, filter_taps):
    context_size = lax.axis_size("ctx")
    data_size = lax.axis_size("dp")
    tok_rows = values.shape[1]
    channels = values.shape[2]
    seq_len = tok_rows * context_size
    local_channels = channels // context_size
    blocks = seq_len // 64
    freq_len = 2 * seq_len
    norm_scale = 1.0 / freq_len
    tables = dft_tables(blocks, freq_len)
    filter_half = filter_taps.astype(jnp.bfloat16)
    filter_columns = lax.all_to_all(filter_half, "ctx", split_axis=1, concat_axis=0, tiled=True)
    matrix = tables[0]
    filter_first = first_section(lax.all_gather(filter_columns, "dp", axis=0, tiled=True), matrix)
    filter_spec = second_section(filter_first, tables)
    value_columns = lax.all_to_all(values[0], "ctx", split_axis=1, concat_axis=0, tiled=True)
    value_spec = spectrum(value_columns, tables)
    conv_columns = inverse_rows(
        inverse_prepare(times_spec(value_spec, filter_spec), tables), tables[1], norm_scale
    ).astype(jnp.bfloat16)
    conv_rows = lax.all_to_all(conv_columns, "ctx", split_axis=0, concat_axis=1, tiled=True)
    output = multiply_round(gate_input[0], conv_rows)
    gate_grad = multiply_round(cotangent[0], conv_rows)
    grad_rows = multiply_round(cotangent[0], gate_input[0])
    grad_columns = lax.all_to_all(grad_rows, "ctx", split_axis=1, concat_axis=0, tiled=True)
    grad_spec = spectrum(grad_columns, tables)
    back_columns = inverse_rows(
        inverse_prepare(times_conj(grad_spec, filter_spec), tables), tables[1], norm_scale
    ).astype(jnp.bfloat16)
    values_grad = lax.all_to_all(back_columns, "ctx", split_axis=0, concat_axis=1, tiled=True)
    filter_twisted = inverse_prepare(times_conj(grad_spec, value_spec), tables)
    whole_rows = inverse_rows(filter_twisted, tables[1], norm_scale)
    reordered = whole_rows.reshape(data_size, context_size, tok_rows // data_size, local_channels)
    reordered = reordered.transpose(1, 0, 2, 3).reshape(seq_len, local_channels)
    received_rows = lax.all_to_all(
        reordered.astype(jnp.bfloat16), "ctx", split_axis=0, concat_axis=1, tiled=True
    ).astype(reordered.dtype)
    filter_grad = lax.psum_scatter(
        received_rows.astype(jnp.bfloat16), "dp", scatter_dimension=0, tiled=True
    ).astype(jnp.float32)
    return (output[None], gate_grad[None], values_grad[None], filter_grad)


def on_device(gate_input, values, cotangent, filter_taps):
    rows, channels = values.shape[1:]
    context_size = lax.axis_size("ctx")
    seq_len = rows * context_size
    table_bytes = 2 * 2 * 2 * seq_len * seq_len
    if table_bytes <= TABLE_LIMIT and context_size % 4 == 0 and channels % (WIDTH * context_size) == 0:
        return in_one_kernel(gate_input, values, cotangent, filter_taps)
    return in_steps(gate_input, values, cotangent, filter_taps)


def solution(mesh):
    in_specs = (
        P("dp", "ctx", None),
        P("dp", "ctx", None),
        P("dp", "ctx", None),
        P(("dp", "ctx"), None),
    )
    out_specs = (
        P("dp", "ctx", None),
        P("dp", "ctx", None),
        P("dp", "ctx", None),
        P(("dp", "ctx"), None),
    )
    return jax.shard_map(
        on_device, mesh=mesh, in_specs=in_specs, out_specs=out_specs, check_vma=False
    )
```

```python
import functools
import math

import jax
import jax.numpy as jnp
import numpy as np
from jax import lax
from jax.experimental import pallas as pl
from jax.experimental.pallas import tpu as pltpu
from jax.sharding import PartitionSpec as P

MESH = pl.DeviceIdType.MESH
WIDTH = 256
TABLE_LIMIT = 8 * 2**20
TILE = 512
OUTER_EIGHTHS = 4


def odd_tables(seq_len):
    turns = np.outer(2 * np.arange(seq_len) + 1, np.arange(seq_len)) % (4 * seq_len)
    angles = turns * (2.0 * math.pi / (4 * seq_len))
    forward = np.concatenate([np.cos(angles), -np.sin(angles)], axis=0)
    inverse = forward.T / seq_len
    tiled = forward.reshape(2, seq_len // TILE, TILE, 2, seq_len // 2)
    forward = tiled.transpose(3, 1, 0, 2, 4).reshape(2, 2 * seq_len, seq_len // 2)
    return jnp.asarray(forward, jnp.bfloat16), jnp.asarray(inverse, jnp.bfloat16)


def dot(left, right):
    return jnp.dot(left, right, preferred_element_type=jnp.float32)


def loop(first, last, body):
    def step(index, carry):
        body(index)
        return carry

    lax.fori_loop(first, last, step, 0)


def kernel(
    dims,
    gate_hbm, values_hbm, cot_hbm, taps_hbm, forward_hbm, inverse_hbm,
    result_rows_ref, filter_grad_ref,
    gate, cot, taps, forward, inverse, taps_half, signal_rows,
    near, whole, taps_cols, taps_spec, near_spec, mixed_near, mixed_far, mixed_taps,
    near_cols, far_cols, partial, partial_in, summed, result_rows, summed_rows,
    load_sem, gather_sem, reduce_sem,
    near_sem, cross_sem, far_sem, taps_sem, taps_cross_sem, back_near_sem, back_far_sem,
    summed_sem, summed_cross_sem,
):
    ctx, dp, rows, seq_len, outer, inner = dims
    side = ctx // 2
    most = max(outer, inner)
    part = seq_len // dp
    own_rows = part // ctx
    half_len = seq_len // 2
    me = lax.axis_index("ctx")
    group = lax.axis_index("dp")
    half = me // side
    place = lax.rem(me, side)
    low = half == 0
    early = group * part < half_len

    def counts(owner):
        first = outer + (owner // side) * (inner - outer)
        second = outer + inner - first
        return first, second, lax.rem(owner, side) // (side // 2)

    def count(owner):
        first, second, late = counts(owner)
        return first + late * (second - first)

    def columns(owner, chunk):
        first, second, late = counts(owner)
        at = lax.rem(owner, side)
        early_at = at - late * (at - side // 2)
        base = early_at * first + (at - early_at) * second
        return pl.ds(pl.multiple_of((base + chunk) * WIDTH, WIDTH), WIDTH)

    def block(index, size):
        return pl.ds(pl.multiple_of(index * size, size), size)

    def remote(src, dst, send_sem, recv_sem, device):
        return pltpu.make_async_remote_copy(
            src_ref=src, dst_ref=dst, send_sem=send_sem, recv_sem=recv_sem,
            device_id=device, device_id_type=MESH,
        )

    def peer_at(offset, crossing):
        where = lax.rem(place + offset + side, side)
        return (1 - half if crossing else half) * side + where

    class Exchange:
        def __init__(self, refs, sems, crossing, inbound):
            self.refs, self.sems, self.crossing, self.inbound = refs, sems, crossing, inbound

        def own(self, chunk):
            source, target = self.refs(chunk, me, me)
            return pltpu.make_async_copy(source, target, self.sems.at[1, chunk, 0])

        def to(self, chunk, offset):
            peer = peer_at(offset, self.crossing)
            source, target = self.refs(chunk, me, peer)
            return remote(source, target, self.sems.at[0, chunk, offset],
                          self.sems.at[1, chunk, offset], {"ctx": peer})

        def back(self, chunk, offset):
            peer = peer_at(-offset, self.crossing)
            source, target = self.refs(chunk, peer, me)
            return remote(source, target, self.sems.at[0, chunk, offset],
                          self.sems.at[1, chunk, offset], {"ctx": peer})

        def each(self, chunk, sending, act):
            def one(offset):
                peer = peer_at(offset if sending else -offset, self.crossing)
                counted = peer if sending == self.inbound else me

                @pl.when(chunk < count(counted))
                def _():
                    act(offset)

            loop(0 if self.crossing else 1, side, one)

        def start(self, chunk):
            self.each(chunk, True, lambda offset: self.to(chunk, offset).start())
            if not self.crossing:
                @pl.when(chunk < count(me))
                def _():
                    self.own(chunk).start()

        def arrive(self, chunk):
            self.each(chunk, False, lambda offset: self.back(chunk, offset).wait_recv())
            if not self.crossing:
                @pl.when(chunk < count(me))
                def _():
                    self.own(chunk).wait()

        def leave(self, chunk):
            self.each(chunk, True, lambda offset: self.to(chunk, offset).wait_send())

    def near_refs(chunk, sender, receiver):
        return (signal_rows.at[0, :, columns(receiver, chunk)],
                near.at[chunk, block(lax.rem(sender, side), rows), :])

    def cross_refs(chunk, sender, receiver):
        return (signal_rows.at[0, :, columns(receiver, chunk)],
                whole.at[chunk, block(sender, rows), :])

    def far_refs(chunk, sender, receiver):
        return (signal_rows.at[1, :, columns(receiver, chunk)],
                whole.at[chunk, block(sender, rows), :])

    def taps_refs(chunk, sender, receiver):
        return (taps_half.at[:, columns(receiver, chunk)],
                taps_cols.at[chunk, block(group * ctx + sender, own_rows), :])

    def back_near_refs(chunk, sender, receiver):
        return (near_cols.at[chunk, block(lax.rem(receiver, side), rows), :],
                result_rows.at[half, :, columns(sender, chunk)])

    def back_far_refs(chunk, sender, receiver):
        return (far_cols.at[chunk, block(lax.rem(receiver, side), rows), :],
                result_rows.at[1 - half, :, columns(sender, chunk)])

    def summed_refs(chunk, sender, receiver):
        return (summed.at[chunk, block(receiver, own_rows), :],
                summed_rows.at[sender // side, :, columns(sender, chunk)])

    near_way = Exchange(near_refs, near_sem, False, True)
    cross_way = Exchange(cross_refs, cross_sem, True, True)
    far_way = Exchange(far_refs, far_sem, False, True)
    taps_way = Exchange(taps_refs, taps_sem, False, True)
    taps_cross_way = Exchange(taps_refs, taps_cross_sem, True, True)
    back_near_way = Exchange(back_near_refs, back_near_sem, False, False)
    back_far_way = Exchange(back_far_refs, back_far_sem, False, False)
    summed_way = Exchange(summed_refs, summed_sem, False, False)
    summed_cross_way = Exchange(summed_refs, summed_cross_sem, True, False)

    loads = [
        pltpu.make_async_copy(src, dst, load_sem.at[at])
        for at, (src, dst) in enumerate(
            [(taps_hbm, taps), (gate_hbm, gate), (cot_hbm, cot),
             (values_hbm, signal_rows.at[half]), (forward_hbm, forward), (inverse_hbm, inverse)]
        )
    ]
    for load in loads[:4]:
        load.start()

    barrier = pltpu.get_barrier_semaphore()
    loop(1, ctx, lambda offset: pl.semaphore_signal(
        barrier, inc=1, device_id={"ctx": lax.rem(me + offset, ctx)}, device_id_type=MESH))
    loop(1, dp, lambda offset: pl.semaphore_signal(
        barrier, inc=1, device_id={"dp": lax.rem(group + offset, dp)}, device_id_type=MESH))
    loads[0].wait()
    taps_half[...] = taps[...].astype(jnp.bfloat16)
    pl.semaphore_wait(barrier, ctx + dp - 2)

    def send_taps(chunk):
        taps_cross_way.start(chunk)
        taps_way.start(chunk)

    loop(0, most, send_taps)
    loads[1].wait()
    loads[2].wait()

    def grad_band(index):
        band = block(index, 16)
        product = gate[band, :].astype(jnp.float32) * cot[band, :].astype(jnp.float32)
        signal_rows[1 - half, band, :] = product.astype(jnp.bfloat16)

    loop(0, rows // 16, grad_band)
    loads[3].wait()

    def send_signals(chunk):
        def turn(offset):
            @pl.when(chunk < count(peer_at(offset, True)))
            def _():
                cross_way.to(chunk, offset).start()

            for way, shift in ((near_way, 1), (far_way, 2)):
                there = lax.rem(offset + shift, side)

                @pl.when(jnp.logical_and(there > 0, chunk < count(peer_at(there, False))))
                def _(way=way, there=there):
                    way.to(chunk, there).start()

        loop(0, side, turn)

        @pl.when(chunk < count(me))
        def _():
            near_way.own(chunk).start()
            far_way.own(chunk).start()

    send_signals(0)
    loads[4].start()
    loads[5].start()
    mine = count(me)

    def gathered(chunk, offset, owner):
        peer = lax.rem(group + offset, dp)
        held = taps_cols.at[chunk, block(owner, part), :]
        return remote(held, held, gather_sem.at[0, chunk, offset], gather_sem.at[1, chunk, offset],
                      {"dp": peer})

    def gather(chunk):
        taps_cross_way.arrive(chunk)
        taps_way.arrive(chunk)
        loop(1, dp, lambda offset: gathered(chunk, offset, group).start())

    loop(0, mine, gather)
    loop(1, most, send_signals)
    loads[4].wait()
    loads[5].wait()
    sign = jnp.where(low, 1.0, -1.0).astype(jnp.float32)
    keep = jnp.where(low, 1.0, 0.0).astype(jnp.float32)

    def reduces(owner):
        return jnp.logical_or(low, owner * part < half_len)

    def reduced(chunk, offset, owner):
        return remote(
            partial.at[chunk, block(owner, part), :], partial_in.at[chunk, offset],
            reduce_sem.at[0, chunk, offset], reduce_sem.at[1, chunk, offset],
            {"dp": lax.rem(group + offset, dp)})

    def reduce_each(chunk, act):
        def one(offset):
            owner = lax.rem(group + offset, dp)

            @pl.when(reduces(owner))
            def _():
                act(reduced(chunk, offset, owner))

        loop(1, dp, one)

    def finish(chunk):
        @pl.when(reduces(group))
        def _():
            loop(1, dp, lambda offset: reduced(chunk, offset, group).wait_recv())
            total = partial[chunk, block(group, part), :].astype(jnp.float32)
            for offset in range(1, dp):
                total = total + partial_in[chunk, offset].astype(jnp.float32)
            summed[chunk] = total.astype(jnp.bfloat16)
            summed_cross_way.start(chunk)
            summed_way.start(chunk)

    def work(chunk):
        loop(1, dp, lambda offset: gathered(
            chunk, offset, lax.rem(group + dp - offset, dp)).wait_recv())
        first, second = pl.ds(0, half_len), pl.ds(half_len, half_len)
        half_type = jnp.bfloat16

        def places(index):
            upper = block(index, TILE)
            lower = pl.ds(pl.multiple_of(seq_len + index * TILE, TILE), TILE)
            return upper, lower, block(index, 2 * TILE)

        def parts(both):
            return both[:TILE], both[TILE:]

        def taps_frequencies(index):
            band = places(index)[2]
            taps_spec[band, :] = dot(forward[0, band, :], taps_cols[chunk, first, :]) + dot(
                forward[1, band, :], taps_cols[chunk, second, :])

        loop(0, seq_len // TILE, taps_frequencies)
        near_way.arrive(chunk)

        def near_frequencies(index):
            upper, lower, band = places(index)
            both = dot(forward[half, band, :], near[chunk])
            near_spec[band, :] = both
            near_real, near_imag = parts(both)
            taps_real, taps_imag = parts(taps_spec[band, :])
            taps_imag = taps_imag * sign
            mixed_near[upper, :] = (near_real * taps_real - near_imag * taps_imag).astype(half_type)
            mixed_near[lower, :] = (near_real * taps_imag + near_imag * taps_real).astype(half_type)

        loop(0, seq_len // TILE, near_frequencies)

        def inverse_rows(index):
            return inverse[pl.ds(pl.multiple_of(half * half_len + index * TILE, TILE), TILE), :]

        def near_tile(index):
            near_cols[chunk, block(index, TILE), :] = dot(
                inverse_rows(index), mixed_near[...]).astype(half_type)

        def far_tile(index):
            far_cols[chunk, block(index, TILE), :] = dot(
                inverse_rows(index), mixed_far[...]).astype(half_type)

        def taps_tile(index):
            band = block(index, TILE)
            partial[chunk, band, :] = dot(inverse[band, :], mixed_taps[...]).astype(half_type)

        loop(0, half_len // TILE, near_tile)
        back_near_way.start(chunk)
        cross_way.arrive(chunk)
        far_way.arrive(chunk)

        def far_frequencies(index):
            upper, lower, band = places(index)
            early_real, early_imag = parts(dot(forward[0, band, :], whole[chunk, first, :]))
            late_real, late_imag = parts(dot(forward[1, band, :], whole[chunk, second, :]))
            near_real, near_imag = parts(near_spec[band, :])
            part_real, part_imag = early_real * keep + late_real, early_imag * keep + late_imag
            mixed_taps[upper, :] = (part_real * near_real + part_imag * near_imag).astype(half_type)
            mixed_taps[lower, :] = (
                (part_imag * near_real - part_real * near_imag) * sign).astype(half_type)
            far_real, far_imag = early_real + late_real, early_imag + late_imag
            taps_real, taps_imag = parts(taps_spec[band, :])
            taps_imag = taps_imag * sign
            mixed_far[upper, :] = (far_real * taps_real + far_imag * taps_imag).astype(half_type)
            mixed_far[lower, :] = (far_imag * taps_real - far_real * taps_imag).astype(half_type)

        loop(0, seq_len // TILE, far_frequencies)
        loop(0, (2 - half) * (half_len // TILE), taps_tile)
        reduce_each(chunk, lambda copy: copy.start())

        @pl.when(chunk > 0)
        def _():
            finish(chunk - 1)

        loop(0, half_len // TILE, far_tile)
        back_far_way.start(chunk)

    loop(0, mine, work)
    finish(mine - 1)

    def results(chunk):
        back_near_way.arrive(chunk)
        back_far_way.arrive(chunk)

    loop(0, most, results)

    result_rows_ref[...] = result_rows[...]

    @pl.when(low)
    def _():
        loop(0, most, summed_way.arrive)

    @pl.when(jnp.logical_not(low))
    def _():
        loop(0, most, summed_cross_way.arrive)

    filter_grad_ref[...] = summed_rows[0].astype(jnp.float32)

    @pl.when(early)
    def _():
        @pl.when(low)
        def _():
            loop(0, most, summed_cross_way.arrive)

        @pl.when(jnp.logical_not(low))
        def _():
            loop(0, most, summed_way.arrive)

        filter_grad_ref[...] += summed_rows[1].astype(jnp.float32)

    def sent(chunk):
        for way in (taps_cross_way, taps_way, cross_way, near_way, far_way,
                    back_near_way, back_far_way):
            way.leave(chunk)

    loop(0, most, sent)

    def sent_sums(chunk):
        loop(1, dp, lambda offset: gathered(chunk, offset, group).wait_send())
        reduce_each(chunk, lambda copy: copy.wait_send())

        @pl.when(reduces(group))
        def _():
            summed_cross_way.leave(chunk)
            summed_way.leave(chunk)

    loop(0, mine, sent_sums)


def gate_kernel(gate, cot, rows, sums, out_ref, gate_grad_ref, values_grad_ref, filter_grad_ref):
    conv = rows[0].astype(jnp.float32)
    out_ref[...] = (gate[...].astype(jnp.float32) * conv).astype(jnp.bfloat16)
    gate_grad_ref[...] = (cot[...].astype(jnp.float32) * conv).astype(jnp.bfloat16)
    values_grad_ref[...] = rows[1]
    filter_grad_ref[...] = sums[...]


def gate_results(gate_input, cotangent, result_rows, sums):
    rows, channels = gate_input.shape
    own_rows = sums.shape[0]
    steps = own_rows // 8
    block = pl.BlockSpec((rows // steps, channels // 2), lambda i, j: (i, j))
    pair = pl.BlockSpec((2, rows // steps, channels // 2), lambda i, j: (0, i, j))
    few = pl.BlockSpec((8, channels // 2), lambda i, j: (i, j))
    shape = jax.ShapeDtypeStruct((rows, channels), jnp.bfloat16)
    return pl.pallas_call(
        gate_kernel,
        grid=(steps, 2),
        in_specs=[block, block, pair, few],
        out_specs=(block, block, block, few),
        out_shape=(shape, shape, shape, jax.ShapeDtypeStruct(sums.shape, jnp.float32)),
        compiler_params=pltpu.CompilerParams(vmem_limit_bytes=60 * 2**20),
    )(gate_input, cotangent, result_rows, sums)


def in_one_kernel(gate_input, values, cotangent, filter_taps):
    ctx = lax.axis_size("ctx")
    dp = lax.axis_size("dp")
    rows, channels = values.shape[1:]
    seq_len = rows * ctx
    own_rows = filter_taps.shape[0]
    part = seq_len // dp
    pair = channels // WIDTH // (ctx // 4)
    outer = max(1, pair * OUTER_EIGHTHS // 8)
    inner = pair - outer
    most = max(outer, inner)
    forward, inverse = odd_tables(seq_len)
    half, full = jnp.bfloat16, jnp.float32
    whole = pltpu.VMEM((most, seq_len, WIDTH), half)
    halves = pltpu.VMEM((most, seq_len // 2, WIDTH), half)
    mix = pltpu.VMEM((2 * seq_len, WIDTH), half)
    spec = pltpu.VMEM((2 * seq_len, WIDTH), full)
    block = pltpu.VMEM((rows, channels), half)
    pair_rows = pltpu.VMEM((2, rows, channels), half)
    sems = pltpu.SemaphoreType.DMA((2, most, ctx // 2))
    groups = pltpu.SemaphoreType.DMA((2, most, dp))
    anywhere = pl.BlockSpec(memory_space=pl.ANY)
    vmem = pl.BlockSpec(memory_space=pltpu.VMEM)
    flops = 12 * seq_len * seq_len * (channels // ctx) * 2
    result_rows, sums = pl.pallas_call(
        functools.partial(kernel, (ctx, dp, rows, seq_len, outer, inner)),
        out_shape=(
            jax.ShapeDtypeStruct((2, rows, channels), half),
            jax.ShapeDtypeStruct((own_rows, channels), full),
        ),
        in_specs=[anywhere] * 6,
        out_specs=(vmem,) * 2,
        scratch_shapes=[
            block, block, pltpu.VMEM((own_rows, channels), full),
            pltpu.VMEM(forward.shape, half), pltpu.VMEM(inverse.shape, half),
            pltpu.VMEM((own_rows, channels), half), pair_rows,
            halves, whole, whole, spec, spec, mix, mix, mix,
            halves, halves, whole, pltpu.VMEM((most, dp, part, WIDTH), half),
            pltpu.VMEM((most, part, WIDTH), half),
            pair_rows, pltpu.VMEM((2, own_rows, channels), half),
            pltpu.SemaphoreType.DMA((6,)), groups, groups,
        ] + [sems] * 9,
        compiler_params=pltpu.CompilerParams(
            collective_id=0, has_side_effects=True, vmem_limit_bytes=58 * 2**20
        ),
        cost_estimate=pl.CostEstimate(
            flops=flops, bytes_accessed=16 * rows * channels, transcendentals=0
        ),
    )(gate_input[0], values[0], cotangent[0], filter_taps, forward, inverse)
    output, gate_grad, values_grad, filter_grad = gate_results(
        gate_input[0], cotangent[0], result_rows, sums
    )
    return output[None], gate_grad[None], values_grad[None], filter_grad


def dft_tables(blocks, freq_len):
    half_blocks = blocks // 2
    row_index = jnp.arange(half_blocks, dtype=jnp.int32)[:, None]
    freq_index = jnp.arange(blocks, dtype=jnp.int32)[None, :]
    angles = (row_index * freq_index % blocks).astype(jnp.float32) * (2.0 * math.pi / blocks)
    first_forward = jnp.stack([jnp.cos(angles), -jnp.sin(angles)], axis=1).astype(jnp.bfloat16)
    first_inverse = jnp.stack([jnp.cos(angles).T, -jnp.sin(angles).T], axis=0).astype(jnp.bfloat16)
    block_index = jnp.arange(blocks, dtype=jnp.int32)[:, None]
    lane_index = jnp.arange(128, dtype=jnp.int32)[None, :]
    twist_angles = (block_index * lane_index % freq_len).astype(jnp.float32) * (
        2.0 * math.pi / freq_len
    )
    twist_cosine = jnp.cos(twist_angles)[:, :, None]
    twist_sine = jnp.sin(twist_angles)[:, :, None]
    inner_index = jnp.arange(128, dtype=jnp.int32)
    inner_angles = (inner_index[:, None] * inner_index[None, :] % 128).astype(jnp.float32) * (
        2.0 * math.pi / 128
    )
    cosine = jnp.cos(inner_angles)
    sine_part = jnp.sin(inner_angles)
    second_forward = jnp.stack(
        [jnp.stack([cosine, -sine_part], axis=1), jnp.stack([sine_part, cosine], axis=1)], axis=0
    ).astype(jnp.bfloat16)
    second_inverse = jnp.stack(
        [jnp.stack([cosine, sine_part], axis=1), jnp.stack([-sine_part, cosine], axis=1)], axis=0
    ).astype(jnp.bfloat16)
    return (first_forward, first_inverse, twist_cosine, twist_sine, second_forward, second_inverse)


def first_section(signal, matrix):
    grouped = signal.reshape(-1, 128, signal.shape[-1])
    return jnp.einsum("abc,arp->rpbc", grouped, matrix, preferred_element_type=jnp.float32)


def second_section(first, tables):
    twisted = jnp.stack(
        [first[0] * tables[2] + first[1] * tables[3], first[1] * tables[2] - first[0] * tables[3]]
    ).astype(jnp.bfloat16)
    return jnp.einsum("rpbc,rbsq->spqc", twisted, tables[4], preferred_element_type=jnp.float32)


def spectrum(signal, tables):
    return second_section(first_section(signal, tables[0]), tables)


def inverse_prepare(spectrum_half, tables):
    mixture = jnp.einsum(
        "rpqc,rqsb->spbc", spectrum_half, tables[5], preferred_element_type=jnp.float32
    )
    return jnp.stack(
        [
            mixture[0] * tables[2] - mixture[1] * tables[3],
            mixture[1] * tables[2] + mixture[0] * tables[3],
        ]
    ).astype(jnp.bfloat16)


def inverse_rows(twisted, matrix, norm_scale):
    rows = (
        jnp.einsum("rpbc,rpa->abc", twisted, matrix, preferred_element_type=jnp.float32)
        * norm_scale
    )
    return rows.reshape(-1, rows.shape[-1])


def times_spec(left_spec, right_spec):
    return jnp.stack(
        [
            left_spec[0] * right_spec[0] - left_spec[1] * right_spec[1],
            left_spec[0] * right_spec[1] + left_spec[1] * right_spec[0],
        ]
    ).astype(jnp.bfloat16)


def times_conj(left_spec, right_spec):
    return jnp.stack(
        [
            left_spec[0] * right_spec[0] + left_spec[1] * right_spec[1],
            left_spec[1] * right_spec[0] - left_spec[0] * right_spec[1],
        ]
    ).astype(jnp.bfloat16)


def multiply_round(left_side, right_side):
    return (left_side.astype(jnp.float32) * right_side.astype(jnp.float32)).astype(jnp.bfloat16)


def in_steps(gate_input, values, cotangent, filter_taps):
    context_size = lax.axis_size("ctx")
    data_size = lax.axis_size("dp")
    tok_rows = values.shape[1]
    channels = values.shape[2]
    seq_len = tok_rows * context_size
    local_channels = channels // context_size
    blocks = seq_len // 64
    freq_len = 2 * seq_len
    norm_scale = 1.0 / freq_len
    tables = dft_tables(blocks, freq_len)
    filter_half = filter_taps.astype(jnp.bfloat16)
    filter_columns = lax.all_to_all(filter_half, "ctx", split_axis=1, concat_axis=0, tiled=True)
    matrix = tables[0]
    filter_first = first_section(lax.all_gather(filter_columns, "dp", axis=0, tiled=True), matrix)
    filter_spec = second_section(filter_first, tables)
    value_columns = lax.all_to_all(values[0], "ctx", split_axis=1, concat_axis=0, tiled=True)
    value_spec = spectrum(value_columns, tables)
    conv_columns = inverse_rows(
        inverse_prepare(times_spec(value_spec, filter_spec), tables), tables[1], norm_scale
    ).astype(jnp.bfloat16)
    conv_rows = lax.all_to_all(conv_columns, "ctx", split_axis=0, concat_axis=1, tiled=True)
    output = multiply_round(gate_input[0], conv_rows)
    gate_grad = multiply_round(cotangent[0], conv_rows)
    grad_rows = multiply_round(cotangent[0], gate_input[0])
    grad_columns = lax.all_to_all(grad_rows, "ctx", split_axis=1, concat_axis=0, tiled=True)
    grad_spec = spectrum(grad_columns, tables)
    back_columns = inverse_rows(
        inverse_prepare(times_conj(grad_spec, filter_spec), tables), tables[1], norm_scale
    ).astype(jnp.bfloat16)
    values_grad = lax.all_to_all(back_columns, "ctx", split_axis=0, concat_axis=1, tiled=True)
    filter_twisted = inverse_prepare(times_conj(grad_spec, value_spec), tables)
    whole_rows = inverse_rows(filter_twisted, tables[1], norm_scale)
    reordered = whole_rows.reshape(data_size, context_size, tok_rows // data_size, local_channels)
    reordered = reordered.transpose(1, 0, 2, 3).reshape(seq_len, local_channels)
    received_rows = lax.all_to_all(
        reordered.astype(jnp.bfloat16), "ctx", split_axis=0, concat_axis=1, tiled=True
    ).astype(reordered.dtype)
    filter_grad = lax.psum_scatter(
        received_rows.astype(jnp.bfloat16), "dp", scatter_dimension=0, tiled=True
    ).astype(jnp.float32)
    return (output[None], gate_grad[None], values_grad[None], filter_grad)


def on_device(gate_input, values, cotangent, filter_taps):
    rows, channels = values.shape[1:]
    context_size = lax.axis_size("ctx")
    seq_len = rows * context_size
    table_bytes = 2 * 2 * 2 * seq_len * seq_len
    if table_bytes <= TABLE_LIMIT and context_size % 4 == 0 and channels % (WIDTH * context_size) == 0:
        return in_one_kernel(gate_input, values, cotangent, filter_taps)
    return in_steps(gate_input, values, cotangent, filter_taps)


def solution(mesh):
    in_specs = (
        P("dp", "ctx", None),
        P("dp", "ctx", None),
        P("dp", "ctx", None),
        P(("dp", "ctx"), None),
    )
    out_specs = (
        P("dp", "ctx", None),
        P("dp", "ctx", None),
        P("dp", "ctx", None),
        P(("dp", "ctx"), None),
    )
    return jax.shard_map(
        on_device, mesh=mesh, in_specs=in_specs, out_specs=out_specs, check_vma=False
    )
```

```python
import functools
import math

import jax
import jax.numpy as jnp
import numpy as np
from jax import lax
from jax.experimental import pallas as pl
from jax.experimental.pallas import tpu as pltpu
from jax.sharding import PartitionSpec as P

MESH = pl.DeviceIdType.MESH
WIDTH = 256
TABLE_LIMIT = 8 * 2**20
TILE = 512
OUTER_EIGHTHS = 4


def odd_tables(seq_len):
    turns = np.outer(2 * np.arange(seq_len) + 1, np.arange(seq_len)) % (4 * seq_len)
    angles = turns * (2.0 * math.pi / (4 * seq_len))
    forward = np.concatenate([np.cos(angles), -np.sin(angles)], axis=0)
    inverse = forward.T / seq_len
    tiled = forward.reshape(2, seq_len // TILE, TILE, 2, seq_len // 2)
    forward = tiled.transpose(3, 1, 0, 2, 4).reshape(2, 2 * seq_len, seq_len // 2)
    return jnp.asarray(forward, jnp.bfloat16), jnp.asarray(inverse, jnp.bfloat16)


def dot(left, right):
    return jnp.dot(left, right, preferred_element_type=jnp.float32)


def loop(first, last, body):
    def step(index, carry):
        body(index)
        return carry

    lax.fori_loop(first, last, step, 0)


def kernel(
    dims,
    gate_hbm, values_hbm, cot_hbm, taps_hbm, forward_hbm, inverse_hbm,
    result_rows_ref, filter_grad_ref,
    gate, cot, taps, forward, inverse, taps_half, signal_rows,
    near, whole, taps_cols, taps_spec, near_spec, mixed_near, mixed_far, mixed_taps,
    near_cols, far_cols, partial, partial_in, summed, result_rows, summed_rows,
    load_sem, gather_sem, reduce_sem,
    near_sem, cross_sem, far_sem, taps_sem, taps_cross_sem, back_near_sem, back_far_sem,
    summed_sem, summed_cross_sem,
):
    ctx, dp, rows, seq_len, outer, inner = dims
    side = ctx // 2
    most = max(outer, inner)
    part = seq_len // dp
    own_rows = part // ctx
    half_len = seq_len // 2
    me = lax.axis_index("ctx")
    group = lax.axis_index("dp")
    half = me // side
    place = lax.rem(me, side)
    low = half == 0
    early = group * part < half_len

    def counts(owner):
        first = outer + (owner // side) * (inner - outer)
        second = outer + inner - first
        return first, second, lax.rem(owner, side) // (side // 2)

    def count(owner):
        first, second, late = counts(owner)
        return first + late * (second - first)

    def columns(owner, chunk):
        first, second, late = counts(owner)
        at = lax.rem(owner, side)
        early_at = at - late * (at - side // 2)
        base = early_at * first + (at - early_at) * second
        return pl.ds(pl.multiple_of((base + chunk) * WIDTH, WIDTH), WIDTH)

    def block(index, size):
        return pl.ds(pl.multiple_of(index * size, size), size)

    def remote(src, dst, send_sem, recv_sem, device):
        return pltpu.make_async_remote_copy(
            src_ref=src, dst_ref=dst, send_sem=send_sem, recv_sem=recv_sem,
            device_id=device, device_id_type=MESH,
        )

    def peer_at(offset, crossing):
        where = lax.rem(place + offset + side, side)
        return (1 - half if crossing else half) * side + where

    class Exchange:
        def __init__(self, refs, sems, crossing, inbound):
            self.refs, self.sems, self.crossing, self.inbound = refs, sems, crossing, inbound

        def own(self, chunk):
            source, target = self.refs(chunk, me, me)
            return pltpu.make_async_copy(source, target, self.sems.at[1, chunk, 0])

        def to(self, chunk, offset):
            peer = peer_at(offset, self.crossing)
            source, target = self.refs(chunk, me, peer)
            return remote(source, target, self.sems.at[0, chunk, offset],
                          self.sems.at[1, chunk, offset], {"ctx": peer})

        def back(self, chunk, offset):
            peer = peer_at(-offset, self.crossing)
            source, target = self.refs(chunk, peer, me)
            return remote(source, target, self.sems.at[0, chunk, offset],
                          self.sems.at[1, chunk, offset], {"ctx": peer})

        def each(self, chunk, sending, act):
            def one(offset):
                peer = peer_at(offset if sending else -offset, self.crossing)
                counted = peer if sending == self.inbound else me

                @pl.when(chunk < count(counted))
                def _():
                    act(offset)

            loop(0 if self.crossing else 1, side, one)

        def start(self, chunk):
            self.each(chunk, True, lambda offset: self.to(chunk, offset).start())
            if not self.crossing:
                @pl.when(chunk < count(me))
                def _():
                    self.own(chunk).start()

        def arrive(self, chunk):
            self.each(chunk, False, lambda offset: self.back(chunk, offset).wait_recv())
            if not self.crossing:
                @pl.when(chunk < count(me))
                def _():
                    self.own(chunk).wait()

        def leave(self, chunk):
            self.each(chunk, True, lambda offset: self.to(chunk, offset).wait_send())

    def near_refs(chunk, sender, receiver):
        return (signal_rows.at[0, :, columns(receiver, chunk)],
                near.at[chunk, block(lax.rem(sender, side), rows), :])

    def cross_refs(chunk, sender, receiver):
        return (signal_rows.at[0, :, columns(receiver, chunk)],
                whole.at[chunk, block(sender, rows), :])

    def far_refs(chunk, sender, receiver):
        return (signal_rows.at[1, :, columns(receiver, chunk)],
                whole.at[chunk, block(sender, rows), :])

    def taps_refs(chunk, sender, receiver):
        return (taps_half.at[:, columns(receiver, chunk)],
                taps_cols.at[chunk, block(group * ctx + sender, own_rows), :])

    def back_near_refs(chunk, sender, receiver):
        return (near_cols.at[chunk, block(lax.rem(receiver, side), rows), :],
                result_rows.at[half, :, columns(sender, chunk)])

    def back_far_refs(chunk, sender, receiver):
        return (far_cols.at[chunk, block(lax.rem(receiver, side), rows), :],
                result_rows.at[1 - half, :, columns(sender, chunk)])

    def summed_refs(chunk, sender, receiver):
        return (summed.at[chunk, block(receiver, own_rows), :],
                summed_rows.at[sender // side, :, columns(sender, chunk)])

    near_way = Exchange(near_refs, near_sem, False, True)
    cross_way = Exchange(cross_refs, cross_sem, True, True)
    far_way = Exchange(far_refs, far_sem, False, True)
    taps_way = Exchange(taps_refs, taps_sem, False, True)
    taps_cross_way = Exchange(taps_refs, taps_cross_sem, True, True)
    back_near_way = Exchange(back_near_refs, back_near_sem, False, False)
    back_far_way = Exchange(back_far_refs, back_far_sem, False, False)
    summed_way = Exchange(summed_refs, summed_sem, False, False)
    summed_cross_way = Exchange(summed_refs, summed_cross_sem, True, False)

    loads = [
        pltpu.make_async_copy(src, dst, load_sem.at[at])
        for at, (src, dst) in enumerate(
            [(taps_hbm, taps), (gate_hbm, gate), (cot_hbm, cot),
             (values_hbm, signal_rows.at[half]), (forward_hbm, forward), (inverse_hbm, inverse)]
        )
    ]
    for load in loads[:4]:
        load.start()

    barrier = pltpu.get_barrier_semaphore()
    loop(1, ctx, lambda offset: pl.semaphore_signal(
        barrier, inc=1, device_id={"ctx": lax.rem(me + offset, ctx)}, device_id_type=MESH))
    loop(1, dp, lambda offset: pl.semaphore_signal(
        barrier, inc=1, device_id={"dp": lax.rem(group + offset, dp)}, device_id_type=MESH))
    loads[0].wait()
    taps_half[...] = taps[...].astype(jnp.bfloat16)
    pl.semaphore_wait(barrier, ctx + dp - 2)

    def send_taps(chunk):
        taps_cross_way.start(chunk)
        taps_way.start(chunk)

    loop(0, most, send_taps)
    loads[1].wait()
    loads[2].wait()

    def grad_band(index):
        band = block(index, 16)
        product = gate[band, :].astype(jnp.float32) * cot[band, :].astype(jnp.float32)
        signal_rows[1 - half, band, :] = product.astype(jnp.bfloat16)

    loop(0, rows // 16, grad_band)
    loads[3].wait()

    def send_signals(chunk):
        near_way.start(chunk)
        cross_way.start(chunk)
        far_way.start(chunk)

    send_signals(0)
    loads[4].start()
    loads[5].start()
    mine = count(me)

    def gathered(chunk, offset, owner):
        peer = lax.rem(group + offset, dp)
        held = taps_cols.at[chunk, block(owner, part), :]
        return remote(held, held, gather_sem.at[0, chunk, offset], gather_sem.at[1, chunk, offset],
                      {"dp": peer})

    def gather(chunk):
        taps_cross_way.arrive(chunk)
        taps_way.arrive(chunk)
        loop(1, dp, lambda offset: gathered(chunk, offset, group).start())

    loop(0, mine, gather)
    loop(1, most, send_signals)
    loads[4].wait()
    loads[5].wait()
    sign = jnp.where(low, 1.0, -1.0).astype(jnp.float32)
    keep = jnp.where(low, 1.0, 0.0).astype(jnp.float32)

    def reduces(owner):
        return jnp.logical_or(low, owner * part < half_len)

    def reduced(chunk, offset, owner):
        return remote(
            partial.at[chunk, block(owner, part), :], partial_in.at[chunk, offset],
            reduce_sem.at[0, chunk, offset], reduce_sem.at[1, chunk, offset],
            {"dp": lax.rem(group + offset, dp)})

    def reduce_each(chunk, act):
        def one(offset):
            owner = lax.rem(group + offset, dp)

            @pl.when(reduces(owner))
            def _():
                act(reduced(chunk, offset, owner))

        loop(1, dp, one)

    def finish(chunk):
        @pl.when(reduces(group))
        def _():
            loop(1, dp, lambda offset: reduced(chunk, offset, group).wait_recv())
            total = partial[chunk, block(group, part), :].astype(jnp.float32)
            for offset in range(1, dp):
                total = total + partial_in[chunk, offset].astype(jnp.float32)
            summed[chunk] = total.astype(jnp.bfloat16)
            summed_cross_way.start(chunk)
            summed_way.start(chunk)

    def work(chunk):
        loop(1, dp, lambda offset: gathered(
            chunk, offset, lax.rem(group + dp - offset, dp)).wait_recv())
        first, second = pl.ds(0, half_len), pl.ds(half_len, half_len)
        half_type = jnp.bfloat16

        def places(index):
            upper = block(index, TILE)
            lower = pl.ds(pl.multiple_of(seq_len + index * TILE, TILE), TILE)
            return upper, lower, block(index, 2 * TILE)

        def parts(both):
            return both[:TILE], both[TILE:]

        def taps_frequencies(index):
            band = places(index)[2]
            taps_spec[band, :] = dot(forward[0, band, :], taps_cols[chunk, first, :]) + dot(
                forward[1, band, :], taps_cols[chunk, second, :])

        loop(0, seq_len // TILE, taps_frequencies)
        near_way.arrive(chunk)

        def near_frequencies(index):
            upper, lower, band = places(index)
            both = dot(forward[half, band, :], near[chunk])
            near_spec[band, :] = both
            near_real, near_imag = parts(both)
            taps_real, taps_imag = parts(taps_spec[band, :])
            taps_imag = taps_imag * sign
            mixed_near[upper, :] = (near_real * taps_real - near_imag * taps_imag).astype(half_type)
            mixed_near[lower, :] = (near_real * taps_imag + near_imag * taps_real).astype(half_type)

        loop(0, seq_len // TILE, near_frequencies)

        def inverse_rows(index):
            return inverse[pl.ds(pl.multiple_of(half * half_len + index * TILE, TILE), TILE), :]

        def near_tile(index):
            near_cols[chunk, block(index, TILE), :] = dot(
                inverse_rows(index), mixed_near[...]).astype(half_type)

        def far_tile(index):
            far_cols[chunk, block(index, TILE), :] = dot(
                inverse_rows(index), mixed_far[...]).astype(half_type)

        def taps_tile(index):
            band = block(index, TILE)
            partial[chunk, band, :] = dot(inverse[band, :], mixed_taps[...]).astype(half_type)

        loop(0, half_len // TILE, near_tile)
        back_near_way.start(chunk)
        cross_way.arrive(chunk)
        far_way.arrive(chunk)

        def far_frequencies(index):
            upper, lower, band = places(index)
            early_real, early_imag = parts(dot(forward[0, band, :], whole[chunk, first, :]))
            late_real, late_imag = parts(dot(forward[1, band, :], whole[chunk, second, :]))
            near_real, near_imag = parts(near_spec[band, :])
            part_real, part_imag = early_real * keep + late_real, early_imag * keep + late_imag
            mixed_taps[upper, :] = (part_real * near_real + part_imag * near_imag).astype(half_type)
            mixed_taps[lower, :] = (
                (part_imag * near_real - part_real * near_imag) * sign).astype(half_type)
            far_real, far_imag = early_real + late_real, early_imag + late_imag
            taps_real, taps_imag = parts(taps_spec[band, :])
            taps_imag = taps_imag * sign
            mixed_far[upper, :] = (far_real * taps_real + far_imag * taps_imag).astype(half_type)
            mixed_far[lower, :] = (far_imag * taps_real - far_real * taps_imag).astype(half_type)

        loop(0, seq_len // TILE, far_frequencies)
        loop(0, (2 - half) * (half_len // TILE), taps_tile)
        reduce_each(chunk, lambda copy: copy.start())

        @pl.when(chunk > 0)
        def _():
            finish(chunk - 1)

        loop(0, half_len // TILE, far_tile)
        back_far_way.start(chunk)

    loop(0, mine, work)
    finish(mine - 1)

    def results(chunk):
        back_near_way.arrive(chunk)
        back_far_way.arrive(chunk)

    loop(0, most, results)

    result_rows_ref[...] = result_rows[...]

    @pl.when(low)
    def _():
        loop(0, most, summed_way.arrive)

    @pl.when(jnp.logical_not(low))
    def _():
        loop(0, most, summed_cross_way.arrive)

    filter_grad_ref[...] = summed_rows[0].astype(jnp.float32)

    @pl.when(early)
    def _():
        @pl.when(low)
        def _():
            loop(0, most, summed_cross_way.arrive)

        @pl.when(jnp.logical_not(low))
        def _():
            loop(0, most, summed_way.arrive)

        filter_grad_ref[...] += summed_rows[1].astype(jnp.float32)

    def sent(chunk):
        for way in (taps_cross_way, taps_way, cross_way, near_way, far_way,
                    back_near_way, back_far_way):
            way.leave(chunk)

    loop(0, most, sent)

    def sent_sums(chunk):
        loop(1, dp, lambda offset: gathered(chunk, offset, group).wait_send())
        reduce_each(chunk, lambda copy: copy.wait_send())

        @pl.when(reduces(group))
        def _():
            summed_cross_way.leave(chunk)
            summed_way.leave(chunk)

    loop(0, mine, sent_sums)


def gate_kernel(gate, cot, rows, sums, out_ref, gate_grad_ref, values_grad_ref, filter_grad_ref):
    conv = rows[0].astype(jnp.float32)
    out_ref[...] = (gate[...].astype(jnp.float32) * conv).astype(jnp.bfloat16)
    gate_grad_ref[...] = (cot[...].astype(jnp.float32) * conv).astype(jnp.bfloat16)
    values_grad_ref[...] = rows[1]
    filter_grad_ref[...] = sums[...]


def gate_results(gate_input, cotangent, result_rows, sums):
    rows, channels = gate_input.shape
    own_rows = sums.shape[0]
    steps = 2
    block = pl.BlockSpec((rows // steps, channels), lambda i: (i, 0))
    pair = pl.BlockSpec((2, rows // steps, channels), lambda i: (0, i, 0))
    few = pl.BlockSpec((own_rows // steps, channels), lambda i: (i, 0))
    shape = jax.ShapeDtypeStruct((rows, channels), jnp.bfloat16)
    return pl.pallas_call(
        gate_kernel,
        grid=(steps,),
        in_specs=[block, block, pair, few],
        out_specs=(block, block, block, few),
        out_shape=(shape, shape, shape, jax.ShapeDtypeStruct(sums.shape, jnp.float32)),
        compiler_params=pltpu.CompilerParams(vmem_limit_bytes=60 * 2**20),
    )(gate_input, cotangent, result_rows, sums)


def in_one_kernel(gate_input, values, cotangent, filter_taps):
    ctx = lax.axis_size("ctx")
    dp = lax.axis_size("dp")
    rows, channels = values.shape[1:]
    seq_len = rows * ctx
    own_rows = filter_taps.shape[0]
    part = seq_len // dp
    pair = channels // WIDTH // (ctx // 4)
    outer = max(1, pair * OUTER_EIGHTHS // 8)
    inner = pair - outer
    most = max(outer, inner)
    forward, inverse = odd_tables(seq_len)
    half, full = jnp.bfloat16, jnp.float32
    whole = pltpu.VMEM((most, seq_len, WIDTH), half)
    halves = pltpu.VMEM((most, seq_len // 2, WIDTH), half)
    mix = pltpu.VMEM((2 * seq_len, WIDTH), half)
    spec = pltpu.VMEM((2 * seq_len, WIDTH), full)
    block = pltpu.VMEM((rows, channels), half)
    pair_rows = pltpu.VMEM((2, rows, channels), half)
    sems = pltpu.SemaphoreType.DMA((2, most, ctx // 2))
    groups = pltpu.SemaphoreType.DMA((2, most, dp))
    anywhere = pl.BlockSpec(memory_space=pl.ANY)
    vmem = pl.BlockSpec(memory_space=pltpu.VMEM)
    flops = 12 * seq_len * seq_len * (channels // ctx) * 2
    result_rows, sums = pl.pallas_call(
        functools.partial(kernel, (ctx, dp, rows, seq_len, outer, inner)),
        out_shape=(
            jax.ShapeDtypeStruct((2, rows, channels), half),
            jax.ShapeDtypeStruct((own_rows, channels), full),
        ),
        in_specs=[anywhere] * 6,
        out_specs=(vmem,) * 2,
        scratch_shapes=[
            block, block, pltpu.VMEM((own_rows, channels), full),
            pltpu.VMEM(forward.shape, half), pltpu.VMEM(inverse.shape, half),
            pltpu.VMEM((own_rows, channels), half), pair_rows,
            halves, whole, whole, spec, spec, mix, mix, mix,
            halves, halves, whole, pltpu.VMEM((most, dp, part, WIDTH), half),
            pltpu.VMEM((most, part, WIDTH), half),
            pair_rows, pltpu.VMEM((2, own_rows, channels), half),
            pltpu.SemaphoreType.DMA((6,)), groups, groups,
        ] + [sems] * 9,
        compiler_params=pltpu.CompilerParams(
            collective_id=0, has_side_effects=True, vmem_limit_bytes=58 * 2**20
        ),
        cost_estimate=pl.CostEstimate(
            flops=flops, bytes_accessed=16 * rows * channels, transcendentals=0
        ),
    )(gate_input[0], values[0], cotangent[0], filter_taps, forward, inverse)
    output, gate_grad, values_grad, filter_grad = gate_results(
        gate_input[0], cotangent[0], result_rows, sums
    )
    return output[None], gate_grad[None], values_grad[None], filter_grad


def dft_tables(blocks, freq_len):
    half_blocks = blocks // 2
    row_index = jnp.arange(half_blocks, dtype=jnp.int32)[:, None]
    freq_index = jnp.arange(blocks, dtype=jnp.int32)[None, :]
    angles = (row_index * freq_index % blocks).astype(jnp.float32) * (2.0 * math.pi / blocks)
    first_forward = jnp.stack([jnp.cos(angles), -jnp.sin(angles)], axis=1).astype(jnp.bfloat16)
    first_inverse = jnp.stack([jnp.cos(angles).T, -jnp.sin(angles).T], axis=0).astype(jnp.bfloat16)
    block_index = jnp.arange(blocks, dtype=jnp.int32)[:, None]
    lane_index = jnp.arange(128, dtype=jnp.int32)[None, :]
    twist_angles = (block_index * lane_index % freq_len).astype(jnp.float32) * (
        2.0 * math.pi / freq_len
    )
    twist_cosine = jnp.cos(twist_angles)[:, :, None]
    twist_sine = jnp.sin(twist_angles)[:, :, None]
    inner_index = jnp.arange(128, dtype=jnp.int32)
    inner_angles = (inner_index[:, None] * inner_index[None, :] % 128).astype(jnp.float32) * (
        2.0 * math.pi / 128
    )
    cosine = jnp.cos(inner_angles)
    sine_part = jnp.sin(inner_angles)
    second_forward = jnp.stack(
        [jnp.stack([cosine, -sine_part], axis=1), jnp.stack([sine_part, cosine], axis=1)], axis=0
    ).astype(jnp.bfloat16)
    second_inverse = jnp.stack(
        [jnp.stack([cosine, sine_part], axis=1), jnp.stack([-sine_part, cosine], axis=1)], axis=0
    ).astype(jnp.bfloat16)
    return (first_forward, first_inverse, twist_cosine, twist_sine, second_forward, second_inverse)


def first_section(signal, matrix):
    grouped = signal.reshape(-1, 128, signal.shape[-1])
    return jnp.einsum("abc,arp->rpbc", grouped, matrix, preferred_element_type=jnp.float32)


def second_section(first, tables):
    twisted = jnp.stack(
        [first[0] * tables[2] + first[1] * tables[3], first[1] * tables[2] - first[0] * tables[3]]
    ).astype(jnp.bfloat16)
    return jnp.einsum("rpbc,rbsq->spqc", twisted, tables[4], preferred_element_type=jnp.float32)


def spectrum(signal, tables):
    return second_section(first_section(signal, tables[0]), tables)


def inverse_prepare(spectrum_half, tables):
    mixture = jnp.einsum(
        "rpqc,rqsb->spbc", spectrum_half, tables[5], preferred_element_type=jnp.float32
    )
    return jnp.stack(
        [
            mixture[0] * tables[2] - mixture[1] * tables[3],
            mixture[1] * tables[2] + mixture[0] * tables[3],
        ]
    ).astype(jnp.bfloat16)


def inverse_rows(twisted, matrix, norm_scale):
    rows = (
        jnp.einsum("rpbc,rpa->abc", twisted, matrix, preferred_element_type=jnp.float32)
        * norm_scale
    )
    return rows.reshape(-1, rows.shape[-1])


def times_spec(left_spec, right_spec):
    return jnp.stack(
        [
            left_spec[0] * right_spec[0] - left_spec[1] * right_spec[1],
            left_spec[0] * right_spec[1] + left_spec[1] * right_spec[0],
        ]
    ).astype(jnp.bfloat16)


def times_conj(left_spec, right_spec):
    return jnp.stack(
        [
            left_spec[0] * right_spec[0] + left_spec[1] * right_spec[1],
            left_spec[1] * right_spec[0] - left_spec[0] * right_spec[1],
        ]
    ).astype(jnp.bfloat16)


def multiply_round(left_side, right_side):
    return (left_side.astype(jnp.float32) * right_side.astype(jnp.float32)).astype(jnp.bfloat16)


def in_steps(gate_input, values, cotangent, filter_taps):
    context_size = lax.axis_size("ctx")
    data_size = lax.axis_size("dp")
    tok_rows = values.shape[1]
    channels = values.shape[2]
    seq_len = tok_rows * context_size
    local_channels = channels // context_size
    blocks = seq_len // 64
    freq_len = 2 * seq_len
    norm_scale = 1.0 / freq_len
    tables = dft_tables(blocks, freq_len)
    filter_half = filter_taps.astype(jnp.bfloat16)
    filter_columns = lax.all_to_all(filter_half, "ctx", split_axis=1, concat_axis=0, tiled=True)
    matrix = tables[0]
    filter_first = first_section(lax.all_gather(filter_columns, "dp", axis=0, tiled=True), matrix)
    filter_spec = second_section(filter_first, tables)
    value_columns = lax.all_to_all(values[0], "ctx", split_axis=1, concat_axis=0, tiled=True)
    value_spec = spectrum(value_columns, tables)
    conv_columns = inverse_rows(
        inverse_prepare(times_spec(value_spec, filter_spec), tables), tables[1], norm_scale
    ).astype(jnp.bfloat16)
    conv_rows = lax.all_to_all(conv_columns, "ctx", split_axis=0, concat_axis=1, tiled=True)
    output = multiply_round(gate_input[0], conv_rows)
    gate_grad = multiply_round(cotangent[0], conv_rows)
    grad_rows = multiply_round(cotangent[0], gate_input[0])
    grad_columns = lax.all_to_all(grad_rows, "ctx", split_axis=1, concat_axis=0, tiled=True)
    grad_spec = spectrum(grad_columns, tables)
    back_columns = inverse_rows(
        inverse_prepare(times_conj(grad_spec, filter_spec), tables), tables[1], norm_scale
    ).astype(jnp.bfloat16)
    values_grad = lax.all_to_all(back_columns, "ctx", split_axis=0, concat_axis=1, tiled=True)
    filter_twisted = inverse_prepare(times_conj(grad_spec, value_spec), tables)
    whole_rows = inverse_rows(filter_twisted, tables[1], norm_scale)
    reordered = whole_rows.reshape(data_size, context_size, tok_rows // data_size, local_channels)
    reordered = reordered.transpose(1, 0, 2, 3).reshape(seq_len, local_channels)
    received_rows = lax.all_to_all(
        reordered.astype(jnp.bfloat16), "ctx", split_axis=0, concat_axis=1, tiled=True
    ).astype(reordered.dtype)
    filter_grad = lax.psum_scatter(
        received_rows.astype(jnp.bfloat16), "dp", scatter_dimension=0, tiled=True
    ).astype(jnp.float32)
    return (output[None], gate_grad[None], values_grad[None], filter_grad)


def on_device(gate_input, values, cotangent, filter_taps):
    rows, channels = values.shape[1:]
    context_size = lax.axis_size("ctx")
    seq_len = rows * context_size
    table_bytes = 2 * 2 * 2 * seq_len * seq_len
    if table_bytes <= TABLE_LIMIT and context_size % 4 == 0 and channels % (WIDTH * context_size) == 0:
        return in_one_kernel(gate_input, values, cotangent, filter_taps)
    return in_steps(gate_input, values, cotangent, filter_taps)


def solution(mesh):
    in_specs = (
        P("dp", "ctx", None),
        P("dp", "ctx", None),
        P("dp", "ctx", None),
        P(("dp", "ctx"), None),
    )
    out_specs = (
        P("dp", "ctx", None),
        P("dp", "ctx", None),
        P("dp", "ctx", None),
        P(("dp", "ctx"), None),
    )
    return jax.shard_map(
        on_device, mesh=mesh, in_specs=in_specs, out_specs=out_specs, check_vma=False
    )
```
